32 devices in a mesh: freq: 4 (over z), layer: 2 (over x), lat: 4 (over y, core).
Axes of the slice: x: 2, y: 2, z: 4, core: 2. Of those that a mesh axis runs over, the one named last changes fastest.
Arguments:
- source: float32 [2, 4, 2, 2, 512, 512], P(None, 'freq', None, 'layer', 'lat'), may hold values from -6 to 6
- contrast: float32 [2, 4, 2, 512, 512], P(None, 'freq', 'layer', 'lat'), may hold values from -0.5 to 0.5
- green: float32 [2, 4, 2, 2, 512, 512], P(None, 'freq', None, 'layer', 'lat'), may hold values from -0.6 to 0.6
- efield: float32 [2, 4, 2, 2, 512, 512], P(None, 'freq', None, 'layer', 'lat'), may hold values from -6 to 6
- cell_class: int32 [2, 512, 512], P('layer', 'lat'), may hold values from 0 to 7
Outputs:
- cell_gradient: float32 [2, 512, 512], P('layer', 'lat')
- class_gradient: float32 [2, 8], P('layer')
The draws below stay inside these ranges and needn't reach their ends.
All inputs are finite; a program needn't handle non-finite values.
Results may differ from the reference program's by a relative error of at most 0.0001.
Values sent between devices are 32-bit elements; how exact they have to be, the bound alone decides.
No kernel may reach another device: no remote copies, remote signals or barrier semaphores. Data moves between devices by JAX's collectives and lax.ppermute only.
A program may use at most 64 MiB of HBM per device.

```python
import jax
import jax.numpy as jnp
from jax import lax

NXY = 512
POLS = 2
ITERS = 2
CLASSES = 8
LAYERS = 2
FREQS = 4


def place_ends(entries, key, least, top_value):
    longest = entries.shape.index(max(entries.shape))
    spots = []
    for shift in (0, 1):
        where = [jax.random.randint(jax.random.fold_in(key, axis), (), 0, length) for axis, length in enumerate(entries.shape)]
        where[longest] = (where[longest] + shift) % entries.shape[longest]
        spots.append(tuple(where))
    return entries.at[spots[0]].set(least).at[spots[1]].set(top_value)


def steps_of(own_key, extent, pieces, smallest, top_value):
    gain = 1.0
    for dim, shards_of in pieces:
        steps = jax.random.uniform(jax.random.fold_in(jax.random.fold_in(own_key, 6), dim), (shards_of,), jnp.float32, smallest / len(pieces), top_value / len(pieces))
        gain = gain * jnp.repeat(jnp.exp(steps), extent[dim] // shards_of).reshape((-1,) + (1,) * (len(extent) - 1 - dim))
    return gain


def bell_draw(stream_key, shape, deviation, limit, shards=(), dtype=jnp.bfloat16):
    entries = jax.random.normal(stream_key, shape, jnp.float32) * deviation
    if len(shards) > 0:
        entries = steps_of(stream_key, shape, shards, -0.22, 0.18) * entries
    return jnp.clip(entries, min=-limit, max=limit).astype(dtype)


def setup_inputs(seed: int = 0) -> dict:
    splits = jax.random.split(jax.random.key(seed), 6)
    return {
        "source": bell_draw(splits[0], (2, FREQS, POLS, LAYERS, NXY, NXY), 1.0, 6.0, ((1, 4), (3, 2), (4, 4)), jnp.float32),
        "contrast": jnp.clip(jax.random.uniform(splits[1], (2, FREQS, LAYERS, NXY, NXY), jnp.float32, -0.5, 0.5) * steps_of(splits[1], (2, FREQS, LAYERS, NXY, NXY), ((1, 4), (2, 2), (3, 4)), -0.4, 0.0), -0.5, 0.5),
        "green": jnp.clip(jax.random.uniform(splits[2], (2, FREQS, LAYERS, LAYERS, NXY, NXY), jnp.float32, -0.6, 0.6) * steps_of(splits[2], (2, FREQS, LAYERS, LAYERS, NXY, NXY), ((1, 4), (3, 2), (4, 4)), -0.4, 0.0), -0.6, 0.6),
        "efield": bell_draw(splits[3], (2, FREQS, POLS, LAYERS, NXY, NXY), 1.0, 6.0, ((1, 4), (3, 2), (4, 4)), jnp.float32),
        "cell_class": place_ends(jax.random.randint(splits[4], (LAYERS, NXY, NXY), 0, CLASSES), jax.random.fold_in(splits[4], 1), 0, CLASSES - 1).astype(jnp.int32),
    }


def one_frequency(items):
    src, con, grn, fwd = items
    start = src[0] + 1j * src[1]
    factor = (con[0] + 1j * con[1])[None]
    kernel = grn[0] + 1j * grn[1]
    field = start
    for step in range(ITERS):
        weighted = factor * field
        spectra = jnp.swapaxes(jnp.fft.fft2(weighted, norm="ortho"), -1, -2)
        mixed = jnp.einsum("oiyx,piyx->poyx", kernel, spectra)
        back = jnp.fft.ifft2(jnp.swapaxes(mixed, -1, -2), norm="ortho")
        field = start + factor * back
    return jnp.sum(fwd[0] * jnp.real(field) - fwd[1] * jnp.imag(field), axis=0)


def reference(source, contrast, green, efield, cell_class):
    per_freq = lax.map(one_frequency, (jnp.moveaxis(source, 1, 0), jnp.moveaxis(contrast, 1, 0), jnp.moveaxis(green, 1, 0), jnp.moveaxis(efield, 1, 0)))
    cell = jnp.sum(per_freq, axis=0).astype(jnp.float32)
    sums = [jnp.sum(jnp.where(cell_class == c, cell, jnp.zeros_like(cell)), axis=(1, 2)) for c in range(CLASSES)]
    classes = (jnp.stack(sums, axis=1) / float(NXY)).astype(jnp.float32)
    return cell, classes
```

```python
import functools
import math

import jax
import jax.numpy as jnp
import ml_dtypes
import numpy as np
from jax import lax
from jax.experimental import pallas as pl
from jax.experimental.pallas import tpu as pltpu
from jax.sharding import PartitionSpec as P

NXY = 512
ITERS = 2
CLASSES = 8


highest = lax.Precision.HIGHEST


def tables(length):
    index = jnp.arange(length, dtype=jnp.int32)
    phase = index[:, None] * index[None, :] % length
    angle = phase.astype(jnp.float32) * (2.0 * math.pi / length)
    factor = 1.0 / math.sqrt(length)
    return (jnp.cos(angle) * factor, jnp.sin(angle) * factor)


def forward(field, cosine, sine):
    first = jnp.einsum("zfplxy,yk->zfplkx", field, cosine, precision=highest)
    second = jnp.einsum("zfplxy,yk->zfplkx", field, sine, precision=highest)
    partial_spec = jnp.stack([first[0] + second[1], first[1] - second[0]])
    turned = lax.all_to_all(partial_spec, "lat", split_axis=4, concat_axis=5, tiled=True)
    first = jnp.einsum("zfplkx,xq->zfplkq", turned, cosine, precision=highest)
    second = jnp.einsum("zfplkx,xq->zfplkq", turned, sine, precision=highest)
    return jnp.stack([first[0] + second[1], first[1] - second[0]])


def inverse(mixed, cosine, sine):
    first = jnp.einsum("lzfpkq,qx->zfplkx", mixed, cosine, precision=highest)
    second = jnp.einsum("lzfpkq,qx->zfplkx", mixed, sine, precision=highest)
    half_back = jnp.stack([first[0] - second[1], first[1] + second[0]])
    turned = lax.all_to_all(half_back, "lat", split_axis=5, concat_axis=4, tiled=True)
    first = jnp.einsum("zfplkx,ky->zfplxy", turned, cosine, precision=highest)
    second = jnp.einsum("zfplkx,ky->zfplxy", turned, sine, precision=highest)
    return jnp.stack([first[0] - second[1], first[1] + second[0]])


def couple_product(left, right):
    return jnp.einsum("foiyx,fpiyx->ofpyx", left, right, precision=highest)


def couple(kernel, spectra):
    real_part = couple_product(kernel[0], spectra[0]) - couple_product(kernel[1], spectra[1])
    imag_part = couple_product(kernel[0], spectra[1]) + couple_product(kernel[1], spectra[0])
    return jnp.stack([real_part, imag_part], axis=1)


def cmul(factor, field):
    return jnp.stack(
        [factor[0] * field[0] - factor[1] * field[1], factor[0] * field[1] + factor[1] * field[0]]
    )


def plain_device(source, contrast, green, efield, cell_class):
    cosine, sine = tables(source.shape[5])
    factor = contrast[:, :, None]
    field = source
    for step in range(ITERS):
        spectra = forward(cmul(factor, field), cosine, sine)
        mixed = lax.psum_scatter(couple(green, spectra), "layer", scatter_dimension=0, tiled=True)
        field = source + cmul(factor, inverse(mixed, cosine, sine))
    cell_terms = jnp.sum(efield[0] * field[0] - efield[1] * field[1], axis=(0, 1))
    cell = lax.psum(cell_terms, "freq")
    onehot = (cell_class[None] == jnp.arange(CLASSES, dtype=jnp.int32)[:, None, None, None]).astype(
        jnp.float32
    )
    local_sums = jnp.einsum("clxy,lxy->lc", onehot, cell_terms, precision=highest) / float(NXY)
    classes = lax.psum(local_sums, ("freq", "lat"))
    return (cell, classes)


VMEM_BYTES = 40 * 1024 * 1024


def split_tables(length, block):
    index = np.arange(length)
    angle = (index[:, None] * index[None, :] % length) * (2.0 * np.pi / length)
    both = np.stack([np.cos(angle), np.sin(angle)]) / math.sqrt(length)
    columns = both.reshape(2, length, length // block, block).transpose(2, 1, 0, 3)
    columns = columns.reshape(length // block, length, 2 * block)
    high = columns.astype(ml_dtypes.bfloat16)
    low = (columns - high.astype(np.float64)).astype(ml_dtypes.bfloat16)
    rows = (high.transpose(0, 2, 1), low.transpose(0, 2, 1))
    return (high, low), tuple(np.ascontiguousarray(part) for part in rows)


def halves(value):
    high = value.astype(jnp.bfloat16)
    return high, (value - high.astype(jnp.float32)).astype(jnp.bfloat16)


def product(left_high, left_low, right_high, right_low):
    def dot(left, right):
        return jnp.dot(left, right, preferred_element_type=jnp.float32)

    return dot(left_high, right_high) + (dot(left_high, right_low) + dot(left_low, right_high))


def along_y(real, imag, high_ref, low_ref, where, sign):
    rows = real.shape[0]
    high, low = halves(jnp.concatenate([real, imag], axis=0))
    got = product(high, low, high_ref[where], low_ref[where])
    width = got.shape[1] // 2
    out_real = got[:rows, :width] - sign * got[rows:, width:]
    out_imag = got[rows:, :width] + sign * got[:rows, width:]
    return out_real, out_imag


def along_x(high_ref, low_ref, where, high, low, sign):
    got = product(high_ref[where], low_ref[where], high, low)
    rows, width = got.shape[0] // 2, got.shape[1] // 2
    out_real = got[:rows, :width] - sign * got[rows:, width:]
    out_imag = got[:rows, width:] + sign * got[rows:, :width]
    return out_real, out_imag


def call(body, outs, args, specs, flops, scratch=()):
    sizes = sum(math.prod(o.shape) * 4 for o in outs)
    return pl.pallas_call(
        body,
        grid=(1,),
        out_shape=outs,
        in_specs=specs,
        out_specs=[whole(o.shape) for o in outs],
        scratch_shapes=list(scratch),
        compiler_params=pltpu.CompilerParams(vmem_limit_bytes=VMEM_BYTES),
        cost_estimate=pl.CostEstimate(flops=flops, bytes_accessed=2 * sizes, transcendentals=0),
    )(*args)


def whole(shape):
    return pl.BlockSpec(tuple(shape), lambda step: (0,) * len(shape))


def pick(shape, pol):
    return pl.BlockSpec((shape[0], 1) + tuple(shape[2:]), lambda step: (0, pol, 0, 0))


def f32(*shape):
    return jax.ShapeDtypeStruct(shape, jnp.float32)


def send(blocks, axis, size):
    got = [blocks[0]]
    for d in range(1, size):
        pairs = [(i, i ^ d) for i in range(size)]
        got.append(lax.ppermute(blocks[d], axis, pairs))
    return got


def forward_blocks(real, imag, high_ref, low_ref, out_refs):
    me = lax.axis_index("lat")
    for d, out in enumerate(out_refs):
        out[0], out[1] = along_y(real, imag, high_ref, low_ref, me ^ d, -1)


def start_body(lat, source, contrast, high_ref, low_ref, *outs):
    m_real, m_imag = contrast[0], contrast[1]
    b_real, b_imag = source[0, 0], source[1, 0]
    real = m_real * b_real - m_imag * b_imag
    imag = m_real * b_imag + m_imag * b_real
    forward_blocks(real, imag, high_ref, low_ref, outs)


def turn_body(green, out):
    for z in range(green.shape[0]):
        for o in range(green.shape[1]):
            out[z, o] = green[z, o].T


def couple_body(lat, layers, *refs):
    parts, (green, high_ref, low_ref), rest = refs[:lat], refs[lat : lat + 3], refs[lat + 3 :]
    outs, (high, low) = rest[:layers], rest[layers:]
    me, layer = lax.axis_index("lat"), lax.axis_index("layer")
    rows, width = parts[0].shape[1:]
    for d, part in enumerate(parts):
        at = pl.ds(pl.multiple_of((me ^ d) * rows, rows), rows)
        for z in range(2):
            high[at, z * width : (z + 1) * width], low[at, z * width : (z + 1) * width] = halves(part[z])
    right_high, right_low = high[...], low[...]
    for k in range(high_ref.shape[0]):
        real, imag = along_x(high_ref, low_ref, k, right_high, right_low, -1)
        at = slice(k * rows, (k + 1) * rows)
        for e, out in enumerate(outs):
            g_real, g_imag = green[0, layer ^ e, at], green[1, layer ^ e, at]
            out[0, at] = g_real * real - g_imag * imag
            out[1, at] = g_real * imag + g_imag * real


def back_body(lat, layers, *refs):
    parts, (high_ref, low_ref), outs = refs[:layers], refs[layers : layers + 2], refs[layers + 2 :]
    me = lax.axis_index("lat")
    mixed = [sum((part[z] for part in parts[1:]), parts[0][z]) for z in range(2)]
    high, low = halves(jnp.concatenate(mixed, axis=1))
    for d, out in enumerate(outs):
        out[0], out[1] = along_x(high_ref, low_ref, me ^ d, high, low, +1)


def gather_lanes(parts, field):
    me = lax.axis_index("lat")
    width = parts[0].shape[2]
    for d, part in enumerate(parts):
        at = pl.ds(pl.multiple_of((me ^ d) * width, width), width)
        for z in range(2):
            field[z, :, at] = part[z]


def update(parts, source, contrast, high_ref, low_ref, field):
    gather_lanes(parts, field)
    back_real, back_imag = field[0], field[1]
    width = parts[0].shape[2]
    for k in range(high_ref.shape[0]):
        real, imag = along_y(back_real, back_imag, high_ref, low_ref, k, +1)
        at = slice(k * width, (k + 1) * width)
        m_real, m_imag = contrast[0, :, at], contrast[1, :, at]
        field[0, :, at] = source[0, 0, :, at] + (m_real * real - m_imag * imag)
        field[1, :, at] = source[1, 0, :, at] + (m_real * imag + m_imag * real)


def again_body(lat, *refs):
    parts, (source, contrast, high_ref, low_ref), rest = refs[:lat], refs[lat : lat + 4], refs[lat + 4 :]
    outs, field = rest[:-1], rest[-1]
    update(parts, source, contrast, high_ref, low_ref, field)
    m_real, m_imag = contrast[0], contrast[1]
    real = m_real * field[0] - m_imag * field[1]
    imag = m_real * field[1] + m_imag * field[0]
    forward_blocks(real, imag, high_ref, low_ref, outs)


def end_body(lat, *refs):
    parts, (source, contrast, efield, high_ref, low_ref), rest = refs[:lat], refs[lat : lat + 5], refs[lat + 5 :]
    before, out, field = (rest[0] if len(rest) == 3 else None), rest[-2], rest[-1]
    update(parts, source, contrast, high_ref, low_ref, field)
    terms = efield[0, 0] * field[0] - efield[1, 0] * field[1]
    out[...] = terms if before is None else before[...] + terms


def deal_body(freqs, cell, kinds, *outs):
    me = lax.axis_index("freq")
    rows = cell.shape[0] // freqs
    sums = []
    for c in range(CLASSES):
        chosen = jnp.where(kinds[...] == c, cell[...], 0.0)
        sums.append(jnp.full((1, cell.shape[1]), jnp.sum(chosen), jnp.float32))
    table = jnp.concatenate(sums, axis=0)
    for d, out in enumerate(outs):
        out[:rows] = cell[pl.ds(pl.multiple_of((me ^ d) * rows, rows), rows)]
        out[rows:] = table


def add_body(*refs):
    parts, (cell, table) = refs[:-2], refs[-2:]
    total = sum((part[...] for part in parts[1:]), parts[0][...])
    rows = cell.shape[0]
    cell[...] = total[:rows]
    table[...] = total[rows:, : table.shape[1]]


def place_body(freqs, lat, *refs):
    blocks, tables, (cell, classes) = refs[:freqs], refs[freqs : freqs + lat], refs[freqs + lat :]
    me = lax.axis_index("freq")
    rows = blocks[0].shape[0]
    for d, block in enumerate(blocks):
        cell[pl.ds(pl.multiple_of((me ^ d) * rows, rows), rows)] = block[...]
    total = sum((table[...] for table in tables[1:]), tables[0][...])
    row = lax.broadcasted_iota(jnp.int32, total.shape, 0)
    lane = lax.broadcasted_iota(jnp.int32, total.shape, 1)
    line = jnp.sum(jnp.where(row == lane, total, 0.0), axis=0, keepdims=True)
    classes[...] = line[:, :CLASSES] / float(NXY)


def fast_device(sizes, source, contrast, green, efield, cell_class):
    freqs, layers, lat = sizes["freq"], sizes["layer"], sizes["lat"]
    pols, rows, length = source.shape[2], source.shape[4], source.shape[5]
    source = source.reshape(2, pols, rows, length)
    efield = efield.reshape(2, pols, rows, length)
    contrast = contrast.reshape(2, rows, length)
    green = green.reshape(2, layers, rows, length)
    kinds = cell_class.reshape(rows, length)
    (col_high, col_low), (row_high, row_low) = split_tables(length, rows)
    col = (jnp.asarray(col_high), jnp.asarray(col_low))
    row = (jnp.asarray(row_high), jnp.asarray(row_low))
    table_specs = [whole(col_high.shape)] * 2
    row_specs = [whole(row_high.shape)] * 2
    block = f32(2, rows, rows)
    spectrum = f32(2, length, rows)
    field = pltpu.VMEM((2, rows, length), jnp.float32)
    held = pltpu.VMEM((length, 2 * rows), jnp.bfloat16)
    stage_flops = 24 * rows * length * length

    turned = call(turn_body, [f32(2, layers, length, rows)], (green,), [whole(green.shape)], 1 << 20)[0]
    cells = None
    chains = []
    for p in range(pols):
        blocks = call(
            functools.partial(start_body, lat),
            [block] * lat,
            (source, contrast, *col),
            [pick(source.shape, p), whole(contrast.shape)] + table_specs,
            stage_flops,
        )
        chains.append(send(blocks, "lat", lat))
    for step in range(ITERS):
        for p in range(pols):
            partial = call(
                functools.partial(couple_body, lat, layers),
                [spectrum] * layers,
                (*chains[p], turned, *row),
                [whole(block.shape)] * lat + [whole(turned.shape)] + row_specs,
                stage_flops,
                [held, held],
            )
            chains[p] = send(partial, "layer", layers)
        for p in range(pols):
            blocks = call(
                functools.partial(back_body, lat, layers),
                [block] * lat,
                (*chains[p], *row),
                [whole(spectrum.shape)] * layers + row_specs,
                stage_flops,
            )
            chains[p] = send(blocks, "lat", lat)
        for p in range(pols):
            common = [whole(block.shape)] * lat + [pick(source.shape, p), whole(contrast.shape)]
            if step < ITERS - 1:
                blocks = call(
                    functools.partial(again_body, lat),
                    [block] * lat,
                    (*chains[p], source, contrast, *col),
                    common + table_specs,
                    2 * stage_flops,
                    [field],
                )
                chains[p] = send(blocks, "lat", lat)
            else:
                more = () if cells is None else (cells,)
                cells = call(
                    functools.partial(end_body, lat),
                    [f32(rows, length)],
                    (*chains[p], source, contrast, efield, *col, *more),
                    common + [pick(efield.shape, p)] + table_specs + [whole((rows, length))] * len(more),
                    stage_flops,
                    [field],
                )[0]
    share = rows // freqs
    dealt = call(
        functools.partial(deal_body, freqs),
        [f32(share + CLASSES, length)] * freqs,
        (cells, kinds),
        [whole((rows, length))] * 2,
        1 << 20,
    )
    dealt = send(dealt, "freq", freqs)
    own, table = call(
        add_body,
        [f32(share, length), f32(CLASSES, 128)],
        tuple(dealt),
        [whole((share + CLASSES, length))] * freqs,
        1 << 20,
    )
    blocks = send([own] * freqs, "freq", freqs)
    tables = send([table] * lat, "lat", lat)
    cell, classes = call(
        functools.partial(place_body, freqs, lat),
        [f32(rows, length), f32(1, CLASSES)],
        (*blocks, *tables),
        [whole((share, length))] * freqs + [whole((CLASSES, 128))] * lat,
        1 << 20,
    )
    return cell.reshape(1, rows, length), classes


def solution(mesh):
    whole_lanes = (
        NXY % (mesh.shape["lat"] * 128) == 0
        and all(mesh.shape[name] & (mesh.shape[name] - 1) == 0 for name in mesh.axis_names)
    )
    per_device = functools.partial(fast_device, dict(mesh.shape)) if whole_lanes else plain_device

    placed = (
        P(None, "freq", None, "layer", "lat", None),
        P(None, "freq", "layer", "lat", None),
        P(None, "freq", None, "layer", "lat", None),
        P(None, "freq", None, "layer", "lat", None),
        P("layer", "lat", None),
    )
    return jax.shard_map(
        per_device,
        mesh=mesh,
        in_specs=placed,
        out_specs=(P("layer", "lat", None), P("layer", None)),
        check_vma=False,
    )
```

```python
import functools
import math

import jax
import jax.numpy as jnp
import ml_dtypes
import numpy as np
from jax import lax
from jax.experimental import pallas as pl
from jax.experimental.pallas import tpu as pltpu
from jax.sharding import PartitionSpec as P

NXY = 512
ITERS = 2
CLASSES = 8


highest = lax.Precision.HIGHEST


def tables(length):
    index = jnp.arange(length, dtype=jnp.int32)
    phase = index[:, None] * index[None, :] % length
    angle = phase.astype(jnp.float32) * (2.0 * math.pi / length)
    factor = 1.0 / math.sqrt(length)
    return (jnp.cos(angle) * factor, jnp.sin(angle) * factor)


def forward(field, cosine, sine):
    first = jnp.einsum("zfplxy,yk->zfplkx", field, cosine, precision=highest)
    second = jnp.einsum("zfplxy,yk->zfplkx", field, sine, precision=highest)
    partial_spec = jnp.stack([first[0] + second[1], first[1] - second[0]])
    turned = lax.all_to_all(partial_spec, "lat", split_axis=4, concat_axis=5, tiled=True)
    first = jnp.einsum("zfplkx,xq->zfplkq", turned, cosine, precision=highest)
    second = jnp.einsum("zfplkx,xq->zfplkq", turned, sine, precision=highest)
    return jnp.stack([first[0] + second[1], first[1] - second[0]])


def inverse(mixed, cosine, sine):
    first = jnp.einsum("lzfpkq,qx->zfplkx", mixed, cosine, precision=highest)
    second = jnp.einsum("lzfpkq,qx->zfplkx", mixed, sine, precision=highest)
    half_back = jnp.stack([first[0] - second[1], first[1] + second[0]])
    turned = lax.all_to_all(half_back, "lat", split_axis=5, concat_axis=4, tiled=True)
    first = jnp.einsum("zfplkx,ky->zfplxy", turned, cosine, precision=highest)
    second = jnp.einsum("zfplkx,ky->zfplxy", turned, sine, precision=highest)
    return jnp.stack([first[0] - second[1], first[1] + second[0]])


def couple_product(left, right):
    return jnp.einsum("foiyx,fpiyx->ofpyx", left, right, precision=highest)


def couple(kernel, spectra):
    real_part = couple_product(kernel[0], spectra[0]) - couple_product(kernel[1], spectra[1])
    imag_part = couple_product(kernel[0], spectra[1]) + couple_product(kernel[1], spectra[0])
    return jnp.stack([real_part, imag_part], axis=1)


def cmul(factor, field):
    return jnp.stack(
        [factor[0] * field[0] - factor[1] * field[1], factor[0] * field[1] + factor[1] * field[0]]
    )


def plain_device(source, contrast, green, efield, cell_class):
    cosine, sine = tables(source.shape[5])
    factor = contrast[:, :, None]
    field = source
    for step in range(ITERS):
        spectra = forward(cmul(factor, field), cosine, sine)
        mixed = lax.psum_scatter(couple(green, spectra), "layer", scatter_dimension=0, tiled=True)
        field = source + cmul(factor, inverse(mixed, cosine, sine))
    cell_terms = jnp.sum(efield[0] * field[0] - efield[1] * field[1], axis=(0, 1))
    cell = lax.psum(cell_terms, "freq")
    onehot = (cell_class[None] == jnp.arange(CLASSES, dtype=jnp.int32)[:, None, None, None]).astype(
        jnp.float32
    )
    local_sums = jnp.einsum("clxy,lxy->lc", onehot, cell_terms, precision=highest) / float(NXY)
    classes = lax.psum(local_sums, ("freq", "lat"))
    return (cell, classes)


VMEM_BYTES = 40 * 1024 * 1024
FIRST_VMEM_BYTES = 62 * 1024 * 1024
PIECES = 2


def split_tables(length, block):
    index = np.arange(length)
    angle = (index[:, None] * index[None, :] % length) * (2.0 * np.pi / length)
    both = np.stack([np.cos(angle), np.sin(angle)]) / math.sqrt(length)
    columns = both.reshape(2, length, length // block, block).transpose(2, 1, 0, 3)
    columns = columns.reshape(length // block, length, 2 * block)
    high = columns.astype(ml_dtypes.bfloat16)
    low = (columns - high.astype(np.float64)).astype(ml_dtypes.bfloat16)
    rows = (high.transpose(0, 2, 1), low.transpose(0, 2, 1))
    return (high, low), tuple(np.ascontiguousarray(part) for part in rows)


def halves(value):
    high = value.astype(jnp.bfloat16)
    return high, (value - high.astype(jnp.float32)).astype(jnp.bfloat16)


def product(left_high, left_low, right_high, right_low):
    def dot(left, right):
        return jnp.dot(left, right, preferred_element_type=jnp.float32)

    return dot(left_high, right_high) + (dot(left_high, right_low) + dot(left_low, right_high))


def along_y(real, imag, high_ref, low_ref, where, sign):
    rows = real.shape[0]
    high, low = halves(jnp.concatenate([real, imag], axis=0))
    got = product(high, low, high_ref[where], low_ref[where])
    width = got.shape[1] // 2
    out_real = got[:rows, :width] - sign * got[rows:, width:]
    out_imag = got[rows:, :width] + sign * got[:rows, width:]
    return out_real, out_imag


def along_x(high_ref, low_ref, where, high, low, sign):
    got = product(high_ref[where], low_ref[where], high, low)
    rows, width = got.shape[0] // 2, got.shape[1] // 2
    out_real = got[:rows, :width] - sign * got[rows:, width:]
    out_imag = got[:rows, width:] + sign * got[rows:, :width]
    return out_real, out_imag


def call(body, outs, args, specs, flops, scratch=(), after=(), vmem=VMEM_BYTES):
    sizes = sum(math.prod(o.shape) * 4 for o in outs)
    taken, tied = len(args), len(after)

    def ordered(*refs):
        body(*refs[:taken], *refs[taken + tied :])

    return pl.pallas_call(
        ordered,
        grid=(1,),
        out_shape=outs,
        in_specs=list(specs) + [pl.BlockSpec(memory_space=pl.ANY)] * tied,
        out_specs=[whole(o.shape) for o in outs],
        scratch_shapes=list(scratch),
        compiler_params=pltpu.CompilerParams(vmem_limit_bytes=vmem),
        cost_estimate=pl.CostEstimate(flops=flops, bytes_accessed=2 * sizes, transcendentals=0),
    )(*args, *after)


def whole(shape):
    return pl.BlockSpec(tuple(shape), lambda step: (0,) * len(shape))


def pick(shape, pol):
    return pl.BlockSpec((shape[0], 1) + tuple(shape[2:]), lambda step: (0, pol, 0, 0))


def f32(*shape):
    return jax.ShapeDtypeStruct(shape, jnp.float32)


def send(blocks, axis, size):
    got = [blocks[0]]
    for d in range(1, size):
        pairs = [(i, i ^ d) for i in range(size)]
        got.append(lax.ppermute(blocks[d], axis, pairs))
    return got


def forward_blocks(real, imag, high_ref, low_ref, out_refs):
    me = lax.axis_index("lat")
    for d, out in enumerate(out_refs):
        out[0], out[1] = along_y(real, imag, high_ref, low_ref, me ^ d, -1)


def weighted(contrast, real, imag):
    m_real, m_imag = contrast[0], contrast[1]
    return m_real * real - m_imag * imag, m_real * imag + m_imag * real


def first_body(lat, source, contrast, high_ref, low_ref, *refs):
    outs, (field, factor, high, low, sems) = refs[:lat], refs[lat:]
    me = lax.axis_index("lat")
    copies = [
        pltpu.make_async_copy(source.at[:, 0], field, sems.at[0]),
        pltpu.make_async_copy(contrast, factor, sems.at[1]),
    ]
    for d in range(lat):
        copies.append(pltpu.make_async_copy(high_ref.at[me ^ d], high.at[d], sems.at[2 + 2 * d]))
        copies.append(pltpu.make_async_copy(low_ref.at[me ^ d], low.at[d], sems.at[3 + 2 * d]))
    for copy in copies:
        copy.start()
    copies[0].wait()
    copies[1].wait()
    real, imag = weighted(factor, field[0], field[1])
    for d, out in enumerate(outs):
        copies[2 + 2 * d].wait()
        copies[3 + 2 * d].wait()
        out[0], out[1] = along_y(real, imag, high, low, d, -1)


def start_body(lat, source, contrast, high_ref, low_ref, *outs):
    real, imag = weighted(contrast, source[0, 0], source[1, 0])
    forward_blocks(real, imag, high_ref, low_ref, outs)


def turn_body(green, out):
    for z in range(green.shape[0]):
        for o in range(green.shape[1]):
            out[z, o] = green[z, o].T


def couple_body(lat, layers, *refs):
    parts, (green, high_ref, low_ref), rest = refs[:lat], refs[lat : lat + 3], refs[lat + 3 :]
    outs, (high, low) = rest[:layers], rest[layers:]
    me, layer = lax.axis_index("lat"), lax.axis_index("layer")
    rows, width = parts[0].shape[1:]
    for d, part in enumerate(parts):
        at = pl.ds(pl.multiple_of((me ^ d) * rows, rows), rows)
        for z in range(2):
            high[at, z * width : (z + 1) * width], low[at, z * width : (z + 1) * width] = halves(part[z])
    right_high, right_low = high[...], low[...]
    for k in range(high_ref.shape[0]):
        real, imag = along_x(high_ref, low_ref, k, right_high, right_low, -1)
        at = slice(k * rows, (k + 1) * rows)
        for e, out in enumerate(outs):
            g_real, g_imag = green[0, layer ^ e, at], green[1, layer ^ e, at]
            out[0, at] = g_real * real - g_imag * imag
            out[1, at] = g_real * imag + g_imag * real


def back_body(lat, layers, *refs):
    parts, (high_ref, low_ref), outs = refs[:layers], refs[layers : layers + 2], refs[layers + 2 :]
    me = lax.axis_index("lat")
    mixed = [sum((part[z] for part in parts[1:]), parts[0][z]) for z in range(2)]
    high, low = halves(jnp.concatenate(mixed, axis=1))
    pieces = len(outs) // lat
    for d in range(lat):
        real, imag = along_x(high_ref, low_ref, me ^ d, high, low, +1)
        rows = real.shape[0] // pieces
        for h in range(pieces):
            out = outs[h * lat + d]
            out[0], out[1] = real[h * rows : (h + 1) * rows], imag[h * rows : (h + 1) * rows]


def gather_lanes(parts, field):
    me = lax.axis_index("lat")
    width = parts[0].shape[2]
    for d, part in enumerate(parts):
        at = pl.ds(pl.multiple_of((me ^ d) * width, width), width)
        for z in range(2):
            field[z, :, at] = part[z]


def update(parts, source, contrast, high_ref, low_ref, field):
    gather_lanes(parts, field)
    back_real, back_imag = field[0], field[1]
    width = parts[0].shape[2]
    for k in range(high_ref.shape[0]):
        real, imag = along_y(back_real, back_imag, high_ref, low_ref, k, +1)
        at = slice(k * width, (k + 1) * width)
        m_real, m_imag = contrast[0, :, at], contrast[1, :, at]
        field[0, :, at] = source[0, 0, :, at] + (m_real * real - m_imag * imag)
        field[1, :, at] = source[1, 0, :, at] + (m_real * imag + m_imag * real)


def again_body(lat, *refs):
    parts, (source, contrast, high_ref, low_ref), rest = refs[:lat], refs[lat : lat + 4], refs[lat + 4 :]
    outs, field = rest[:-1], rest[-1]
    update(parts, source, contrast, high_ref, low_ref, field)
    real, imag = weighted(contrast, field[0], field[1])
    forward_blocks(real, imag, high_ref, low_ref, outs)


def terms_of(parts, source, contrast, efield, high_ref, low_ref, field):
    update(parts, source, contrast, high_ref, low_ref, field)
    return efield[0, 0] * field[0] - efield[1, 0] * field[1]


def end_body(lat, *refs):
    parts, (source, contrast, efield, high_ref, low_ref), rest = refs[:lat], refs[lat : lat + 5], refs[lat + 5 :]
    before, out, field = (rest[0] if len(rest) == 3 else None), rest[-2], rest[-1]
    terms = terms_of(parts, source, contrast, efield, high_ref, low_ref, field)
    out[...] = terms if before is None else before[...] + terms


def deal_body(freqs, lat, last, *refs):
    parts, (source, contrast, efield, high_ref, low_ref), rest = refs[:lat], refs[lat : lat + 5], refs[lat + 5 :]
    before, kinds, rest = rest[0], rest[1], rest[2:]
    sums = None
    if last:
        sums, rest = rest[0], rest[1:]
    outs, rest = rest[:freqs], rest[freqs:]
    field, cell = rest[-2:]
    cell[...] = before[...] + terms_of(parts, source, contrast, efield, high_ref, low_ref, field)
    me = lax.axis_index("freq")
    rows, width = cell.shape[0] // freqs, 128
    lines = []
    for c in range(CLASSES):
        chosen = jnp.where(kinds[...] == c, cell[...], 0.0)
        lines.append(jnp.full((1, width), jnp.sum(chosen), jnp.float32))
    table = jnp.concatenate(lines, axis=0)
    if last:
        table = table + sums[...]
    else:
        rest[0][...] = table
    for d, out in enumerate(outs):
        block = cell[pl.ds(pl.multiple_of((me ^ d) * rows, rows), rows)]
        count = block.shape[1] // width
        for k in range(count):
            out[k * rows : (k + 1) * rows] = block[:, k * width : (k + 1) * width]
        if last:
            out[count * rows :] = table


def add_body(freqs, *refs):
    parts, outs = refs[:freqs], refs[freqs:]
    total = sum((part[...] for part in parts[1:]), parts[0][...])
    rows = outs[0].shape[0]
    outs[0][...] = total[:rows]
    if len(outs) > 1:
        outs[1][...] = total[rows:]


def place_body(freqs, lat, pieces, *refs):
    blocks, refs = refs[: freqs * pieces], refs[freqs * pieces :]
    tables, (cell, classes) = refs[:lat], refs[lat:]
    me = lax.axis_index("freq")
    width = blocks[0].shape[1]
    count = cell.shape[1] // width
    rows = blocks[0].shape[0] // count
    for h in range(pieces):
        for d in range(freqs):
            at = pl.multiple_of((h * freqs + (me ^ d)) * rows, rows)
            for k in range(count):
                piece = blocks[h * freqs + d][k * rows : (k + 1) * rows]
                cell[pl.ds(at, rows), k * width : (k + 1) * width] = piece
    total = sum((table[...] for table in tables[1:]), tables[0][...])
    row = lax.broadcasted_iota(jnp.int32, total.shape, 0)
    lane = lax.broadcasted_iota(jnp.int32, total.shape, 1)
    line = jnp.sum(jnp.where(row == lane, total, 0.0), axis=0, keepdims=True)
    classes[...] = line[:, :CLASSES] / float(NXY)


def fast_device(sizes, source, contrast, green, efield, cell_class):
    freqs, layers, lat = sizes["freq"], sizes["layer"], sizes["lat"]
    pols, rows, length = source.shape[2], source.shape[4], source.shape[5]
    source = source.reshape(2, pols, rows, length)
    efield = efield.reshape(2, pols, rows, length)
    contrast = contrast.reshape(2, rows, length)
    green = green.reshape(2, layers, rows, length)
    kinds = cell_class.reshape(rows, length)
    (col_high, col_low), (row_high, row_low) = split_tables(length, rows)
    col = (jnp.asarray(col_high), jnp.asarray(col_low))
    row = (jnp.asarray(row_high), jnp.asarray(row_low))
    table_specs = [whole(col_high.shape)] * 2
    row_specs = [whole(row_high.shape)] * 2
    block = f32(2, rows, rows)
    spectrum = f32(2, length, rows)
    held = pltpu.VMEM((length, 2 * rows), jnp.bfloat16)
    stage_flops = 24 * rows * length * length
    last = pols - 1
    order = []

    def kernel(body, outs, args, specs, flops=stage_flops, scratch=(), vmem=VMEM_BYTES):
        got = call(body, outs, args, specs, flops, scratch, tuple(order[-1:]), vmem)
        order.append(got[0])
        return got

    def start(p):
        if p > 0:
            body, scratch = functools.partial(start_body, lat), ()
            specs = [pick(source.shape, p), whole(contrast.shape)] + table_specs
        else:
            body = functools.partial(first_body, lat)
            specs = [pl.BlockSpec(memory_space=pltpu.HBM)] * 4
            scratch = [
                pltpu.VMEM((2, rows, length), jnp.float32),
                pltpu.VMEM((2, rows, length), jnp.float32),
                pltpu.VMEM(col_high.shape, jnp.bfloat16),
                pltpu.VMEM(col_low.shape, jnp.bfloat16),
                pltpu.SemaphoreType.DMA((2 + 2 * lat,)),
            ]
        vmem = VMEM_BYTES if p > 0 else FIRST_VMEM_BYTES
        got = kernel(body, [block] * lat, (source, contrast, *col), specs, scratch=scratch, vmem=vmem)
        return send(got, "lat", lat)

    def couple(parts):
        body = functools.partial(couple_body, lat, layers)
        specs = [whole(block.shape)] * lat + [whole(turned.shape)] + row_specs
        got = kernel(body, [spectrum] * layers, (*parts, turned, *row), specs, scratch=[held, held])
        return send(got, "layer", layers)

    def back(parts, pieces):
        body = functools.partial(back_body, lat, layers)
        outs = [f32(2, rows // pieces, rows)] * (lat * pieces)
        got = kernel(body, outs, (*parts, *row), [whole(spectrum.shape)] * layers + row_specs)
        return [send(got[h * lat : (h + 1) * lat], "lat", lat) for h in range(pieces)]

    def field_specs(p, count, h):
        return [whole((2, count, rows))] * lat + [
            pl.BlockSpec((2, 1, count, length), lambda step: (0, p, h, 0)),
            pl.BlockSpec((2, count, length), lambda step: (0, h, 0)),
        ]

    def again(p, parts):
        body = functools.partial(again_body, lat)
        scratch = [pltpu.VMEM((2, rows, length), jnp.float32)]
        args = (*parts, source, contrast, *col)
        got = kernel(body, [block] * lat, args, field_specs(p, rows, 0) + table_specs, 2 * stage_flops, scratch)
        return send(got, "lat", lat)

    def end(p, parts, cells):
        more = () if cells is None else (cells,)
        specs = field_specs(p, rows, 0) + [pick(efield.shape, p)] + table_specs + [whole((rows, length))] * len(more)
        args = (*parts, source, contrast, efield, *col, *more)
        scratch = [pltpu.VMEM((2, rows, length), jnp.float32)]
        return kernel(functools.partial(end_body, lat), [f32(rows, length)], args, specs, scratch=scratch)[0]

    def deal(parts, cells, h, sums):
        count = rows // PIECES
        share = count // freqs * (length // 128)
        final = h == PIECES - 1
        more = () if sums is None else (sums,)
        specs = field_specs(last, count, h)
        specs += [pl.BlockSpec((2, 1, count, length), lambda step: (0, last, h, 0))] + table_specs
        specs += [pl.BlockSpec((count, length), lambda step: (h, 0))] * 2 + [whole((CLASSES, 128))] * len(more)
        args = (*parts, source, contrast, efield, *col, cells, kinds, *more)
        outs = [f32(share + (CLASSES if final else 0), 128)] * freqs + ([] if final else [f32(CLASSES, 128)])
        scratch = [pltpu.VMEM((2, count, length), jnp.float32), pltpu.VMEM((count, length), jnp.float32)]
        body = functools.partial(deal_body, freqs, lat, final)
        got = kernel(body, outs, args, specs, scratch=scratch)
        return send(got[:freqs], "freq", freqs), (None if final else got[freqs])

    def add(dealt, final):
        share = rows // PIECES // freqs * (length // 128)
        outs = [f32(share, 128)] + ([f32(CLASSES, 128)] if final else [])
        return kernel(functools.partial(add_body, freqs), outs, tuple(dealt), [whole(dealt[0].shape)] * freqs, 1 << 16)

    chains = [start(p) for p in range(pols)]
    turned = kernel(turn_body, [f32(2, layers, length, rows)], (green,), [whole(green.shape)], 1 << 20)[0]
    chains = [couple(chain) for chain in chains]
    for step in range(ITERS - 1):
        turns = [None] * pols
        for p in range(pols):
            turns[p] = back(chains[p], 1)[0]
            if p > 0:
                chains[p - 1] = couple(turns[p - 1])
            turns[p] = again(p, turns[p])
        chains[last] = couple(turns[last])
    cells = None
    for p in range(last):
        cells = end(p, back(chains[p], 1)[0], cells)
    turned_back = back(chains[last], PIECES)
    dealt, sums = [], None
    for h in range(PIECES):
        got, sums = deal(turned_back[h], cells, h, sums)
        dealt.append(got)
    blocks = []
    for h in range(PIECES):
        own = add(dealt[h], h == PIECES - 1)
        blocks += send([own[0]] * freqs, "freq", freqs)
    tables = send([own[1]] * lat, "lat", lat)
    cell, classes = kernel(
        functools.partial(place_body, freqs, lat, PIECES),
        [f32(rows, length), f32(1, CLASSES)],
        (*blocks, *tables),
        [whole(blocks[0].shape)] * len(blocks) + [whole((CLASSES, 128))] * lat,
        1 << 16,
    )
    return cell.reshape(1, rows, length), classes


def solution(mesh):
    whole_lanes = (
        NXY % (mesh.shape["lat"] * 128) == 0
        and NXY % (mesh.shape["lat"] * mesh.shape["freq"] * PIECES * 8) == 0
        and all(mesh.shape[name] & (mesh.shape[name] - 1) == 0 for name in mesh.axis_names)
    )
    per_device = functools.partial(fast_device, dict(mesh.shape)) if whole_lanes else plain_device

    placed = (
        P(None, "freq", None, "layer", "lat", None),
        P(None, "freq", "layer", "lat", None),
        P(None, "freq", None, "layer", "lat", None),
        P(None, "freq", None, "layer", "lat", None),
        P("layer", "lat", None),
    )
    return jax.shard_map(
        per_device,
        mesh=mesh,
        in_specs=placed,
        out_specs=(P("layer", "lat", None), P("layer", None)),
        check_vma=False,
    )
```

```python
import functools
import math

import jax
import jax.numpy as jnp
import ml_dtypes
import numpy as np
from jax import lax
from jax.experimental import pallas as pl
from jax.experimental.pallas import tpu as pltpu
from jax.sharding import PartitionSpec as P

NXY = 512
ITERS = 2
CLASSES = 8


highest = lax.Precision.HIGHEST


def tables(length):
    index = jnp.arange(length, dtype=jnp.int32)
    phase = index[:, None] * index[None, :] % length
    angle = phase.astype(jnp.float32) * (2.0 * math.pi / length)
    factor = 1.0 / math.sqrt(length)
    return (jnp.cos(angle) * factor, jnp.sin(angle) * factor)


def forward(field, cosine, sine):
    first = jnp.einsum("zfplxy,yk->zfplkx", field, cosine, precision=highest)
    second = jnp.einsum("zfplxy,yk->zfplkx", field, sine, precision=highest)
    partial_spec = jnp.stack([first[0] + second[1], first[1] - second[0]])
    turned = lax.all_to_all(partial_spec, "lat", split_axis=4, concat_axis=5, tiled=True)
    first = jnp.einsum("zfplkx,xq->zfplkq", turned, cosine, precision=highest)
    second = jnp.einsum("zfplkx,xq->zfplkq", turned, sine, precision=highest)
    return jnp.stack([first[0] + second[1], first[1] - second[0]])


def inverse(mixed, cosine, sine):
    first = jnp.einsum("lzfpkq,qx->zfplkx", mixed, cosine, precision=highest)
    second = jnp.einsum("lzfpkq,qx->zfplkx", mixed, sine, precision=highest)
    half_back = jnp.stack([first[0] - second[1], first[1] + second[0]])
    turned = lax.all_to_all(half_back, "lat", split_axis=5, concat_axis=4, tiled=True)
    first = jnp.einsum("zfplkx,ky->zfplxy", turned, cosine, precision=highest)
    second = jnp.einsum("zfplkx,ky->zfplxy", turned, sine, precision=highest)
    return jnp.stack([first[0] - second[1], first[1] + second[0]])


def couple_product(left, right):
    return jnp.einsum("foiyx,fpiyx->ofpyx", left, right, precision=highest)


def couple(kernel, spectra):
    real_part = couple_product(kernel[0], spectra[0]) - couple_product(kernel[1], spectra[1])
    imag_part = couple_product(kernel[0], spectra[1]) + couple_product(kernel[1], spectra[0])
    return jnp.stack([real_part, imag_part], axis=1)


def cmul(factor, field):
    return jnp.stack(
        [factor[0] * field[0] - factor[1] * field[1], factor[0] * field[1] + factor[1] * field[0]]
    )


def plain_device(source, contrast, green, efield, cell_class):
    cosine, sine = tables(source.shape[5])
    factor = contrast[:, :, None]
    field = source
    for step in range(ITERS):
        spectra = forward(cmul(factor, field), cosine, sine)
        mixed = lax.psum_scatter(couple(green, spectra), "layer", scatter_dimension=0, tiled=True)
        field = source + cmul(factor, inverse(mixed, cosine, sine))
    cell_terms = jnp.sum(efield[0] * field[0] - efield[1] * field[1], axis=(0, 1))
    cell = lax.psum(cell_terms, "freq")
    onehot = (cell_class[None] == jnp.arange(CLASSES, dtype=jnp.int32)[:, None, None, None]).astype(
        jnp.float32
    )
    local_sums = jnp.einsum("clxy,lxy->lc", onehot, cell_terms, precision=highest) / float(NXY)
    classes = lax.psum(local_sums, ("freq", "lat"))
    return (cell, classes)


VMEM_BYTES = 40 * 1024 * 1024
CHUNKS = 2
PIECES = 2
FINE = 16


def small_tables(length):
    index = np.arange(length)

    def waves(first):
        angle = (first[:, None] * index[None, :] % length) * (2.0 * np.pi / length)
        return np.stack([np.cos(angle), np.sin(angle)])

    coarse = waves(index[::FINE]) / math.sqrt(length)
    return coarse.astype(np.float32), waves(index[:FINE]).astype(np.float32)


def halves(value):
    high = value.astype(jnp.bfloat16)
    return high, (value - high.astype(jnp.float32)).astype(jnp.bfloat16)


def product(left_high, left_low, right_high, right_low):
    def dot(left, right):
        return jnp.dot(left, right, preferred_element_type=jnp.float32)

    return dot(left_high, right_high) + (dot(left_high, right_low) + dot(left_low, right_high))


def along_y(real, imag, high_ref, low_ref, where, sign):
    rows = real.shape[0]
    high, low = halves(jnp.concatenate([real, imag], axis=0))
    got = product(high, low, high_ref[where], low_ref[where])
    width = got.shape[1] // 2
    out_real = got[:rows, :width] - sign * got[rows:, width:]
    out_imag = got[rows:, :width] + sign * got[:rows, width:]
    return out_real, out_imag


def swap(packed):
    return pltpu.roll(packed, packed.shape[1] // 2, 1)


def signs(shape, sign):
    lane = lax.broadcasted_iota(jnp.int32, shape, 1)
    return jnp.where(lane < shape[1] // 2, -float(sign), float(sign))


def along_x(high_ref, low_ref, where, high, low, sign):
    got = product(high_ref[where], low_ref[where], high, low)
    rows = got.shape[0] // 2
    return got[:rows] + signs((rows, got.shape[1]), sign) * swap(got[rows:])


def call(body, outs, args, specs, flops, scratch=(), after=(), vmem=VMEM_BYTES):
    sizes = sum(math.prod(o.shape) * 4 for o in outs)
    taken, tied = len(args), len(after)

    def ordered(*refs):
        body(*refs[:taken], *refs[taken + tied :])

    return pl.pallas_call(
        ordered,
        grid=(1,),
        out_shape=outs,
        in_specs=list(specs) + [pl.BlockSpec(memory_space=pl.ANY)] * tied,
        out_specs=[whole(o.shape) for o in outs],
        scratch_shapes=list(scratch),
        compiler_params=pltpu.CompilerParams(vmem_limit_bytes=vmem),
        cost_estimate=pl.CostEstimate(flops=flops, bytes_accessed=2 * sizes, transcendentals=0),
    )(*args, *after)


def whole(shape):
    return pl.BlockSpec(tuple(shape), lambda step: (0,) * len(shape))


def pick(shape, pol):
    return pl.BlockSpec((shape[0], 1) + tuple(shape[2:]), lambda step: (0, pol, 0, 0))


def f32(*shape):
    return jax.ShapeDtypeStruct(shape, jnp.float32)


def send(blocks, axis, size):
    got = [blocks[0]]
    for d in range(1, size):
        pairs = [(i, i ^ d) for i in range(size)]
        got.append(lax.ppermute(blocks[d], axis, pairs))
    return got


def table_body(coarse, fine, col_high, col_low, row_high, row_low):
    blocks, _, length = row_high.shape
    width = length // blocks
    f_real, f_imag = fine[0], fine[1]
    for a in range(coarse.shape[1]):
        c_real, c_imag = coarse[0, a : a + 1], coarse[1, a : a + 1]
        pair = (c_real * f_real - c_imag * f_imag, c_real * f_imag + c_imag * f_real)
        block, first = a * FINE // width, a * FINE % width
        for z, part in enumerate(pair):
            for value, row, col in zip(halves(part), (row_high, row_low), (col_high, col_low)):
                row[block, z * width + first : z * width + first + FINE] = value
                for k in range(blocks):
                    spot = slice(a * FINE, (a + 1) * FINE)
                    col[k, spot, z * width : (z + 1) * width] = value[:, k * width : (k + 1) * width]


def forward_blocks(lat, real, imag, high_ref, low_ref, out_refs):
    me = lax.axis_index("lat")
    for d in range(lat):
        got = along_y(real, imag, high_ref, low_ref, me ^ d, -1)
        half = got[0].shape[1] // CHUNKS
        for c in range(CHUNKS):
            pair = [part[:, c * half : (c + 1) * half] for part in got]
            out_refs[c * lat + d][...] = jnp.concatenate(pair, axis=1)


def weighted(contrast, real, imag):
    m_real, m_imag = contrast[0], contrast[1]
    return m_real * real - m_imag * imag, m_real * imag + m_imag * real


def start_body(lat, source, contrast, high_ref, low_ref, *outs):
    real, imag = weighted(contrast, source[0, 0], source[1, 0])
    forward_blocks(lat, real, imag, high_ref, low_ref, outs)


def turn_body(green, out):
    half = green.shape[2] // CHUNKS
    for o in range(green.shape[1]):
        for z in range(2):
            turned = green[z, o].T
            for c in range(CHUNKS):
                piece = turned[:, c * half : (c + 1) * half]
                out[z, o, c] = jnp.concatenate([piece if z == 0 else -piece, piece], axis=1)


def couple_body(lat, layers, *refs):
    parts, (green, high_ref, low_ref), rest = refs[:lat], refs[lat : lat + 3], refs[lat + 3 :]
    outs, (high, low) = rest[:layers], rest[layers:]
    me, layer = lax.axis_index("lat"), lax.axis_index("layer")
    rows = parts[0].shape[0]
    for d, part in enumerate(parts):
        at = pl.ds(pl.multiple_of((me ^ d) * rows, rows), rows)
        high[at], low[at] = halves(part[...])
    right_high, right_low = high[...], low[...]
    for k in range(high_ref.shape[0]):
        spectra = along_x(high_ref, low_ref, k, right_high, right_low, -1)
        swapped = swap(spectra)
        at = slice(k * rows, (k + 1) * rows)
        for e, out in enumerate(outs):
            out[at] = green[0, layer ^ e, 0, at] * spectra + green[1, layer ^ e, 0, at] * swapped


def back_body(lat, layers, *refs):
    parts, (high_ref, low_ref), outs = refs[:layers], refs[layers : layers + 2], refs[layers + 2 :]
    me = lax.axis_index("lat")
    high, low = halves(sum((part[...] for part in parts[1:]), parts[0][...]))
    pieces = len(outs) // lat
    for d in range(lat):
        got = along_x(high_ref, low_ref, me ^ d, high, low, +1)
        rows = got.shape[0] // pieces
        for h in range(pieces):
            outs[h * lat + d][...] = got[h * rows : (h + 1) * rows]


def gather_lanes(lat, parts, field):
    me = lax.axis_index("lat")
    half = parts[0].shape[1] // 2
    width = half * CHUNKS
    for d in range(lat):
        at = pl.ds(pl.multiple_of((me ^ d) * width, width), width)
        for z in range(2):
            pair = [parts[c * lat + d][:, z * half : (z + 1) * half] for c in range(CHUNKS)]
            field[z, :, at] = jnp.concatenate(pair, axis=1)


def update(lat, parts, source, contrast, high_ref, low_ref, field):
    gather_lanes(lat, parts, field)
    back_real, back_imag = field[0], field[1]
    width = high_ref.shape[2] // 2
    for k in range(high_ref.shape[0]):
        real, imag = along_y(back_real, back_imag, high_ref, low_ref, k, +1)
        at = slice(k * width, (k + 1) * width)
        m_real, m_imag = contrast[0, :, at], contrast[1, :, at]
        field[0, :, at] = source[0, 0, :, at] + (m_real * real - m_imag * imag)
        field[1, :, at] = source[1, 0, :, at] + (m_real * imag + m_imag * real)


def again_body(lat, *refs):
    count = lat * CHUNKS
    parts, (source, contrast, high_ref, low_ref), rest = refs[:count], refs[count : count + 4], refs[count + 4 :]
    outs, field = rest[:-1], rest[-1]
    update(lat, parts, source, contrast, high_ref, low_ref, field)
    real, imag = weighted(contrast, field[0], field[1])
    forward_blocks(lat, real, imag, high_ref, low_ref, outs)


def terms_of(lat, parts, source, contrast, efield, high_ref, low_ref, field):
    update(lat, parts, source, contrast, high_ref, low_ref, field)
    return efield[0, 0] * field[0] - efield[1, 0] * field[1]


def end_body(lat, *refs):
    count = lat * CHUNKS
    parts, (source, contrast, efield, high_ref, low_ref), rest = refs[:count], refs[count : count + 5], refs[count + 5 :]
    before, out, field = (rest[0] if len(rest) == 3 else None), rest[-2], rest[-1]
    terms = terms_of(lat, parts, source, contrast, efield, high_ref, low_ref, field)
    out[...] = terms if before is None else before[...] + terms


def deal_body(lat, last, *refs):
    count = lat * CHUNKS
    parts, (source, contrast, efield, high_ref, low_ref), rest = refs[:count], refs[count : count + 5], refs[count + 5 :]
    before, kinds, rest = rest[0], rest[1], rest[2:]
    sums = None
    if last:
        sums, rest = rest[0], rest[1:]
    gone, kept, table, field, cell = rest
    cell[...] = before[...] + terms_of(lat, parts, source, contrast, efield, high_ref, low_ref, field)
    bit = lax.axis_index("freq") & 1
    width = gone.shape[1]
    lines = []
    for c in range(CLASSES):
        chosen = jnp.where(kinds[...] == c, cell[...], 0.0)
        lines.append(jnp.full((1, width), jnp.sum(chosen), jnp.float32))
    found = jnp.concatenate(lines, axis=0)
    table[...] = found + sums[...] if last else found
    rows = cell.shape[0] // 2
    for which, out in ((1 - bit, gone), (bit, kept)):
        block = cell[pl.ds(pl.multiple_of(which * rows, rows), rows)]
        for k in range(block.shape[1] // width):
            out[k * rows : (k + 1) * rows] = block[:, k * width : (k + 1) * width]


def total_of(refs):
    return sum((ref[...] for ref in refs[1:]), refs[0][...])


def keep_body(tables, *refs):
    out = refs[-1]
    rows = refs[0].shape[0]
    out[:rows] = refs[0][...] + refs[1][...]
    if tables:
        out[rows:] = total_of(refs[2:-1])


def add_body(one, two, out):
    out[...] = one[...] + two[...]


def place_body(pieces, *refs):
    halves_of, (cell, classes) = refs[: 2 * pieces], refs[2 * pieces :]
    bit = lax.axis_index("freq") & 1
    width = halves_of[0].shape[1]
    count = cell.shape[1] // width
    rows = cell.shape[0] // (2 * pieces)
    for h in range(pieces):
        for which, ref in ((bit, halves_of[2 * h]), (1 - bit, halves_of[2 * h + 1])):
            at = pl.multiple_of((2 * h + which) * rows, rows)
            for k in range(count):
                cell[pl.ds(at, rows), k * width : (k + 1) * width] = ref[k * rows : (k + 1) * rows]
    total = halves_of[-2][count * rows :] + halves_of[-1][count * rows :]
    row = lax.broadcasted_iota(jnp.int32, total.shape, 0)
    lane = lax.broadcasted_iota(jnp.int32, total.shape, 1)
    line = jnp.sum(jnp.where(row == lane, total, 0.0), axis=0, keepdims=True)
    classes[...] = line[:, :CLASSES] / float(NXY)


def fast_device(sizes, source, contrast, green, efield, cell_class):
    freqs, layers, lat = sizes["freq"], sizes["layer"], sizes["lat"]
    pols, rows, length = source.shape[2], source.shape[4], source.shape[5]
    source = source.reshape(2, pols, rows, length)
    efield = efield.reshape(2, pols, rows, length)
    contrast = contrast.reshape(2, rows, length)
    green = green.reshape(2, layers, rows, length)
    kinds = cell_class.reshape(rows, length)
    packed = 2 * rows // CHUNKS
    col_shape, row_shape = (lat, length, 2 * rows), (lat, 2 * rows, length)
    table_specs, row_specs = [whole(col_shape)] * 2, [whole(row_shape)] * 2
    block = f32(rows, packed)
    spectrum = f32(length, packed)
    held = pltpu.VMEM((length, packed), jnp.bfloat16)
    full = pltpu.VMEM((2, rows, length), jnp.float32)
    stage_flops = 24 * rows * length * length
    last = pols - 1
    order = []

    def kernel(body, outs, args, specs, flops=stage_flops, scratch=()):
        got = call(body, outs, args, specs, flops, scratch, tuple(order[-1:]))
        order.append(got[0])
        return got

    def sent(got):
        return [send(got[c * lat : (c + 1) * lat], "lat", lat) for c in range(CHUNKS)]

    coarse, fine = small_tables(length)
    tables = kernel(
        table_body,
        [jax.ShapeDtypeStruct(shape, jnp.bfloat16) for shape in (col_shape,) * 2 + (row_shape,) * 2],
        (jnp.asarray(coarse), jnp.asarray(fine)),
        [whole(coarse.shape), whole(fine.shape)],
        1 << 20,
    )
    col, row = tuple(tables[:2]), tuple(tables[2:])

    def start(p):
        specs = [pick(source.shape, p), whole(contrast.shape)] + table_specs
        return sent(kernel(functools.partial(start_body, lat), [block] * (lat * CHUNKS), (source, contrast, *col), specs))

    def couple(parts, c):
        body = functools.partial(couple_body, lat, layers)
        piece = pl.BlockSpec((2, layers, 1, length, packed), lambda step: (0, 0, c, 0, 0))
        specs = [whole(block.shape)] * lat + [piece] + row_specs
        got = kernel(body, [spectrum] * layers, (*parts, turned, *row), specs, scratch=[held, held])
        return send(got, "layer", layers)

    def back(parts, pieces=1):
        body = functools.partial(back_body, lat, layers)
        outs = [f32(rows // pieces, packed)] * (lat * pieces)
        got = kernel(body, outs, (*parts, *row), [whole(spectrum.shape)] * layers + row_specs)
        return [send(got[h * lat : (h + 1) * lat], "lat", lat) for h in range(pieces)]

    def field_specs(p, count, h):
        return [
            pl.BlockSpec((2, 1, count, length), lambda step: (0, p, h, 0)),
            pl.BlockSpec((2, count, length), lambda step: (0, h, 0)),
        ]

    def again(p, chunks):
        parts = [part for chunk in chunks for part in chunk]
        body = functools.partial(again_body, lat)
        specs = [whole(block.shape)] * len(parts) + field_specs(p, rows, 0) + table_specs
        args = (*parts, source, contrast, *col)
        return sent(kernel(body, [block] * (lat * CHUNKS), args, specs, 2 * stage_flops, [full]))

    def end(p, chunks, cells):
        parts = [part for chunk in chunks for part in chunk]
        more = () if cells is None else (cells,)
        specs = [whole(block.shape)] * len(parts) + field_specs(p, rows, 0) + [pick(efield.shape, p)]
        specs += table_specs + [whole((rows, length))] * len(more)
        args = (*parts, source, contrast, efield, *col, *more)
        return kernel(functools.partial(end_body, lat), [f32(rows, length)], args, specs, scratch=[full])[0]

    def deal(chunks, cells, h, sums):
        count = rows // PIECES
        parts, specs = [], []
        for chunk in chunks:
            for part in chunk:
                first = h if part.shape[0] > count else 0
                parts.append(part)
                specs.append(pl.BlockSpec((count, packed), lambda step, first=first: (first, 0)))
        share = count // 2 * (length // 128)
        final = h == PIECES - 1
        more = (sums,) if final else ()
        specs += field_specs(last, count, h)
        specs += [pl.BlockSpec((2, 1, count, length), lambda step: (0, last, h, 0))] + table_specs
        specs += [pl.BlockSpec((count, length), lambda step: (h, 0))] * 2 + [whole((CLASSES, 128))] * len(more)
        args = (*parts, source, contrast, efield, *col, cells, kinds, *more)
        scratch = [pltpu.VMEM((2, count, length), jnp.float32), pltpu.VMEM((count, length), jnp.float32)]
        outs = [f32(share, 128)] * 2 + [f32(CLASSES, 128)]
        return kernel(functools.partial(deal_body, lat, final), outs, args, specs, scratch=scratch)

    def across(value, d):
        return lax.ppermute(value, "freq", [(i, i ^ d) for i in range(freqs)])

    def simple(body, shape, args):
        return kernel(body, [f32(*shape)], tuple(args), [whole(arg.shape) for arg in args], 1 << 16)[0]

    chains = [[None] * CHUNKS for p in range(pols)]
    ahead = start(0)
    turned = kernel(turn_body, [f32(2, layers, CHUNKS, length, packed)], (green,), [whole(green.shape)], 1 << 20)[0]
    for p in range(pols):
        chains[p][0] = couple(ahead[0], 0)
        later = start(p + 1) if p < last else None
        for c in range(1, CHUNKS):
            if p == 1:
                chains[0][c - 1] = back(chains[0][c - 1])[0]
            chains[p][c] = couple(ahead[c], c)
        ahead = later
    done = [CHUNKS - 1 if p == 0 and last > 0 else 0 for p in range(pols)]
    for step in range(ITERS - 1):
        moved = [None] * pols
        for p in range(pols):
            for c in range(done[p], CHUNKS):
                chains[p][c] = back(chains[p][c])[0]
                if p > 0 and c == done[p]:
                    chains[p - 1][0] = couple(moved[p - 1][0], 0)
                elif p > 0:
                    chains[p - 1][c] = couple(moved[p - 1][c], c)
            moved[p] = again(p, chains[p])
        for c in range(CHUNKS):
            chains[last][c] = couple(moved[last][c], c)
        done = [0] * pols
    cells = None
    for p in range(last):
        cells = end(p, [back(chains[p][c])[0] for c in range(CHUNKS)], cells)
    begun = [back(chains[last][c])[0] for c in range(CHUNKS - 1)]
    pieces = back(chains[last][CHUNKS - 1], PIECES)
    kept, came, sums = [None] * PIECES, [None] * PIECES, None
    for h in range(PIECES):
        gone, kept[h], sums = deal(begun + [pieces[h]], cells, h, sums)
        came[h] = across(gone, 1)
    sums = send([sums] * lat, "lat", lat)
    for h in range(PIECES):
        final = h == PIECES - 1
        more = sums if final else []
        shape = (kept[h].shape[0] + (CLASSES if final else 0), 128)
        kept[h] = simple(functools.partial(keep_body, final), shape, [kept[h], came[h], *more])
        came[h] = across(kept[h], 2) if freqs > 2 else None
    d = 2
    while d < freqs:
        for h in range(PIECES):
            kept[h] = simple(add_body, kept[h].shape, [kept[h], came[h]])
            came[h] = across(kept[h], 2 * d) if 2 * d < freqs else across(kept[h], 1)
        d *= 2
    both = [part for pair in zip(kept, came) for part in pair]
    cell, classes = kernel(
        functools.partial(place_body, PIECES),
        [f32(rows, length), f32(1, CLASSES)],
        tuple(both),
        [whole(part.shape) for part in both],
        1 << 16,
    )
    return cell.reshape(1, rows, length), classes


def solution(mesh):
    whole_lanes = (
        NXY % (mesh.shape["lat"] * 128) == 0
        and NXY % (mesh.shape["lat"] * CHUNKS * 64) == 0
        and NXY % (mesh.shape["lat"] * PIECES * 16) == 0
        and mesh.shape["freq"] > 1
        and all(mesh.shape[name] & (mesh.shape[name] - 1) == 0 for name in mesh.axis_names)
    )
    per_device = functools.partial(fast_device, dict(mesh.shape)) if whole_lanes else plain_device

    placed = (
        P(None, "freq", None, "layer", "lat", None),
        P(None, "freq", "layer", "lat", None),
        P(None, "freq", None, "layer", "lat", None),
        P(None, "freq", None, "layer", "lat", None),
        P("layer", "lat", None),
    )
    return jax.shard_map(
        per_device,
        mesh=mesh,
        in_specs=placed,
        out_specs=(P("layer", "lat", None), P("layer", None)),
        check_vma=False,
    )
```

```python
import functools
import math

import jax
import jax.numpy as jnp
import ml_dtypes
import numpy as np
from jax import lax
from jax.experimental import pallas as pl
from jax.experimental.pallas import tpu as pltpu
from jax.sharding import PartitionSpec as P

NXY = 512
ITERS = 2
CLASSES = 8


highest = lax.Precision.HIGHEST


def tables(length):
    index = jnp.arange(length, dtype=jnp.int32)
    phase = index[:, None] * index[None, :] % length
    angle = phase.astype(jnp.float32) * (2.0 * math.pi / length)
    factor = 1.0 / math.sqrt(length)
    return (jnp.cos(angle) * factor, jnp.sin(angle) * factor)


def forward(field, cosine, sine):
    first = jnp.einsum("zfplxy,yk->zfplkx", field, cosine, precision=highest)
    second = jnp.einsum("zfplxy,yk->zfplkx", field, sine, precision=highest)
    partial_spec = jnp.stack([first[0] + second[1], first[1] - second[0]])
    turned = lax.all_to_all(partial_spec, "lat", split_axis=4, concat_axis=5, tiled=True)
    first = jnp.einsum("zfplkx,xq->zfplkq", turned, cosine, precision=highest)
    second = jnp.einsum("zfplkx,xq->zfplkq", turned, sine, precision=highest)
    return jnp.stack([first[0] + second[1], first[1] - second[0]])


def inverse(mixed, cosine, sine):
    first = jnp.einsum("lzfpkq,qx->zfplkx", mixed, cosine, precision=highest)
    second = jnp.einsum("lzfpkq,qx->zfplkx", mixed, sine, precision=highest)
    half_back = jnp.stack([first[0] - second[1], first[1] + second[0]])
    turned = lax.all_to_all(half_back, "lat", split_axis=5, concat_axis=4, tiled=True)
    first = jnp.einsum("zfplkx,ky->zfplxy", turned, cosine, precision=highest)
    second = jnp.einsum("zfplkx,ky->zfplxy", turned, sine, precision=highest)
    return jnp.stack([first[0] - second[1], first[1] + second[0]])


def couple_product(left, right):
    return jnp.einsum("foiyx,fpiyx->ofpyx", left, right, precision=highest)


def couple(kernel, spectra):
    real_part = couple_product(kernel[0], spectra[0]) - couple_product(kernel[1], spectra[1])
    imag_part = couple_product(kernel[0], spectra[1]) + couple_product(kernel[1], spectra[0])
    return jnp.stack([real_part, imag_part], axis=1)


def cmul(factor, field):
    return jnp.stack(
        [factor[0] * field[0] - factor[1] * field[1], factor[0] * field[1] + factor[1] * field[0]]
    )


def plain_device(source, contrast, green, efield, cell_class):
    cosine, sine = tables(source.shape[5])
    factor = contrast[:, :, None]
    field = source
    for step in range(ITERS):
        spectra = forward(cmul(factor, field), cosine, sine)
        mixed = lax.psum_scatter(couple(green, spectra), "layer", scatter_dimension=0, tiled=True)
        field = source + cmul(factor, inverse(mixed, cosine, sine))
    cell_terms = jnp.sum(efield[0] * field[0] - efield[1] * field[1], axis=(0, 1))
    cell = lax.psum(cell_terms, "freq")
    onehot = (cell_class[None] == jnp.arange(CLASSES, dtype=jnp.int32)[:, None, None, None]).astype(
        jnp.float32
    )
    local_sums = jnp.einsum("clxy,lxy->lc", onehot, cell_terms, precision=highest) / float(NXY)
    classes = lax.psum(local_sums, ("freq", "lat"))
    return (cell, classes)


VMEM_BYTES = 40 * 1024 * 1024
FIRST_VMEM_BYTES = 62 * 1024 * 1024
FINE = 16


def small_tables(length):
    index = np.arange(length)

    def waves(first):
        angle = (first[:, None] * index[None, :] % length) * (2.0 * np.pi / length)
        return np.stack([np.cos(angle), np.sin(angle)])

    both = [waves(index[::FINE]) / math.sqrt(length), waves(index[:FINE])]
    return np.concatenate(both, axis=1).astype(np.float32)


def halves(value):
    high = value.astype(jnp.bfloat16)
    return high, (value - high.astype(jnp.float32)).astype(jnp.bfloat16)


def product(left_high, left_low, right_high, right_low):
    def dot(left, right):
        return jnp.dot(left, right, preferred_element_type=jnp.float32)

    return dot(left_high, right_high) + (dot(left_high, right_low) + dot(left_low, right_high))


def along_y(real, imag, high_ref, low_ref, where, sign):
    rows = real.shape[0]
    high, low = halves(jnp.concatenate([real, imag], axis=0))
    got = product(high, low, high_ref[where], low_ref[where])
    width = got.shape[1] // 2
    out_real = got[:rows, :width] - sign * got[rows:, width:]
    out_imag = got[rows:, :width] + sign * got[:rows, width:]
    return out_real, out_imag


def along_x(high_ref, low_ref, where, high, low, sign):
    got = product(high_ref[where], low_ref[where], high, low)
    rows, width = got.shape[0] // 2, got.shape[1] // 2
    out_real = got[:rows, :width] - sign * got[rows:, width:]
    out_imag = got[:rows, width:] + sign * got[rows:, :width]
    return out_real, out_imag


def call(body, outs, args, specs, flops, scratch=(), after=(), vmem=VMEM_BYTES):
    sizes = sum(math.prod(o.shape) * 4 for o in outs)
    taken, tied = len(args), len(after)

    def ordered(*refs):
        body(*refs[:taken], *refs[taken + tied :])

    return pl.pallas_call(
        ordered,
        grid=(1,),
        out_shape=outs,
        in_specs=list(specs) + [pl.BlockSpec(memory_space=pl.ANY)] * tied,
        out_specs=[whole(o.shape) for o in outs],
        scratch_shapes=list(scratch),
        compiler_params=pltpu.CompilerParams(vmem_limit_bytes=vmem),
        cost_estimate=pl.CostEstimate(flops=flops, bytes_accessed=2 * sizes, transcendentals=0),
    )(*args, *after)


def whole(shape):
    return pl.BlockSpec(tuple(shape), lambda step: (0,) * len(shape))


def pick(shape, pol):
    return pl.BlockSpec((shape[0], 1) + tuple(shape[2:]), lambda step: (0, pol, 0, 0))


def f32(*shape):
    return jax.ShapeDtypeStruct(shape, jnp.float32)


def send(blocks, axis, size):
    got = [blocks[0]] + [None] * (size - 1)
    for d in sorted(range(1, size), key=lambda d: (d < 2, d)):
        got[d] = lax.ppermute(blocks[d], axis, [(i, i ^ d) for i in range(size)])
    return got


def make_tables(small, col_high, col_low, row_high=None, row_low=None):
    blocks, length, width = col_high.shape
    width = width // 2
    steps = length // FINE
    f_real, f_imag = small[0, steps:], small[1, steps:]
    for a in range(steps):
        c_real, c_imag = small[0, a : a + 1], small[1, a : a + 1]
        pair = (c_real * f_real - c_imag * f_imag, c_real * f_imag + c_imag * f_real)
        block, first = a * FINE // width, a * FINE % width
        for z, part in enumerate(pair):
            for value, row, col in zip(halves(part), (row_high, row_low), (col_high, col_low)):
                if row is not None:
                    row[block, z * width + first : z * width + first + FINE] = value
                for k in range(blocks):
                    spot = slice(a * FINE, (a + 1) * FINE)
                    col[k, spot, z * width : (z + 1) * width] = value[:, k * width : (k + 1) * width]


def forward_blocks(real, imag, high_ref, low_ref, out_refs):
    me = lax.axis_index("lat")
    for d, out in enumerate(out_refs):
        out[0], out[1] = along_y(real, imag, high_ref, low_ref, me ^ d, -1)


def weighted(contrast, real, imag):
    m_real, m_imag = contrast[0], contrast[1]
    return m_real * real - m_imag * imag, m_real * imag + m_imag * real


def first_body(lat, source, contrast, small, *refs):
    outs, (field, factor, waves, high, low, sems) = refs[:lat], refs[lat:]
    copies = [
        pltpu.make_async_copy(small, waves, sems.at[0]),
        pltpu.make_async_copy(source.at[:, 0], field, sems.at[1]),
        pltpu.make_async_copy(contrast, factor, sems.at[2]),
    ]
    for copy in copies:
        copy.start()
    copies[0].wait()
    make_tables(waves, high, low)
    copies[1].wait()
    copies[2].wait()
    real, imag = weighted(factor, field[0], field[1])
    forward_blocks(real, imag, high, low, outs)


def start_body(lat, source, contrast, high_ref, low_ref, *outs):
    real, imag = weighted(contrast, source[0, 0], source[1, 0])
    forward_blocks(real, imag, high_ref, low_ref, outs)


def turn_body(green, out):
    for z in range(green.shape[0]):
        for o in range(green.shape[1]):
            out[z, o] = green[z, o].T


def couple_body(lat, layers, *refs):
    parts, (green, high_ref, low_ref), rest = refs[:lat], refs[lat : lat + 3], refs[lat + 3 :]
    outs, (high, low) = rest[:layers], rest[layers:]
    me, layer = lax.axis_index("lat"), lax.axis_index("layer")
    rows, width = parts[0].shape[1:]
    for d, part in enumerate(parts):
        at = pl.ds(pl.multiple_of((me ^ d) * rows, rows), rows)
        for z in range(2):
            high[at, z * width : (z + 1) * width], low[at, z * width : (z + 1) * width] = halves(part[z])
    right_high, right_low = high[...], low[...]
    for k in range(high_ref.shape[0]):
        real, imag = along_x(high_ref, low_ref, k, right_high, right_low, -1)
        at = slice(k * rows, (k + 1) * rows)
        for e, out in enumerate(outs):
            g_real, g_imag = green[0, layer ^ e, at], green[1, layer ^ e, at]
            out[0, at] = g_real * real - g_imag * imag
            out[1, at] = g_real * imag + g_imag * real


def back_body(lat, layers, *refs):
    parts, (high_ref, low_ref), outs = refs[:layers], refs[layers : layers + 2], refs[layers + 2 :]
    me = lax.axis_index("lat")
    mixed = [sum((part[z] for part in parts[1:]), parts[0][z]) for z in range(2)]
    high, low = halves(jnp.concatenate(mixed, axis=1))
    for d, out in enumerate(outs):
        out[0], out[1] = along_x(high_ref, low_ref, me ^ d, high, low, +1)


def gather_lanes(parts, field):
    me = lax.axis_index("lat")
    width = parts[0].shape[2]
    for d, part in enumerate(parts):
        at = pl.ds(pl.multiple_of((me ^ d) * width, width), width)
        for z in range(2):
            field[z, :, at] = part[z]


def update(parts, source, contrast, high_ref, low_ref, field):
    gather_lanes(parts, field)
    back_real, back_imag = field[0], field[1]
    width = parts[0].shape[2]
    for k in range(high_ref.shape[0]):
        real, imag = along_y(back_real, back_imag, high_ref, low_ref, k, +1)
        at = slice(k * width, (k + 1) * width)
        m_real, m_imag = contrast[0, :, at], contrast[1, :, at]
        field[0, :, at] = source[0, 0, :, at] + (m_real * real - m_imag * imag)
        field[1, :, at] = source[1, 0, :, at] + (m_real * imag + m_imag * real)


def again_body(lat, *refs):
    parts, (source, contrast, high_ref, low_ref), rest = refs[:lat], refs[lat : lat + 4], refs[lat + 4 :]
    outs, field = rest[:-1], rest[-1]
    update(parts, source, contrast, high_ref, low_ref, field)
    real, imag = weighted(contrast, field[0], field[1])
    forward_blocks(real, imag, high_ref, low_ref, outs)


def terms_of(parts, source, contrast, efield, high_ref, low_ref, field):
    update(parts, source, contrast, high_ref, low_ref, field)
    return efield[0, 0] * field[0] - efield[1, 0] * field[1]


def end_body(lat, *refs):
    parts, (source, contrast, efield, high_ref, low_ref), rest = refs[:lat], refs[lat : lat + 5], refs[lat + 5 :]
    before, out, field = (rest[0] if len(rest) == 3 else None), rest[-2], rest[-1]
    terms = terms_of(parts, source, contrast, efield, high_ref, low_ref, field)
    out[...] = terms if before is None else before[...] + terms


def deal_body(lat, *refs):
    parts, (source, contrast, efield, high_ref, low_ref), rest = refs[:lat], refs[lat : lat + 5], refs[lat + 5 :]
    before, kinds, gone, kept, table, field, cell = rest
    cell[...] = before[...] + terms_of(parts, source, contrast, efield, high_ref, low_ref, field)
    bit = lax.axis_index("freq") & 1
    width = table.shape[1]
    rows = cell.shape[0] // 2
    for which, out in ((1 - bit, gone), (bit, kept)):
        block = cell[pl.ds(pl.multiple_of(which * rows, rows), rows)]
        for k in range(block.shape[1] // width):
            out[k * rows : (k + 1) * rows] = block[:, k * width : (k + 1) * width]
    lines = []
    for c in range(CLASSES):
        chosen = jnp.where(kinds[...] == c, cell[...], 0.0)
        lines.append(jnp.full((1, width), jnp.sum(chosen), jnp.float32))
    table[...] = jnp.concatenate(lines, axis=0)


def keep_body(one, two, *refs):
    tables, out = refs[:-1], refs[-1]
    rows = one.shape[0]
    out[:rows] = one[...] + two[...]
    out[rows:] = sum((table[...] for table in tables[1:]), tables[0][...])


def add_body(one, two, out):
    out[...] = one[...] + two[...]


def place_body(own, other, cell, classes):
    bit = lax.axis_index("freq") & 1
    width = own.shape[1]
    count = cell.shape[1] // width
    rows = cell.shape[0] // 2
    for which, ref in ((bit, own), (1 - bit, other)):
        at = pl.ds(pl.multiple_of(which * rows, rows), rows)
        for k in range(count):
            cell[at, k * width : (k + 1) * width] = ref[k * rows : (k + 1) * rows]
    total = own[count * rows :] + other[count * rows :]
    row = lax.broadcasted_iota(jnp.int32, total.shape, 0)
    lane = lax.broadcasted_iota(jnp.int32, total.shape, 1)
    line = jnp.sum(jnp.where(row == lane, total, 0.0), axis=0, keepdims=True)
    classes[...] = line[:, :CLASSES] / float(NXY)


def fast_device(sizes, source, contrast, green, efield, cell_class):
    freqs, layers, lat = sizes["freq"], sizes["layer"], sizes["lat"]
    pols, rows, length = source.shape[2], source.shape[4], source.shape[5]
    source = source.reshape(2, pols, rows, length)
    efield = efield.reshape(2, pols, rows, length)
    contrast = contrast.reshape(2, rows, length)
    green = green.reshape(2, layers, rows, length)
    kinds = cell_class.reshape(rows, length)
    col_shape, row_shape = (lat, length, 2 * rows), (lat, 2 * rows, length)
    table_specs, row_specs = [whole(col_shape)] * 2, [whole(row_shape)] * 2
    block = f32(2, rows, rows)
    spectrum = f32(2, length, rows)
    held = pltpu.VMEM((length, 2 * rows), jnp.bfloat16)
    full = pltpu.VMEM((2, rows, length), jnp.float32)
    stage_flops = 24 * rows * length * length
    last = pols - 1
    order = []

    def kernel(body, outs, args, specs, flops=stage_flops, scratch=(), vmem=VMEM_BYTES):
        got = call(body, outs, args, specs, flops, scratch, tuple(order[-1:]), vmem)
        order.append(got[0])
        return got

    small = jnp.asarray(small_tables(length))

    def first():
        specs = [pl.BlockSpec(memory_space=pltpu.HBM)] * 3
        scratch = [
            full,
            full,
            pltpu.VMEM(small.shape, jnp.float32),
            pltpu.VMEM(col_shape, jnp.bfloat16),
            pltpu.VMEM(col_shape, jnp.bfloat16),
            pltpu.SemaphoreType.DMA((3,)),
        ]
        body = functools.partial(first_body, lat)
        args = (source, contrast, small)
        return send(kernel(body, [block] * lat, args, specs, scratch=scratch, vmem=FIRST_VMEM_BYTES), "lat", lat)

    def start(p):
        specs = [pick(source.shape, p), whole(contrast.shape)] + table_specs
        return send(kernel(functools.partial(start_body, lat), [block] * lat, (source, contrast, *col), specs), "lat", lat)

    def couple(parts):
        body = functools.partial(couple_body, lat, layers)
        specs = [whole(block.shape)] * lat + [whole(turned.shape)] + row_specs
        got = kernel(body, [spectrum] * layers, (*parts, turned, *row), specs, scratch=[held, held])
        return send(got, "layer", layers)

    def back(parts):
        body = functools.partial(back_body, lat, layers)
        specs = [whole(spectrum.shape)] * layers + row_specs
        return send(kernel(body, [block] * lat, (*parts, *row), specs), "lat", lat)

    def field_specs(p):
        return [whole(block.shape)] * lat + [pick(source.shape, p), whole(contrast.shape)]

    def again(p, parts):
        args = (*parts, source, contrast, *col)
        specs = field_specs(p) + table_specs
        got = kernel(functools.partial(again_body, lat), [block] * lat, args, specs, 2 * stage_flops, [full])
        return send(got, "lat", lat)

    def end(p, parts, cells):
        more = () if cells is None else (cells,)
        specs = field_specs(p) + [pick(efield.shape, p)] + table_specs + [whole((rows, length))] * len(more)
        args = (*parts, source, contrast, efield, *col, *more)
        return kernel(functools.partial(end_body, lat), [f32(rows, length)], args, specs, scratch=[full])[0]

    def deal(parts, cells):
        specs = field_specs(last) + [pick(efield.shape, last)] + table_specs + [whole((rows, length))] * 2
        args = (*parts, source, contrast, efield, *col, cells, kinds)
        outs = [f32(rows // 2 * (length // 128), 128)] * 2 + [f32(CLASSES, 128)]
        scratch = [full, pltpu.VMEM((rows, length), jnp.float32)]
        return kernel(functools.partial(deal_body, lat), outs, args, specs, scratch=scratch)

    def across(value, d):
        return lax.ppermute(value, "freq", [(i, i ^ d) for i in range(freqs)])

    def simple(body, shape, args):
        return kernel(body, [f32(*shape)], tuple(args), [whole(arg.shape) for arg in args], 1 << 16)[0]

    chains = [first()]
    tables = kernel(
        make_tables,
        [jax.ShapeDtypeStruct(shape, jnp.bfloat16) for shape in (col_shape,) * 2 + (row_shape,) * 2],
        (small,),
        [whole(small.shape)],
        1 << 20,
    )
    col, row = tuple(tables[:2]), tuple(tables[2:])
    chains += [start(p) for p in range(1, pols)]
    turned = kernel(turn_body, [f32(2, layers, length, rows)], (green,), [whole(green.shape)], 1 << 20)[0]
    chains = [couple(chain) for chain in chains]
    for step in range(ITERS - 1):
        turns = [None] * pols
        for p in range(pols):
            turns[p] = back(chains[p])
            if p > 0:
                chains[p - 1] = couple(turns[p - 1])
            turns[p] = again(p, turns[p])
        chains[last] = couple(turns[last])
    cells = jnp.zeros((rows, length), jnp.float32) if last == 0 else None
    for p in range(last):
        cells = end(p, back(chains[p]), cells)
    gone, kept, found = deal(back(chains[last]), cells)
    came = across(gone, 1)
    found = send([found] * lat, "lat", lat)
    kept = simple(keep_body, (kept.shape[0] + CLASSES, 128), [kept, came, *found])
    d = 2
    while d < freqs:
        kept = simple(add_body, kept.shape, [kept, across(kept, d)])
        d *= 2
    both = (kept, across(kept, 1))
    outs = [f32(rows, length), f32(1, CLASSES)]
    cell, classes = kernel(place_body, outs, both, [whole(part.shape) for part in both], 1 << 16)
    return cell.reshape(1, rows, length), classes


def solution(mesh):
    whole_lanes = (
        NXY % (mesh.shape["lat"] * 128) == 0
        and NXY % (mesh.shape["lat"] * 128) == 0
        and mesh.shape["freq"] > 1
        and all(mesh.shape[name] & (mesh.shape[name] - 1) == 0 for name in mesh.axis_names)
    )
    per_device = functools.partial(fast_device, dict(mesh.shape)) if whole_lanes else plain_device

    placed = (
        P(None, "freq", None, "layer", "lat", None),
        P(None, "freq", "layer", "lat", None),
        P(None, "freq", None, "layer", "lat", None),
        P(None, "freq", None, "layer", "lat", None),
        P("layer", "lat", None),
    )
    return jax.shard_map(
        per_device,
        mesh=mesh,
        in_specs=placed,
        out_specs=(P("layer", "lat", None), P("layer", None)),
        check_vma=False,
    )
```

```python
import functools
import math

import jax
import jax.numpy as jnp
import ml_dtypes
import numpy as np
from jax import lax
from jax.experimental import pallas as pl
from jax.experimental.pallas import tpu as pltpu
from jax.sharding import PartitionSpec as P

NXY = 512
ITERS = 2
CLASSES = 8


highest = lax.Precision.HIGHEST


def tables(length):
    index = jnp.arange(length, dtype=jnp.int32)
    phase = index[:, None] * index[None, :] % length
    angle = phase.astype(jnp.float32) * (2.0 * math.pi / length)
    factor = 1.0 / math.sqrt(length)
    return (jnp.cos(angle) * factor, jnp.sin(angle) * factor)


def forward(field, cosine, sine):
    first = jnp.einsum("zfplxy,yk->zfplkx", field, cosine, precision=highest)
    second = jnp.einsum("zfplxy,yk->zfplkx", field, sine, precision=highest)
    partial_spec = jnp.stack([first[0] + second[1], first[1] - second[0]])
    turned = lax.all_to_all(partial_spec, "lat", split_axis=4, concat_axis=5, tiled=True)
    first = jnp.einsum("zfplkx,xq->zfplkq", turned, cosine, precision=highest)
    second = jnp.einsum("zfplkx,xq->zfplkq", turned, sine, precision=highest)
    return jnp.stack([first[0] + second[1], first[1] - second[0]])


def inverse(mixed, cosine, sine):
    first = jnp.einsum("lzfpkq,qx->zfplkx", mixed, cosine, precision=highest)
    second = jnp.einsum("lzfpkq,qx->zfplkx", mixed, sine, precision=highest)
    half_back = jnp.stack([first[0] - second[1], first[1] + second[0]])
    turned = lax.all_to_all(half_back, "lat", split_axis=5, concat_axis=4, tiled=True)
    first = jnp.einsum("zfplkx,ky->zfplxy", turned, cosine, precision=highest)
    second = jnp.einsum("zfplkx,ky->zfplxy", turned, sine, precision=highest)
    return jnp.stack([first[0] - second[1], first[1] + second[0]])


def couple_product(left, right):
    return jnp.einsum("foiyx,fpiyx->ofpyx", left, right, precision=highest)


def couple(kernel, spectra):
    real_part = couple_product(kernel[0], spectra[0]) - couple_product(kernel[1], spectra[1])
    imag_part = couple_product(kernel[0], spectra[1]) + couple_product(kernel[1], spectra[0])
    return jnp.stack([real_part, imag_part], axis=1)


def cmul(factor, field):
    return jnp.stack(
        [factor[0] * field[0] - factor[1] * field[1], factor[0] * field[1] + factor[1] * field[0]]
    )


def plain_device(source, contrast, green, efield, cell_class):
    cosine, sine = tables(source.shape[5])
    factor = contrast[:, :, None]
    field = source
    for step in range(ITERS):
        spectra = forward(cmul(factor, field), cosine, sine)
        mixed = lax.psum_scatter(couple(green, spectra), "layer", scatter_dimension=0, tiled=True)
        field = source + cmul(factor, inverse(mixed, cosine, sine))
    cell_terms = jnp.sum(efield[0] * field[0] - efield[1] * field[1], axis=(0, 1))
    cell = lax.psum(cell_terms, "freq")
    onehot = (cell_class[None] == jnp.arange(CLASSES, dtype=jnp.int32)[:, None, None, None]).astype(
        jnp.float32
    )
    local_sums = jnp.einsum("clxy,lxy->lc", onehot, cell_terms, precision=highest) / float(NXY)
    classes = lax.psum(local_sums, ("freq", "lat"))
    return (cell, classes)


VMEM_BYTES = 40 * 1024 * 1024
FIRST_VMEM_BYTES = 62 * 1024 * 1024
FINE = 16


def small_tables(length):
    index = np.arange(length)

    def waves(first):
        angle = (first[:, None] * index[None, :] % length) * (2.0 * np.pi / length)
        return np.stack([np.cos(angle), np.sin(angle)])

    both = [waves(index[::FINE]) / math.sqrt(length), waves(index[:FINE])]
    return np.concatenate(both, axis=1).astype(np.float32)


def halves(value):
    high = value.astype(jnp.bfloat16)
    return high, (value - high.astype(jnp.float32)).astype(jnp.bfloat16)


def product(left_high, left_low, right_high, right_low):
    def dot(left, right):
        return jnp.dot(left, right, preferred_element_type=jnp.float32)

    return dot(left_high, right_high) + (dot(left_high, right_low) + dot(left_low, right_high))


def along_y(real, imag, high_ref, low_ref, where, sign):
    rows = real.shape[0]
    high, low = halves(jnp.concatenate([real, imag], axis=0))
    got = product(high, low, high_ref[where], low_ref[where])
    width = got.shape[1] // 2
    out_real = got[:rows, :width] - sign * got[rows:, width:]
    out_imag = got[rows:, :width] + sign * got[:rows, width:]
    return out_real, out_imag


def along_x(high_ref, low_ref, where, high, low, sign):
    got = product(high_ref[where], low_ref[where], high, low)
    rows, width = got.shape[0] // 2, got.shape[1] // 2
    out_real = got[:rows, :width] - sign * got[rows:, width:]
    out_imag = got[:rows, width:] + sign * got[rows:, :width]
    return out_real, out_imag


def call(body, outs, args, specs, flops, scratch=(), after=(), vmem=VMEM_BYTES):
    sizes = sum(math.prod(o.shape) * 4 for o in outs)
    taken, tied = len(args), len(after)

    def ordered(*refs):
        body(*refs[:taken], *refs[taken + tied :])

    return pl.pallas_call(
        ordered,
        grid=(1,),
        out_shape=outs,
        in_specs=list(specs) + [pl.BlockSpec(memory_space=pl.ANY)] * tied,
        out_specs=[whole(o.shape) for o in outs],
        scratch_shapes=list(scratch),
        compiler_params=pltpu.CompilerParams(vmem_limit_bytes=vmem),
        cost_estimate=pl.CostEstimate(flops=flops, bytes_accessed=2 * sizes, transcendentals=0),
    )(*args, *after)


def whole(shape):
    return pl.BlockSpec(tuple(shape), lambda step: (0,) * len(shape))


def pick(shape, pol):
    return pl.BlockSpec((shape[0], 1) + tuple(shape[2:]), lambda step: (0, pol, 0, 0))


def f32(*shape):
    return jax.ShapeDtypeStruct(shape, jnp.float32)


def turns(size):
    return sorted(range(size), key=lambda d: (d == 1, d))


def send(blocks, axis, size):
    got = [blocks[0]]
    for d, block in zip(turns(size)[1:], blocks[1:]):
        got.append(lax.ppermute(block, axis, [(i, i ^ d) for i in range(size)]))
    return got


def make_tables(small, col_high, col_low, row_high=None, row_low=None):
    blocks, length, width = col_high.shape
    width = width // 2
    steps = length // FINE
    f_real, f_imag = small[0, steps:], small[1, steps:]
    for a in range(steps):
        c_real, c_imag = small[0, a : a + 1], small[1, a : a + 1]
        pair = (c_real * f_real - c_imag * f_imag, c_real * f_imag + c_imag * f_real)
        block, first = a * FINE // width, a * FINE % width
        for z, part in enumerate(pair):
            for value, row, col in zip(halves(part), (row_high, row_low), (col_high, col_low)):
                if row is not None:
                    row[block, z * width + first : z * width + first + FINE] = value
                for k in range(blocks):
                    spot = slice(a * FINE, (a + 1) * FINE)
                    col[k, spot, z * width : (z + 1) * width] = value[:, k * width : (k + 1) * width]


def forward_blocks(real, imag, high_ref, low_ref, out_refs):
    me = lax.axis_index("lat")
    for d, out in zip(turns(len(out_refs)), out_refs):
        out[0], out[1] = along_y(real, imag, high_ref, low_ref, me ^ d, -1)


def weighted(contrast, real, imag):
    m_real, m_imag = contrast[0], contrast[1]
    return m_real * real - m_imag * imag, m_real * imag + m_imag * real


def first_body(lat, source, contrast, small, *refs):
    outs, (field, factor, waves, high, low, sems) = refs[:lat], refs[lat:]
    copies = [
        pltpu.make_async_copy(small, waves, sems.at[0]),
        pltpu.make_async_copy(source.at[:, 0], field, sems.at[1]),
        pltpu.make_async_copy(contrast, factor, sems.at[2]),
    ]
    for copy in copies:
        copy.start()
    copies[0].wait()
    make_tables(waves, high, low)
    copies[1].wait()
    copies[2].wait()
    real, imag = weighted(factor, field[0], field[1])
    forward_blocks(real, imag, high, low, outs)


def start_body(lat, source, contrast, high_ref, low_ref, *outs):
    real, imag = weighted(contrast, source[0, 0], source[1, 0])
    forward_blocks(real, imag, high_ref, low_ref, outs)


def turn_body(green, out):
    for z in range(green.shape[0]):
        for o in range(green.shape[1]):
            out[z, o] = green[z, o].T


def couple_body(lat, layers, *refs):
    parts, (green, high_ref, low_ref), rest = refs[:lat], refs[lat : lat + 3], refs[lat + 3 :]
    outs, (high, low) = rest[:layers], rest[layers:]
    me, layer = lax.axis_index("lat"), lax.axis_index("layer")
    rows, width = parts[0].shape[1:]
    for d, part in zip(turns(len(parts)), parts):
        at = pl.ds(pl.multiple_of((me ^ d) * rows, rows), rows)
        for z in range(2):
            high[at, z * width : (z + 1) * width], low[at, z * width : (z + 1) * width] = halves(part[z])
    right_high, right_low = high[...], low[...]
    for k in range(high_ref.shape[0]):
        real, imag = along_x(high_ref, low_ref, k, right_high, right_low, -1)
        at = slice(k * rows, (k + 1) * rows)
        for e, out in enumerate(outs):
            g_real, g_imag = green[0, layer ^ e, at], green[1, layer ^ e, at]
            out[0, at] = g_real * real - g_imag * imag
            out[1, at] = g_real * imag + g_imag * real


def back_body(lat, layers, *refs):
    parts, (high_ref, low_ref), outs = refs[:layers], refs[layers : layers + 2], refs[layers + 2 :]
    me = lax.axis_index("lat")
    mixed = [sum((part[z] for part in parts[1:]), parts[0][z]) for z in range(2)]
    high, low = halves(jnp.concatenate(mixed, axis=1))
    for d, out in zip(turns(lat), outs):
        out[0], out[1] = along_x(high_ref, low_ref, me ^ d, high, low, +1)


def gather_lanes(parts, field):
    me = lax.axis_index("lat")
    width = parts[0].shape[2]
    for d, part in zip(turns(len(parts)), parts):
        at = pl.ds(pl.multiple_of((me ^ d) * width, width), width)
        for z in range(2):
            field[z, :, at] = part[z]


def update(parts, source, contrast, high_ref, low_ref, field):
    gather_lanes(parts, field)
    back_real, back_imag = field[0], field[1]
    width = parts[0].shape[2]
    for k in range(high_ref.shape[0]):
        real, imag = along_y(back_real, back_imag, high_ref, low_ref, k, +1)
        at = slice(k * width, (k + 1) * width)
        m_real, m_imag = contrast[0, :, at], contrast[1, :, at]
        field[0, :, at] = source[0, 0, :, at] + (m_real * real - m_imag * imag)
        field[1, :, at] = source[1, 0, :, at] + (m_real * imag + m_imag * real)


def again_body(lat, *refs):
    parts, (source, contrast, high_ref, low_ref), rest = refs[:lat], refs[lat : lat + 4], refs[lat + 4 :]
    outs, field = rest[:-1], rest[-1]
    update(parts, source, contrast, high_ref, low_ref, field)
    real, imag = weighted(contrast, field[0], field[1])
    forward_blocks(real, imag, high_ref, low_ref, outs)


def terms_of(parts, source, contrast, efield, high_ref, low_ref, field):
    update(parts, source, contrast, high_ref, low_ref, field)
    return efield[0, 0] * field[0] - efield[1, 0] * field[1]


def end_body(lat, *refs):
    parts, (source, contrast, efield, high_ref, low_ref), rest = refs[:lat], refs[lat : lat + 5], refs[lat + 5 :]
    before, out, field = (rest[0] if len(rest) == 3 else None), rest[-2], rest[-1]
    terms = terms_of(parts, source, contrast, efield, high_ref, low_ref, field)
    out[...] = terms if before is None else before[...] + terms


def deal_body(lat, *refs):
    parts, (source, contrast, efield, high_ref, low_ref), rest = refs[:lat], refs[lat : lat + 5], refs[lat + 5 :]
    before, gone, kept, cell, field = rest
    cell[...] = before[...] + terms_of(parts, source, contrast, efield, high_ref, low_ref, field)
    bit = lax.axis_index("freq") & 1
    width = gone.shape[1]
    rows = cell.shape[0] // 2
    for which, out in ((1 - bit, gone), (bit, kept)):
        block = cell[pl.ds(pl.multiple_of(which * rows, rows), rows)]
        for k in range(block.shape[1] // width):
            out[k * rows : (k + 1) * rows] = block[:, k * width : (k + 1) * width]


def class_body(cell, kinds, table):
    lines = []
    for c in range(CLASSES):
        chosen = jnp.where(kinds[...] == c, cell[...], 0.0)
        lines.append(jnp.full((1, table.shape[1]), jnp.sum(chosen), jnp.float32))
    table[...] = jnp.concatenate(lines, axis=0)


def keep_body(one, two, *refs):
    tables, out = refs[:-1], refs[-1]
    rows = one.shape[0]
    out[:rows] = one[...] + two[...]
    out[rows:] = sum((table[...] for table in tables[1:]), tables[0][...])


def add_body(one, two, out):
    out[...] = one[...] + two[...]


def place_body(own, other, cell, classes):
    bit = lax.axis_index("freq") & 1
    width = own.shape[1]
    count = cell.shape[1] // width
    rows = cell.shape[0] // 2
    for which, ref in ((bit, own), (1 - bit, other)):
        at = pl.ds(pl.multiple_of(which * rows, rows), rows)
        for k in range(count):
            cell[at, k * width : (k + 1) * width] = ref[k * rows : (k + 1) * rows]
    total = own[count * rows :] + other[count * rows :]
    row = lax.broadcasted_iota(jnp.int32, total.shape, 0)
    lane = lax.broadcasted_iota(jnp.int32, total.shape, 1)
    line = jnp.sum(jnp.where(row == lane, total, 0.0), axis=0, keepdims=True)
    classes[...] = line[:, :CLASSES] / float(NXY)


def fast_device(sizes, source, contrast, green, efield, cell_class):
    freqs, layers, lat = sizes["freq"], sizes["layer"], sizes["lat"]
    pols, rows, length = source.shape[2], source.shape[4], source.shape[5]
    source = source.reshape(2, pols, rows, length)
    efield = efield.reshape(2, pols, rows, length)
    contrast = contrast.reshape(2, rows, length)
    green = green.reshape(2, layers, rows, length)
    kinds = cell_class.reshape(rows, length)
    col_shape, row_shape = (lat, length, 2 * rows), (lat, 2 * rows, length)
    table_specs, row_specs = [whole(col_shape)] * 2, [whole(row_shape)] * 2
    block = f32(2, rows, rows)
    spectrum = f32(2, length, rows)
    held = pltpu.VMEM((length, 2 * rows), jnp.bfloat16)
    full = pltpu.VMEM((2, rows, length), jnp.float32)
    stage_flops = 24 * rows * length * length
    last = pols - 1
    order = []

    def kernel(body, outs, args, specs, flops=stage_flops, scratch=(), vmem=VMEM_BYTES):
        got = call(body, outs, args, specs, flops, scratch, tuple(order[-1:]), vmem)
        order.append(got[0])
        return got

    small = jnp.asarray(small_tables(length))

    def first():
        specs = [pl.BlockSpec(memory_space=pltpu.HBM)] * 3
        scratch = [
            full,
            full,
            pltpu.VMEM(small.shape, jnp.float32),
            pltpu.VMEM(col_shape, jnp.bfloat16),
            pltpu.VMEM(col_shape, jnp.bfloat16),
            pltpu.SemaphoreType.DMA((3,)),
        ]
        body = functools.partial(first_body, lat)
        args = (source, contrast, small)
        return send(kernel(body, [block] * lat, args, specs, scratch=scratch, vmem=FIRST_VMEM_BYTES), "lat", lat)

    def start(p):
        specs = [pick(source.shape, p), whole(contrast.shape)] + table_specs
        return send(kernel(functools.partial(start_body, lat), [block] * lat, (source, contrast, *col), specs), "lat", lat)

    def couple(parts):
        body = functools.partial(couple_body, lat, layers)
        specs = [whole(block.shape)] * lat + [whole(turned.shape)] + row_specs
        got = kernel(body, [spectrum] * layers, (*parts, turned, *row), specs, scratch=[held, held])
        return send(got, "layer", layers)

    def back(parts):
        body = functools.partial(back_body, lat, layers)
        specs = [whole(spectrum.shape)] * layers + row_specs
        return send(kernel(body, [block] * lat, (*parts, *row), specs), "lat", lat)

    def field_specs(p):
        return [whole(block.shape)] * lat + [pick(source.shape, p), whole(contrast.shape)]

    def again(p, parts):
        args = (*parts, source, contrast, *col)
        specs = field_specs(p) + table_specs
        got = kernel(functools.partial(again_body, lat), [block] * lat, args, specs, 2 * stage_flops, [full])
        return send(got, "lat", lat)

    def end(p, parts, cells):
        more = () if cells is None else (cells,)
        specs = field_specs(p) + [pick(efield.shape, p)] + table_specs + [whole((rows, length))] * len(more)
        args = (*parts, source, contrast, efield, *col, *more)
        return kernel(functools.partial(end_body, lat), [f32(rows, length)], args, specs, scratch=[full])[0]

    def deal(parts, cells):
        specs = field_specs(last) + [pick(efield.shape, last)] + table_specs + [whole((rows, length))]
        args = (*parts, source, contrast, efield, *col, cells)
        outs = [f32(rows // 2 * (length // 128), 128)] * 2 + [f32(rows, length)]
        return kernel(functools.partial(deal_body, lat), outs, args, specs, scratch=[full])

    def across(value, d):
        return lax.ppermute(value, "freq", [(i, i ^ d) for i in range(freqs)])

    def simple(body, shape, args):
        return kernel(body, [f32(*shape)], tuple(args), [whole(arg.shape) for arg in args], 1 << 16)[0]

    chains = [first()]
    tables = kernel(
        make_tables,
        [jax.ShapeDtypeStruct(shape, jnp.bfloat16) for shape in (col_shape,) * 2 + (row_shape,) * 2],
        (small,),
        [whole(small.shape)],
        1 << 20,
    )
    col, row = tuple(tables[:2]), tuple(tables[2:])
    chains += [start(p) for p in range(1, pols)]
    turned = kernel(turn_body, [f32(2, layers, length, rows)], (green,), [whole(green.shape)], 1 << 20)[0]
    chains = [couple(chain) for chain in chains]
    for step in range(ITERS - 1):
        turns = [None] * pols
        for p in range(pols):
            turns[p] = back(chains[p])
            if p > 0:
                chains[p - 1] = couple(turns[p - 1])
            turns[p] = again(p, turns[p])
        chains[last] = couple(turns[last])
    cells = jnp.zeros((rows, length), jnp.float32) if last == 0 else None
    for p in range(last):
        cells = end(p, back(chains[p]), cells)
    gone, kept, terms = deal(back(chains[last]), cells)
    came = across(gone, 1)
    found = simple(class_body, (CLASSES, 128), [terms, kinds])
    found = send([found] * lat, "lat", lat)
    kept = simple(keep_body, (kept.shape[0] + CLASSES, 128), [kept, came, *found])
    d = 2
    while d < freqs:
        kept = simple(add_body, kept.shape, [kept, across(kept, d)])
        d *= 2
    both = (kept, across(kept, 1))
    outs = [f32(rows, length), f32(1, CLASSES)]
    cell, classes = kernel(place_body, outs, both, [whole(part.shape) for part in both], 1 << 16)
    return cell.reshape(1, rows, length), classes


def solution(mesh):
    whole_lanes = (
        NXY % (mesh.shape["lat"] * 128) == 0
        and NXY % (mesh.shape["lat"] * 128) == 0
        and mesh.shape["freq"] > 1
        and all(mesh.shape[name] & (mesh.shape[name] - 1) == 0 for name in mesh.axis_names)
    )
    per_device = functools.partial(fast_device, dict(mesh.shape)) if whole_lanes else plain_device

    placed = (
        P(None, "freq", None, "layer", "lat", None),
        P(None, "freq", "layer", "lat", None),
        P(None, "freq", None, "layer", "lat", None),
        P(None, "freq", None, "layer", "lat", None),
        P("layer", "lat", None),
    )
    return jax.shard_map(
        per_device,
        mesh=mesh,
        in_specs=placed,
        out_specs=(P("layer", "lat", None), P("layer", None)),
        check_vma=False,
    )
```

```python
import functools
import math

import jax
import jax.numpy as jnp
import ml_dtypes
import numpy as np
from jax import lax
from jax.experimental import pallas as pl
from jax.experimental.pallas import tpu as pltpu
from jax.sharding import PartitionSpec as P

NXY = 512
ITERS = 2
CLASSES = 8


highest = lax.Precision.HIGHEST


def tables(length):
    index = jnp.arange(length, dtype=jnp.int32)
    phase = index[:, None] * index[None, :] % length
    angle = phase.astype(jnp.float32) * (2.0 * math.pi / length)
    factor = 1.0 / math.sqrt(length)
    return (jnp.cos(angle) * factor, jnp.sin(angle) * factor)


def forward(field, cosine, sine):
    first = jnp.einsum("zfplxy,yk->zfplkx", field, cosine, precision=highest)
    second = jnp.einsum("zfplxy,yk->zfplkx", field, sine, precision=highest)
    partial_spec = jnp.stack([first[0] + second[1], first[1] - second[0]])
    turned = lax.all_to_all(partial_spec, "lat", split_axis=4, concat_axis=5, tiled=True)
    first = jnp.einsum("zfplkx,xq->zfplkq", turned, cosine, precision=highest)
    second = jnp.einsum("zfplkx,xq->zfplkq", turned, sine, precision=highest)
    return jnp.stack([first[0] + second[1], first[1] - second[0]])


def inverse(mixed, cosine, sine):
    first = jnp.einsum("lzfpkq,qx->zfplkx", mixed, cosine, precision=highest)
    second = jnp.einsum("lzfpkq,qx->zfplkx", mixed, sine, precision=highest)
    half_back = jnp.stack([first[0] - second[1], first[1] + second[0]])
    turned = lax.all_to_all(half_back, "lat", split_axis=5, concat_axis=4, tiled=True)
    first = jnp.einsum("zfplkx,ky->zfplxy", turned, cosine, precision=highest)
    second = jnp.einsum("zfplkx,ky->zfplxy", turned, sine, precision=highest)
    return jnp.stack([first[0] - second[1], first[1] + second[0]])


def couple_product(left, right):
    return jnp.einsum("foiyx,fpiyx->ofpyx", left, right, precision=highest)


def couple(kernel, spectra):
    real_part = couple_product(kernel[0], spectra[0]) - couple_product(kernel[1], spectra[1])
    imag_part = couple_product(kernel[0], spectra[1]) + couple_product(kernel[1], spectra[0])
    return jnp.stack([real_part, imag_part], axis=1)


def cmul(factor, field):
    return jnp.stack(
        [factor[0] * field[0] - factor[1] * field[1], factor[0] * field[1] + factor[1] * field[0]]
    )


def plain_device(source, contrast, green, efield, cell_class):
    cosine, sine = tables(source.shape[5])
    factor = contrast[:, :, None]
    field = source
    for step in range(ITERS):
        spectra = forward(cmul(factor, field), cosine, sine)
        mixed = lax.psum_scatter(couple(green, spectra), "layer", scatter_dimension=0, tiled=True)
        field = source + cmul(factor, inverse(mixed, cosine, sine))
    cell_terms = jnp.sum(efield[0] * field[0] - efield[1] * field[1], axis=(0, 1))
    cell = lax.psum(cell_terms, "freq")
    onehot = (cell_class[None] == jnp.arange(CLASSES, dtype=jnp.int32)[:, None, None, None]).astype(
        jnp.float32
    )
    local_sums = jnp.einsum("clxy,lxy->lc", onehot, cell_terms, precision=highest) / float(NXY)
    classes = lax.psum(local_sums, ("freq", "lat"))
    return (cell, classes)


VMEM_BYTES = 40 * 1024 * 1024
FIRST_VMEM_BYTES = 62 * 1024 * 1024
FINE = 16


def small_tables(length):
    index = np.arange(length)

    def waves(first):
        angle = (first[:, None] * index[None, :] % length) * (2.0 * np.pi / length)
        return np.stack([np.cos(angle), np.sin(angle)])

    both = [waves(index[::FINE]) / math.sqrt(length), waves(index[:FINE])]
    return np.concatenate(both, axis=1).astype(np.float32)


def halves(value):
    high = value.astype(jnp.bfloat16)
    return high, (value - high.astype(jnp.float32)).astype(jnp.bfloat16)


def product(left_high, left_low, right_high, right_low):
    def dot(left, right):
        return jnp.dot(left, right, preferred_element_type=jnp.float32)

    return dot(left_high, right_high) + (dot(left_high, right_low) + dot(left_low, right_high))


def along_y(real, imag, high_ref, low_ref, where, sign):
    rows = real.shape[0]
    high, low = halves(jnp.concatenate([real, imag], axis=0))
    got = product(high, low, high_ref[where], low_ref[where])
    width = got.shape[1] // 2
    out_real = got[:rows, :width] - sign * got[rows:, width:]
    out_imag = got[rows:, :width] + sign * got[:rows, width:]
    return out_real, out_imag


def along_x(high_ref, low_ref, where, high, low, sign):
    got = product(high_ref[where], low_ref[where], high, low)
    rows, width = got.shape[0] // 2, got.shape[1] // 2
    out_real = got[:rows, :width] - sign * got[rows:, width:]
    out_imag = got[:rows, width:] + sign * got[rows:, :width]
    return out_real, out_imag


def call(body, outs, args, specs, flops, scratch=(), after=(), vmem=VMEM_BYTES):
    sizes = sum(math.prod(o.shape) * 4 for o in outs)
    taken, tied = len(args), len(after)

    def ordered(*refs):
        body(*refs[:taken], *refs[taken + tied :])

    return pl.pallas_call(
        ordered,
        grid=(1,),
        out_shape=outs,
        in_specs=list(specs) + [pl.BlockSpec(memory_space=pl.ANY)] * tied,
        out_specs=[whole(o.shape) for o in outs],
        scratch_shapes=list(scratch),
        compiler_params=pltpu.CompilerParams(vmem_limit_bytes=vmem),
        cost_estimate=pl.CostEstimate(flops=flops, bytes_accessed=2 * sizes, transcendentals=0),
    )(*args, *after)


def whole(shape):
    return pl.BlockSpec(tuple(shape), lambda step: (0,) * len(shape))


def pick(shape, pol):
    return pl.BlockSpec((shape[0], 1) + tuple(shape[2:]), lambda step: (0, pol, 0, 0))


def f32(*shape):
    return jax.ShapeDtypeStruct(shape, jnp.float32)


def turns(size):
    return sorted(range(size), key=lambda d: (d == 1, d))


def send(blocks, axis, size):
    got = [blocks[0]]
    for d, block in zip(turns(size)[1:], blocks[1:]):
        got.append(lax.ppermute(block, axis, [(i, i ^ d) for i in range(size)]))
    return got


def make_tables(small, col_high, col_low, row_high=None, row_low=None):
    blocks, length, width = col_high.shape
    width = width // 2
    steps = length // FINE
    f_real, f_imag = small[0, steps:], small[1, steps:]
    for a in range(steps):
        c_real, c_imag = small[0, a : a + 1], small[1, a : a + 1]
        pair = (c_real * f_real - c_imag * f_imag, c_real * f_imag + c_imag * f_real)
        block, first = a * FINE // width, a * FINE % width
        for z, part in enumerate(pair):
            for value, row, col in zip(halves(part), (row_high, row_low), (col_high, col_low)):
                if row is not None:
                    row[block, z * width + first : z * width + first + FINE] = value
                for k in range(blocks):
                    spot = slice(a * FINE, (a + 1) * FINE)
                    col[k, spot, z * width : (z + 1) * width] = value[:, k * width : (k + 1) * width]


def forward_blocks(real, imag, high_ref, low_ref, out_refs, bits):
    me = lax.axis_index("lat")
    for d, out in zip(bits, out_refs):
        out[0], out[1] = along_y(real, imag, high_ref, low_ref, me ^ d, -1)


def weighted(contrast, real, imag):
    m_real, m_imag = contrast[0], contrast[1]
    return m_real * real - m_imag * imag, m_real * imag + m_imag * real


def first_body(lat, source, contrast, small, *refs):
    outs, (field, factor, waves, high, low, sems) = refs[:lat], refs[lat:]
    copies = [
        pltpu.make_async_copy(small, waves, sems.at[0]),
        pltpu.make_async_copy(source.at[:, 0], field, sems.at[1]),
        pltpu.make_async_copy(contrast, factor, sems.at[2]),
    ]
    for copy in copies:
        copy.start()
    copies[0].wait()
    make_tables(waves, high, low)
    copies[1].wait()
    copies[2].wait()
    real, imag = weighted(factor, field[0], field[1])
    forward_blocks(real, imag, high, low, outs, turns(lat))


def start_body(lat, source, contrast, high_ref, low_ref, *outs):
    real, imag = weighted(contrast, source[0, 0], source[1, 0])
    forward_blocks(real, imag, high_ref, low_ref, outs, turns(lat))


def turn_body(green, out):
    for z in range(green.shape[0]):
        for o in range(green.shape[1]):
            out[z, o] = green[z, o].T


def blocks_of(bits, width):
    me = lax.axis_index("lat")
    return [pl.ds(pl.multiple_of((me ^ d) * width, width), width) for d in bits]


def spectrum_part(parts, bits, high_ref, low_ref, k):
    columns = blocks_of(bits, parts[0].shape[1])
    high, low = halves(jnp.concatenate([jnp.concatenate([part[0], part[1]], axis=1) for part in parts], axis=0))
    table_high, table_low = [jnp.concatenate([ref[k, :, at] for at in columns], axis=1) for ref in (high_ref, low_ref)]
    got = product(table_high, table_low, high, low)
    rows, width = got.shape[0] // 2, got.shape[1] // 2
    return got[:rows, :width] + got[rows:, width:], got[:rows, width:] - got[rows:, :width]


def spectrum_body(bits, *refs):
    parts, (high_ref, low_ref, out) = refs[: len(bits)], refs[len(bits) :]
    rows = high_ref.shape[1] // 2
    for k in range(high_ref.shape[0]):
        at = slice(k * rows, (k + 1) * rows)
        out[0, at], out[1, at] = spectrum_part(parts, bits, high_ref, low_ref, k)


def couple_body(bits, *refs):
    parts, (begun, green, high_ref, low_ref), outs = refs[: len(bits)], refs[len(bits) : len(bits) + 4], refs[len(bits) + 4 :]
    layer = lax.axis_index("layer")
    rows = high_ref.shape[1] // 2
    for k in range(high_ref.shape[0]):
        at = slice(k * rows, (k + 1) * rows)
        real, imag = spectrum_part(parts, bits, high_ref, low_ref, k)
        real, imag = begun[0, at] + real, begun[1, at] + imag
        for e, out in enumerate(outs):
            g_real, g_imag = green[0, layer ^ e, at], green[1, layer ^ e, at]
            out[0, at] = g_real * real - g_imag * imag
            out[1, at] = g_real * imag + g_imag * real


def back_body(bits, layers, *refs):
    parts, (high_ref, low_ref), outs = refs[:layers], refs[layers : layers + 2], refs[layers + 2 :]
    me = lax.axis_index("lat")
    mixed = [sum((part[z] for part in parts[1:]), parts[0][z]) for z in range(2)]
    high, low = halves(jnp.concatenate(mixed, axis=1))
    for d, out in zip(bits, outs):
        out[0], out[1] = along_x(high_ref, low_ref, me ^ d, high, low, +1)


def field_part(parts, bits, high_ref, low_ref, k, rows):
    spots = blocks_of(bits, parts[0].shape[2])
    both = [jnp.concatenate([part[z, rows] for part in parts], axis=1) for z in range(2)]
    high, low = halves(jnp.concatenate(both, axis=0))
    table_high, table_low = [jnp.concatenate([ref[k, at] for at in spots], axis=0) for ref in (high_ref, low_ref)]
    got = product(high, low, table_high, table_low)
    count, width = got.shape[0] // 2, got.shape[1] // 2
    return got[:count, :width] - got[count:, width:], got[count:, :width] + got[:count, width:]


def field_body(bits, *refs):
    parts, (high_ref, low_ref, out) = refs[: len(bits)], refs[len(bits) :]
    width = high_ref.shape[2] // 2
    for k in range(high_ref.shape[0]):
        at = slice(k * width, (k + 1) * width)
        out[0, :, at], out[1, :, at] = field_part(parts, bits, high_ref, low_ref, k, slice(None))


def update(parts, bits, begun, source, contrast, high_ref, low_ref, field, rows=slice(None)):
    width = high_ref.shape[2] // 2
    for k in range(high_ref.shape[0]):
        at = slice(k * width, (k + 1) * width)
        real, imag = field_part(parts, bits, high_ref, low_ref, k, rows)
        real, imag = begun[0, rows, at] + real, begun[1, rows, at] + imag
        m_real, m_imag = contrast[0, rows, at], contrast[1, rows, at]
        field[0, :, at] = source[0, 0, rows, at] + (m_real * real - m_imag * imag)
        field[1, :, at] = source[1, 0, rows, at] + (m_real * imag + m_imag * real)


def again_body(lat, bits, *refs):
    parts, (begun, source, contrast, high_ref, low_ref), rest = refs[: len(bits)], refs[len(bits) : len(bits) + 5], refs[len(bits) + 5 :]
    out, ahead, field = rest
    update(parts, bits, begun, source, contrast, high_ref, low_ref, field)
    ahead[0], ahead[1] = weighted(contrast, field[0], field[1])
    forward_blocks(ahead[0], ahead[1], high_ref, low_ref, [out], turns(lat)[1:2])


def rest_body(bits, ahead, high_ref, low_ref, *outs):
    forward_blocks(ahead[0], ahead[1], high_ref, low_ref, outs, bits)


def end_body(bits, *refs):
    parts, rest = refs[: len(bits)], refs[len(bits) :]
    (begun, source, contrast, efield, high_ref, low_ref), rest = rest[:6], rest[6:]
    before, out, field = (rest[0] if len(rest) == 3 else None), rest[-2], rest[-1]
    update(parts, bits, begun, source, contrast, high_ref, low_ref, field)
    terms = efield[0, 0] * field[0] - efield[1, 0] * field[1]
    out[...] = terms if before is None else before[...] + terms


def half_rows(which, rows):
    return pl.ds(pl.multiple_of(which * rows, rows), rows)


def deal_body(bits, kept, *refs):
    parts, rest = refs[: len(bits)], refs[len(bits) :]
    begun, source, contrast, efield, high_ref, low_ref, before, out, field = rest
    bit = lax.axis_index("freq") & 1
    count = field.shape[1]
    at = half_rows(bit if kept else 1 - bit, count)
    update(parts, bits, begun, source, contrast, high_ref, low_ref, field, at)
    cell = before[at] + (efield[0, 0, at] * field[0] - efield[1, 0, at] * field[1])
    width = out.shape[1]
    for k in range(cell.shape[1] // width):
        out[k * count : (k + 1) * count] = cell[:, k * width : (k + 1) * width]


def class_body(gone, kept, kinds, table):
    bit = lax.axis_index("freq") & 1
    count, width = kinds.shape[0] // 2, gone.shape[1]
    spots = [slice(k * width, (k + 1) * width) for k in range(kinds.shape[1] // width)]
    sides = []
    for cell, which in ((gone, 1 - bit), (kept, bit)):
        sides.append((cell[...], jnp.concatenate([kinds[half_rows(which, count), at] for at in spots], axis=0)))
    lines = []
    for c in range(CLASSES):
        chosen = sum(jnp.where(kind == c, cell, 0.0) for cell, kind in sides)
        lines.append(jnp.full((1, width), jnp.sum(chosen), jnp.float32))
    table[...] = jnp.concatenate(lines, axis=0)


def keep_body(one, two, *refs):
    tables, out = refs[:-1], refs[-1]
    rows = one.shape[0]
    out[:rows] = one[...] + two[...]
    out[rows:] = sum((table[...] for table in tables[1:]), tables[0][...])


def add_body(one, two, out):
    out[...] = one[...] + two[...]


def place_body(own, other, cell, classes):
    bit = lax.axis_index("freq") & 1
    width = own.shape[1]
    count = cell.shape[1] // width
    rows = cell.shape[0] // 2
    for which, ref in ((bit, own), (1 - bit, other)):
        at = pl.ds(pl.multiple_of(which * rows, rows), rows)
        for k in range(count):
            cell[at, k * width : (k + 1) * width] = ref[k * rows : (k + 1) * rows]
    total = own[count * rows :] + other[count * rows :]
    row = lax.broadcasted_iota(jnp.int32, total.shape, 0)
    lane = lax.broadcasted_iota(jnp.int32, total.shape, 1)
    line = jnp.sum(jnp.where(row == lane, total, 0.0), axis=0, keepdims=True)
    classes[...] = line[:, :CLASSES] / float(NXY)


def fast_device(sizes, source, contrast, green, efield, cell_class):
    freqs, layers, lat = sizes["freq"], sizes["layer"], sizes["lat"]
    pols, rows, length = source.shape[2], source.shape[4], source.shape[5]
    source = source.reshape(2, pols, rows, length)
    efield = efield.reshape(2, pols, rows, length)
    contrast = contrast.reshape(2, rows, length)
    green = green.reshape(2, layers, rows, length)
    kinds = cell_class.reshape(rows, length)
    col_shape, row_shape = (lat, length, 2 * rows), (lat, 2 * rows, length)
    table_specs, row_specs = [whole(col_shape)] * 2, [whole(row_shape)] * 2
    block = f32(2, rows, rows)
    spectrum = f32(2, length, rows)
    full = pltpu.VMEM((2, rows, length), jnp.float32)
    stage_flops = 24 * rows * length * length
    last = pols - 1
    order = []
    bits, near = turns(lat), lat // 2

    def kernel(body, outs, args, specs, flops=stage_flops, scratch=(), vmem=VMEM_BYTES):
        got = call(body, outs, args, specs, flops, scratch, tuple(order[-1:]), vmem)
        order.append(got[0])
        return got

    small = jnp.asarray(small_tables(length))

    def first():
        specs = [pl.BlockSpec(memory_space=pltpu.HBM)] * 3
        scratch = [
            full,
            full,
            pltpu.VMEM(small.shape, jnp.float32),
            pltpu.VMEM(col_shape, jnp.bfloat16),
            pltpu.VMEM(col_shape, jnp.bfloat16),
            pltpu.SemaphoreType.DMA((3,)),
        ]
        body = functools.partial(first_body, lat)
        args = (source, contrast, small)
        return send(kernel(body, [block] * lat, args, specs, scratch=scratch, vmem=FIRST_VMEM_BYTES), "lat", lat)

    def start(p):
        specs = [pick(source.shape, p), whole(contrast.shape)] + table_specs
        return send(kernel(functools.partial(start_body, lat), [block] * lat, (source, contrast, *col), specs), "lat", lat)

    def couple(parts):
        specs = [whole(block.shape)] * near + row_specs
        begun = kernel(functools.partial(spectrum_body, bits[:near]), [spectrum], (*parts[:near], *row), specs)[0]
        specs = [whole(block.shape)] * (lat - near) + [whole(spectrum.shape), whole(turned.shape)] + row_specs
        body = functools.partial(couple_body, bits[near:])
        got = kernel(body, [spectrum] * layers, (*parts[near:], begun, turned, *row), specs)
        return send(got, "layer", layers)

    early, later = bits[1:2], bits[:1] + bits[2:]

    def turn_block(value, d):
        return lax.ppermute(value, "lat", [(i, i ^ d) for i in range(lat)])

    def merged(ahead, got):
        return [got[0], ahead] + [turn_block(value, d) for value, d in zip(got[1:], later[1:])]

    def back(parts):
        specs = [whole(spectrum.shape)] * layers + row_specs

        def some(chosen):
            body = functools.partial(back_body, chosen, layers)
            return kernel(body, [block] * len(chosen), (*parts, *row), specs, stage_flops * len(chosen) // lat)

        ahead = turn_block(some(early)[0], early[0])
        return merged(ahead, some(later))

    def fields(p, parts):
        specs = [whole(block.shape)] * near + table_specs
        begun = kernel(functools.partial(field_body, bits[:near]), [f32(2, rows, length)], (*parts[:near], *col), specs)[0]
        specs = [whole(block.shape)] * (lat - near) + [whole(begun.shape), pick(source.shape, p), whole(contrast.shape)]
        return (*parts[near:], begun, source, contrast), specs

    def again(p, parts):
        args, specs = fields(p, parts)
        outs = [block, f32(2, rows, length)]
        body = functools.partial(again_body, lat, bits[near:])
        got = kernel(body, outs, (*args, *col), specs + table_specs, stage_flops, [full])
        ahead = turn_block(got[0], early[0])
        body = functools.partial(rest_body, later)
        got = kernel(body, [block] * len(later), (got[1], *col), [whole((2, rows, length))] + table_specs)
        return merged(ahead, got)

    def end(p, parts, cells):
        more = () if cells is None else (cells,)
        args, specs = fields(p, parts)
        specs += [pick(efield.shape, p)] + table_specs + [whole((rows, length))] * len(more)
        args = (*args, efield, *col, *more)
        body = functools.partial(end_body, bits[near:])
        return kernel(body, [f32(rows, length)], args, specs, scratch=[full])[0]

    def deal(operands, cells, kept):
        args, specs = operands
        specs = specs + [pick(efield.shape, last)] + table_specs + [whole((rows, length))]
        args = (*args, efield, *col, cells)
        outs = [f32(rows // 2 * (length // 128), 128)]
        scratch = [pltpu.VMEM((2, rows // 2, length), jnp.float32)]
        body = functools.partial(deal_body, bits[near:], kept)
        return kernel(body, outs, args, specs, stage_flops // 2, scratch)[0]

    def across(value, d):
        return lax.ppermute(value, "freq", [(i, i ^ d) for i in range(freqs)])

    def simple(body, shape, args):
        return kernel(body, [f32(*shape)], tuple(args), [whole(arg.shape) for arg in args], 1 << 16)[0]

    chains = [first()]
    tables = kernel(
        make_tables,
        [jax.ShapeDtypeStruct(shape, jnp.bfloat16) for shape in (col_shape,) * 2 + (row_shape,) * 2],
        (small,),
        [whole(small.shape)],
        1 << 20,
    )
    col, row = tuple(tables[:2]), tuple(tables[2:])
    chains += [start(p) for p in range(1, pols)]
    turned = kernel(turn_body, [f32(2, layers, length, rows)], (green,), [whole(green.shape)], 1 << 20)[0]
    chains = [couple(chain) for chain in chains]
    for step in range(ITERS - 1):
        moved = [None] * pols
        for p in range(pols):
            moved[p] = back(chains[p])
            if p > 0:
                chains[p - 1] = couple(moved[p - 1])
            moved[p] = again(p, moved[p])
        chains[last] = couple(moved[last])
    cells = jnp.zeros((rows, length), jnp.float32) if last == 0 else None
    for p in range(last):
        cells = end(p, back(chains[p]), cells)
    final = fields(last, back(chains[last]))
    gone = deal(final, cells, False)
    came = across(gone, 1)
    kept = deal(final, cells, True)
    found = simple(class_body, (CLASSES, 128), [gone, kept, kinds])
    found = send([found] * lat, "lat", lat)
    kept = simple(keep_body, (kept.shape[0] + CLASSES, 128), [kept, came, *found])
    d = 2
    while d < freqs:
        kept = simple(add_body, kept.shape, [kept, across(kept, d)])
        d *= 2
    both = (kept, across(kept, 1))
    outs = [f32(rows, length), f32(1, CLASSES)]
    cell, classes = kernel(place_body, outs, both, [whole(part.shape) for part in both], 1 << 16)
    return cell.reshape(1, rows, length), classes


def solution(mesh):
    whole_lanes = (
        NXY % (mesh.shape["lat"] * 128) == 0
        and NXY % (mesh.shape["lat"] * 128) == 0
        and mesh.shape["freq"] > 1
        and all(mesh.shape[name] & (mesh.shape[name] - 1) == 0 for name in mesh.axis_names)
    )
    per_device = functools.partial(fast_device, dict(mesh.shape)) if whole_lanes else plain_device

    placed = (
        P(None, "freq", None, "layer", "lat", None),
        P(None, "freq", "layer", "lat", None),
        P(None, "freq", None, "layer", "lat", None),
        P(None, "freq", None, "layer", "lat", None),
        P("layer", "lat", None),
    )
    return jax.shard_map(
        per_device,
        mesh=mesh,
        in_specs=placed,
        out_specs=(P("layer", "lat", None), P("layer", None)),
        check_vma=False,
    )
```

```python
import functools
import math

import jax
import jax.numpy as jnp
import ml_dtypes
import numpy as np
from jax import lax
from jax.experimental import pallas as pl
from jax.experimental.pallas import tpu as pltpu
from jax.sharding import PartitionSpec as P

NXY = 512
ITERS = 2
CLASSES = 8


highest = lax.Precision.HIGHEST


def tables(length):
    index = jnp.arange(length, dtype=jnp.int32)
    phase = index[:, None] * index[None, :] % length
    angle = phase.astype(jnp.float32) * (2.0 * math.pi / length)
    factor = 1.0 / math.sqrt(length)
    return (jnp.cos(angle) * factor, jnp.sin(angle) * factor)


def forward(field, cosine, sine):
    first = jnp.einsum("zfplxy,yk->zfplkx", field, cosine, precision=highest)
    second = jnp.einsum("zfplxy,yk->zfplkx", field, sine, precision=highest)
    partial_spec = jnp.stack([first[0] + second[1], first[1] - second[0]])
    turned = lax.all_to_all(partial_spec, "lat", split_axis=4, concat_axis=5, tiled=True)
    first = jnp.einsum("zfplkx,xq->zfplkq", turned, cosine, precision=highest)
    second = jnp.einsum("zfplkx,xq->zfplkq", turned, sine, precision=highest)
    return jnp.stack([first[0] + second[1], first[1] - second[0]])


def inverse(mixed, cosine, sine):
    first = jnp.einsum("lzfpkq,qx->zfplkx", mixed, cosine, precision=highest)
    second = jnp.einsum("lzfpkq,qx->zfplkx", mixed, sine, precision=highest)
    half_back = jnp.stack([first[0] - second[1], first[1] + second[0]])
    turned = lax.all_to_all(half_back, "lat", split_axis=5, concat_axis=4, tiled=True)
    first = jnp.einsum("zfplkx,ky->zfplxy", turned, cosine, precision=highest)
    second = jnp.einsum("zfplkx,ky->zfplxy", turned, sine, precision=highest)
    return jnp.stack([first[0] - second[1], first[1] + second[0]])


def couple_product(left, right):
    return jnp.einsum("foiyx,fpiyx->ofpyx", left, right, precision=highest)


def couple(kernel, spectra):
    real_part = couple_product(kernel[0], spectra[0]) - couple_product(kernel[1], spectra[1])
    imag_part = couple_product(kernel[0], spectra[1]) + couple_product(kernel[1], spectra[0])
    return jnp.stack([real_part, imag_part], axis=1)


def cmul(factor, field):
    return jnp.stack(
        [factor[0] * field[0] - factor[1] * field[1], factor[0] * field[1] + factor[1] * field[0]]
    )


def plain_device(source, contrast, green, efield, cell_class):
    cosine, sine = tables(source.shape[5])
    factor = contrast[:, :, None]
    field = source
    for step in range(ITERS):
        spectra = forward(cmul(factor, field), cosine, sine)
        mixed = lax.psum_scatter(couple(green, spectra), "layer", scatter_dimension=0, tiled=True)
        field = source + cmul(factor, inverse(mixed, cosine, sine))
    cell_terms = jnp.sum(efield[0] * field[0] - efield[1] * field[1], axis=(0, 1))
    cell = lax.psum(cell_terms, "freq")
    onehot = (cell_class[None] == jnp.arange(CLASSES, dtype=jnp.int32)[:, None, None, None]).astype(
        jnp.float32
    )
    local_sums = jnp.einsum("clxy,lxy->lc", onehot, cell_terms, precision=highest) / float(NXY)
    classes = lax.psum(local_sums, ("freq", "lat"))
    return (cell, classes)


VMEM_BYTES = 40 * 1024 * 1024
FIRST_VMEM_BYTES = 62 * 1024 * 1024
FINE = 16
CHUNKS = 2


def small_tables(length):
    index = np.arange(length)

    def waves(first):
        angle = (first[:, None] * index[None, :] % length) * (2.0 * np.pi / length)
        return np.stack([np.cos(angle), np.sin(angle)])

    both = [waves(index[::FINE]) / math.sqrt(length), waves(index[:FINE])]
    return np.concatenate(both, axis=1).astype(np.float32)


def halves(value):
    high = value.astype(jnp.bfloat16)
    return high, (value - high.astype(jnp.float32)).astype(jnp.bfloat16)


def product(left_high, left_low, right_high, right_low):
    def dot(left, right):
        return jnp.dot(left, right, preferred_element_type=jnp.float32)

    return dot(left_high, right_high) + (dot(left_high, right_low) + dot(left_low, right_high))


def along_y(real, imag, high_ref, low_ref, where, sign):
    rows = real.shape[0]
    high, low = halves(jnp.concatenate([real, imag], axis=0))
    got = product(high, low, high_ref[where], low_ref[where])
    width = got.shape[1] // 2
    out_real = got[:rows, :width] - sign * got[rows:, width:]
    out_imag = got[rows:, :width] + sign * got[:rows, width:]
    return out_real, out_imag


def along_x(high_ref, low_ref, where, high, low, sign):
    got = product(high_ref[where], low_ref[where], high, low)
    rows, width = got.shape[0] // 2, got.shape[1] // 2
    out_real = got[:rows, :width] - sign * got[rows:, width:]
    out_imag = got[:rows, width:] + sign * got[rows:, :width]
    return out_real, out_imag


def call(body, outs, args, specs, flops, scratch=(), after=(), vmem=VMEM_BYTES):
    sizes = sum(math.prod(o.shape) * 4 for o in outs)
    taken, tied = len(args), len(after)

    def ordered(*refs):
        body(*refs[:taken], *refs[taken + tied :])

    return pl.pallas_call(
        ordered,
        grid=(1,),
        out_shape=outs,
        in_specs=list(specs) + [pl.BlockSpec(memory_space=pl.ANY)] * tied,
        out_specs=[whole(o.shape) for o in outs],
        scratch_shapes=list(scratch),
        compiler_params=pltpu.CompilerParams(vmem_limit_bytes=vmem),
        cost_estimate=pl.CostEstimate(flops=flops, bytes_accessed=2 * sizes, transcendentals=0),
    )(*args, *after)


def whole(shape):
    return pl.BlockSpec(tuple(shape), lambda step: (0,) * len(shape))


def pick(shape, pol):
    return pl.BlockSpec((shape[0], 1) + tuple(shape[2:]), lambda step: (0, pol, 0, 0))


def f32(*shape):
    return jax.ShapeDtypeStruct(shape, jnp.float32)


def turns(size):
    return sorted(range(size), key=lambda d: (d == 1, d))


def send(blocks, axis, size):
    got = [blocks[0]]
    for d, block in zip(turns(size)[1:], blocks[1:]):
        got.append(lax.ppermute(block, axis, [(i, i ^ d) for i in range(size)]))
    return got


def make_tables(small, col_high, col_low, row_high=None, row_low=None):
    blocks, length, width = col_high.shape
    width = width // 2
    steps = length // FINE
    f_real, f_imag = small[0, steps:], small[1, steps:]
    for a in range(steps):
        c_real, c_imag = small[0, a : a + 1], small[1, a : a + 1]
        pair = (c_real * f_real - c_imag * f_imag, c_real * f_imag + c_imag * f_real)
        block, first = a * FINE // width, a * FINE % width
        for z, part in enumerate(pair):
            for value, row, col in zip(halves(part), (row_high, row_low), (col_high, col_low)):
                if row is not None:
                    row[block, z * width + first : z * width + first + FINE] = value
                for k in range(blocks):
                    spot = slice(a * FINE, (a + 1) * FINE)
                    col[k, spot, z * width : (z + 1) * width] = value[:, k * width : (k + 1) * width]


def forward_blocks(real, imag, high_ref, low_ref, out_refs, bits):
    me = lax.axis_index("lat")
    for d, out in zip(bits, out_refs):
        out[0], out[1] = along_y(real, imag, high_ref, low_ref, me ^ d, -1)


def weighted(contrast, real, imag):
    m_real, m_imag = contrast[0], contrast[1]
    return m_real * real - m_imag * imag, m_real * imag + m_imag * real


def first_body(lat, source, contrast, small, *refs):
    outs, (field, factor, waves, high, low, sems) = refs[:lat], refs[lat:]
    copies = [
        pltpu.make_async_copy(small, waves, sems.at[0]),
        pltpu.make_async_copy(source.at[:, 0], field, sems.at[1]),
        pltpu.make_async_copy(contrast, factor, sems.at[2]),
    ]
    for copy in copies:
        copy.start()
    copies[0].wait()
    make_tables(waves, high, low)
    copies[1].wait()
    copies[2].wait()
    real, imag = weighted(factor, field[0], field[1])
    forward_blocks(real, imag, high, low, outs, turns(lat))


def start_body(lat, source, contrast, high_ref, low_ref, *outs):
    real, imag = weighted(contrast, source[0, 0], source[1, 0])
    forward_blocks(real, imag, high_ref, low_ref, outs, turns(lat))


def turn_body(green, out):
    for z in range(green.shape[0]):
        for o in range(green.shape[1]):
            out[z, o] = green[z, o].T


def blocks_of(bits, width):
    me = lax.axis_index("lat")
    return [pl.ds(pl.multiple_of((me ^ d) * width, width), width) for d in bits]


def spectrum_part(parts, bits, high_ref, low_ref, k):
    columns = blocks_of(bits, parts[0].shape[1])
    high, low = halves(jnp.concatenate([jnp.concatenate([part[0], part[1]], axis=1) for part in parts], axis=0))
    table_high, table_low = [jnp.concatenate([ref[k, :, at] for at in columns], axis=1) for ref in (high_ref, low_ref)]
    got = product(table_high, table_low, high, low)
    rows, width = got.shape[0] // 2, got.shape[1] // 2
    return got[:rows, :width] + got[rows:, width:], got[:rows, width:] - got[rows:, :width]


def spectrum_body(bits, *refs):
    parts, (high_ref, low_ref, out) = refs[: len(bits)], refs[len(bits) :]
    rows = high_ref.shape[1] // 2
    for k in range(high_ref.shape[0]):
        at = slice(k * rows, (k + 1) * rows)
        out[0, at], out[1, at] = spectrum_part(parts, bits, high_ref, low_ref, k)


def couple_body(bits, *refs):
    parts, (begun, green, high_ref, low_ref), outs = refs[: len(bits)], refs[len(bits) : len(bits) + 4], refs[len(bits) + 4 :]
    layer = lax.axis_index("layer")
    rows = high_ref.shape[1] // 2
    for k in range(high_ref.shape[0]):
        at = slice(k * rows, (k + 1) * rows)
        real, imag = spectrum_part(parts, bits, high_ref, low_ref, k)
        real, imag = begun[0, at] + real, begun[1, at] + imag
        chunks = len(outs) // green.shape[1]
        for e in range(green.shape[1]):
            g_real, g_imag = green[0, layer ^ e, at], green[1, layer ^ e, at]
            pair = (g_real * real - g_imag * imag, g_real * imag + g_imag * real)
            if chunks == 1:
                outs[e][0, at], outs[e][1, at] = pair
            else:
                half = real.shape[1] // chunks
                for c in range(chunks):
                    spot = slice(c * half, (c + 1) * half)
                    outs[e * chunks + c][at] = jnp.concatenate([part[:, spot] for part in pair], axis=1)


def back_body(bits, layers, *refs):
    parts, (high_ref, low_ref), outs = refs[:layers], refs[layers : layers + 2], refs[layers + 2 :]
    me = lax.axis_index("lat")
    mixed = [sum((part[z] for part in parts[1:]), parts[0][z]) for z in range(2)]
    high, low = halves(jnp.concatenate(mixed, axis=1))
    for d, out in zip(bits, outs):
        out[0], out[1] = along_x(high_ref, low_ref, me ^ d, high, low, +1)


def back_chunk_body(bits, layers, *refs):
    parts, (high_ref, low_ref), outs = refs[:layers], refs[layers : layers + 2], refs[layers + 2 :]
    me = lax.axis_index("lat")
    high, low = halves(sum((part[...] for part in parts[1:]), parts[0][...]))
    for d, out in zip(bits, outs):
        got = product(high_ref[me ^ d], low_ref[me ^ d], high, low)
        rows, width = got.shape[0] // 2, got.shape[1]
        lane = lax.broadcasted_iota(jnp.int32, (rows, width), 1)
        turned = pltpu.roll(got[rows:], width // 2, 1)
        out[...] = got[:rows] + jnp.where(lane < width // 2, -turned, turned)


def field_part(parts, bits, high_ref, low_ref, k, rows, chunk=None):
    if chunk is None:
        spots = blocks_of(bits, parts[0].shape[2])
        both = [jnp.concatenate([part[z, rows] for part in parts], axis=1) for z in range(2)]
    else:
        me = lax.axis_index("lat")
        half = parts[0].shape[1] // 2
        spots = [pl.ds(pl.multiple_of(((me ^ d) * CHUNKS + chunk) * half, half), half) for d in bits]
        lanes = [slice(z * half, (z + 1) * half) for z in range(2)]
        both = [jnp.concatenate([part[rows, at] for part in parts], axis=1) for at in lanes]
    high, low = halves(jnp.concatenate(both, axis=0))
    table_high, table_low = [jnp.concatenate([ref[k, at] for at in spots], axis=0) for ref in (high_ref, low_ref)]
    got = product(high, low, table_high, table_low)
    count, width = got.shape[0] // 2, got.shape[1] // 2
    return got[:count, :width] - got[count:, width:], got[:count, width:] + got[count:, :width]


def field_body(bits, chunk, *refs):
    parts, (high_ref, low_ref, out) = refs[: len(bits)], refs[len(bits) :]
    width = high_ref.shape[2] // 2
    for k in range(high_ref.shape[0]):
        at = slice(k * width, (k + 1) * width)
        out[0, :, at], out[1, :, at] = field_part(parts, bits, high_ref, low_ref, k, slice(None), chunk)


def update(parts, bits, begun, source, contrast, high_ref, low_ref, field, rows=slice(None), chunk=None):
    width = high_ref.shape[2] // 2
    for k in range(high_ref.shape[0]):
        at = slice(k * width, (k + 1) * width)
        real, imag = field_part(parts, bits, high_ref, low_ref, k, rows, chunk)
        real, imag = begun[0, rows, at] + real, begun[1, rows, at] + imag
        m_real, m_imag = contrast[0, rows, at], contrast[1, rows, at]
        field[0, :, at] = source[0, 0, rows, at] + (m_real * real - m_imag * imag)
        field[1, :, at] = source[1, 0, rows, at] + (m_real * imag + m_imag * real)


def again_body(lat, bits, *refs):
    parts, (begun, source, contrast, high_ref, low_ref), rest = refs[: len(bits)], refs[len(bits) : len(bits) + 5], refs[len(bits) + 5 :]
    out, ahead, field = rest
    update(parts, bits, begun, source, contrast, high_ref, low_ref, field)
    ahead[0], ahead[1] = weighted(contrast, field[0], field[1])
    forward_blocks(ahead[0], ahead[1], high_ref, low_ref, [out], turns(lat)[1:2])


def rest_body(bits, ahead, high_ref, low_ref, *outs):
    forward_blocks(ahead[0], ahead[1], high_ref, low_ref, outs, bits)


def end_body(bits, *refs):
    parts, rest = refs[: len(bits)], refs[len(bits) :]
    (begun, source, contrast, efield, high_ref, low_ref), rest = rest[:6], rest[6:]
    before, out, field = (rest[0] if len(rest) == 3 else None), rest[-2], rest[-1]
    update(parts, bits, begun, source, contrast, high_ref, low_ref, field)
    terms = efield[0, 0] * field[0] - efield[1, 0] * field[1]
    out[...] = terms if before is None else before[...] + terms


def half_rows(which, rows):
    return pl.ds(pl.multiple_of(which * rows, rows), rows)


def deal_body(bits, kept, *refs):
    parts, rest = refs[: len(bits)], refs[len(bits) :]
    begun, source, contrast, efield, high_ref, low_ref, before, out, field = rest
    bit = lax.axis_index("freq") & 1
    count = field.shape[1]
    at = half_rows(bit if kept else 1 - bit, count)
    update(parts, bits, begun, source, contrast, high_ref, low_ref, field, at, CHUNKS - 1)
    cell = before[at] + (efield[0, 0, at] * field[0] - efield[1, 0, at] * field[1])
    width = out.shape[1]
    for k in range(cell.shape[1] // width):
        out[k * count : (k + 1) * count] = cell[:, k * width : (k + 1) * width]


def class_body(gone, kept, kinds, table):
    bit = lax.axis_index("freq") & 1
    count, width = kinds.shape[0] // 2, gone.shape[1]
    spots = [slice(k * width, (k + 1) * width) for k in range(kinds.shape[1] // width)]
    sides = []
    for cell, which in ((gone, 1 - bit), (kept, bit)):
        sides.append((cell[...], jnp.concatenate([kinds[half_rows(which, count), at] for at in spots], axis=0)))
    lines = []
    for c in range(CLASSES):
        chosen = sum(jnp.where(kind == c, cell, 0.0) for cell, kind in sides)
        lines.append(jnp.full((1, width), jnp.sum(chosen), jnp.float32))
    table[...] = jnp.concatenate(lines, axis=0)


def keep_body(one, two, *refs):
    tables, out = refs[:-1], refs[-1]
    rows = one.shape[0]
    out[:rows] = one[...] + two[...]
    out[rows:] = sum((table[...] for table in tables[1:]), tables[0][...])


def add_body(one, two, out):
    out[...] = one[...] + two[...]


def place_body(own, other, cell, classes):
    bit = lax.axis_index("freq") & 1
    width = own.shape[1]
    count = cell.shape[1] // width
    rows = cell.shape[0] // 2
    for which, ref in ((bit, own), (1 - bit, other)):
        at = pl.ds(pl.multiple_of(which * rows, rows), rows)
        for k in range(count):
            cell[at, k * width : (k + 1) * width] = ref[k * rows : (k + 1) * rows]
    total = own[count * rows :] + other[count * rows :]
    row = lax.broadcasted_iota(jnp.int32, total.shape, 0)
    lane = lax.broadcasted_iota(jnp.int32, total.shape, 1)
    line = jnp.sum(jnp.where(row == lane, total, 0.0), axis=0, keepdims=True)
    classes[...] = line[:, :CLASSES] / float(NXY)


def fast_device(sizes, source, contrast, green, efield, cell_class):
    freqs, layers, lat = sizes["freq"], sizes["layer"], sizes["lat"]
    pols, rows, length = source.shape[2], source.shape[4], source.shape[5]
    source = source.reshape(2, pols, rows, length)
    efield = efield.reshape(2, pols, rows, length)
    contrast = contrast.reshape(2, rows, length)
    green = green.reshape(2, layers, rows, length)
    kinds = cell_class.reshape(rows, length)
    col_shape, row_shape = (lat, length, 2 * rows), (lat, 2 * rows, length)
    table_specs, row_specs = [whole(col_shape)] * 2, [whole(row_shape)] * 2
    block = f32(2, rows, rows)
    spectrum = f32(2, length, rows)
    full = pltpu.VMEM((2, rows, length), jnp.float32)
    stage_flops = 24 * rows * length * length
    last = pols - 1
    order = []
    bits, near = turns(lat), lat // 2

    def kernel(body, outs, args, specs, flops=stage_flops, scratch=(), vmem=VMEM_BYTES):
        got = call(body, outs, args, specs, flops, scratch, tuple(order[-1:]), vmem)
        order.append(got[0])
        return got

    small = jnp.asarray(small_tables(length))

    def first():
        specs = [pl.BlockSpec(memory_space=pltpu.HBM)] * 3
        scratch = [
            full,
            full,
            pltpu.VMEM(small.shape, jnp.float32),
            pltpu.VMEM(col_shape, jnp.bfloat16),
            pltpu.VMEM(col_shape, jnp.bfloat16),
            pltpu.SemaphoreType.DMA((3,)),
        ]
        body = functools.partial(first_body, lat)
        args = (source, contrast, small)
        return send(kernel(body, [block] * lat, args, specs, scratch=scratch, vmem=FIRST_VMEM_BYTES), "lat", lat)

    def start(p):
        specs = [pick(source.shape, p), whole(contrast.shape)] + table_specs
        return send(kernel(functools.partial(start_body, lat), [block] * lat, (source, contrast, *col), specs), "lat", lat)

    def couple(parts, chunks=1):
        specs = [whole(block.shape)] * near + row_specs
        begun = kernel(functools.partial(spectrum_body, bits[:near]), [spectrum], (*parts[:near], *row), specs)[0]
        specs = [whole(block.shape)] * (lat - near) + [whole(spectrum.shape), whole(turned.shape)] + row_specs
        body = functools.partial(couple_body, bits[near:])
        outs = [spectrum if chunks == 1 else f32(length, 2 * rows // chunks)] * (layers * chunks)
        got = kernel(body, outs, (*parts[near:], begun, turned, *row), specs)
        got = [send(got[c::chunks], "layer", layers) for c in range(chunks)]
        return got[0] if chunks == 1 else got

    early, later = bits[1:2], bits[:1] + bits[2:]

    def turn_block(value, d):
        return lax.ppermute(value, "lat", [(i, i ^ d) for i in range(lat)])

    def merged(ahead, got):
        return [got[0], ahead] + [turn_block(value, d) for value, d in zip(got[1:], later[1:])]

    def back(parts, chunk=False):
        specs = [whole(parts[0].shape)] * layers + row_specs

        def some(chosen):
            body = functools.partial(back_chunk_body if chunk else back_body, chosen, layers)
            outs = [f32(rows, parts[0].shape[1]) if chunk else block] * len(chosen)
            return kernel(body, outs, (*parts, *row), specs, stage_flops * len(chosen) // lat)

        ahead = turn_block(some(early)[0], early[0])
        return merged(ahead, some(later))

    def fields(p, parts):
        specs = [whole(block.shape)] * near + table_specs
        begun = kernel(functools.partial(field_body, bits[:near], None), [f32(2, rows, length)], (*parts[:near], *col), specs)[0]
        specs = [whole(block.shape)] * (lat - near) + [whole(begun.shape), pick(source.shape, p), whole(contrast.shape)]
        return (*parts[near:], begun, source, contrast), specs

    def again(p, parts):
        args, specs = fields(p, parts)
        outs = [block, f32(2, rows, length)]
        body = functools.partial(again_body, lat, bits[near:])
        got = kernel(body, outs, (*args, *col), specs + table_specs, stage_flops, [full])
        ahead = turn_block(got[0], early[0])
        body = functools.partial(rest_body, later)
        got = kernel(body, [block] * len(later), (got[1], *col), [whole((2, rows, length))] + table_specs)
        return merged(ahead, got)

    def end(p, operands, cells):
        more = () if cells is None else (cells,)
        args, specs = operands
        specs += [pick(efield.shape, p)] + table_specs + [whole((rows, length))] * len(more)
        args = (*args, efield, *col, *more)
        body = functools.partial(end_body, bits[near:])
        return kernel(body, [f32(rows, length)], args, specs, scratch=[full])[0]

    def chunk_fields(p, chunks):
        parts = chunks[0]
        packed = [whole(part.shape) for part in parts]
        body = functools.partial(field_body, bits, 0)
        begun = kernel(body, [f32(2, rows, length)], (*parts, *col), packed + table_specs)[0]
        specs = packed + [whole(begun.shape), pick(source.shape, p), whole(contrast.shape)]
        return (*chunks[1], begun, source, contrast), specs

    def deal(operands, cells, kept):
        args, specs = operands
        specs = specs + [pick(efield.shape, last)] + table_specs + [whole((rows, length))]
        args = (*args, efield, *col, cells)
        outs = [f32(rows // 2 * (length // 128), 128)]
        scratch = [pltpu.VMEM((2, rows // 2, length), jnp.float32)]
        body = functools.partial(deal_body, bits, kept)
        return kernel(body, outs, args, specs, stage_flops // 2, scratch)[0]

    def across(value, d):
        return lax.ppermute(value, "freq", [(i, i ^ d) for i in range(freqs)])

    def simple(body, shape, args):
        return kernel(body, [f32(*shape)], tuple(args), [whole(arg.shape) for arg in args], 1 << 16)[0]

    chains = [first()]
    tables = kernel(
        make_tables,
        [jax.ShapeDtypeStruct(shape, jnp.bfloat16) for shape in (col_shape,) * 2 + (row_shape,) * 2],
        (small,),
        [whole(small.shape)],
        1 << 20,
    )
    col, row = tuple(tables[:2]), tuple(tables[2:])
    chains += [start(p) for p in range(1, pols)]
    turned = kernel(turn_body, [f32(2, layers, length, rows)], (green,), [whole(green.shape)], 1 << 20)[0]
    chains = [couple(chain) for chain in chains]
    for step in range(ITERS - 1):
        moved = [None] * pols
        for p in range(pols):
            moved[p] = back(chains[p])
            if p > 0:
                chains[p - 1] = couple(moved[p - 1])
            moved[p] = again(p, moved[p])
        chains[last] = couple(moved[last], CHUNKS if step == ITERS - 2 else 1)
    cells = None
    for p in range(last - 1):
        cells = end(p, fields(p, back(chains[p])), cells)
    begun = fields(last - 1, back(chains[last - 1]))
    ahead = [back(chains[last][0], True)]
    cells = end(last - 1, begun, cells)
    ahead.append(back(chains[last][1], True))
    final = chunk_fields(last, ahead)
    gone = deal(final, cells, False)
    came = across(gone, 1)
    kept = deal(final, cells, True)
    found = simple(class_body, (CLASSES, 128), [gone, kept, kinds])
    found = send([found] * lat, "lat", lat)
    kept = simple(keep_body, (kept.shape[0] + CLASSES, 128), [kept, came, *found])
    d = 2
    while d < freqs:
        kept = simple(add_body, kept.shape, [kept, across(kept, d)])
        d *= 2
    both = (kept, across(kept, 1))
    outs = [f32(rows, length), f32(1, CLASSES)]
    cell, classes = kernel(place_body, outs, both, [whole(part.shape) for part in both], 1 << 16)
    return cell.reshape(1, rows, length), classes


def solution(mesh):
    whole_lanes = (
        NXY % (mesh.shape["lat"] * 128) == 0
        and NXY % (mesh.shape["lat"] * 128) == 0
        and mesh.shape["freq"] > 1
        and all(mesh.shape[name] & (mesh.shape[name] - 1) == 0 for name in mesh.axis_names)
    )
    per_device = functools.partial(fast_device, dict(mesh.shape)) if whole_lanes else plain_device

    placed = (
        P(None, "freq", None, "layer", "lat", None),
        P(None, "freq", "layer", "lat", None),
        P(None, "freq", None, "layer", "lat", None),
        P(None, "freq", None, "layer", "lat", None),
        P("layer", "lat", None),
    )
    return jax.shard_map(
        per_device,
        mesh=mesh,
        in_specs=placed,
        out_specs=(P("layer", "lat", None), P("layer", None)),
        check_vma=False,
    )
```

```python
import functools
import math

import jax
import jax.numpy as jnp
import ml_dtypes
import numpy as np
from jax import lax
from jax.experimental import pallas as pl
from jax.experimental.pallas import tpu as pltpu
from jax.sharding import PartitionSpec as P

NXY = 512
ITERS = 2
CLASSES = 8


highest = lax.Precision.HIGHEST


def tables(length):
    index = jnp.arange(length, dtype=jnp.int32)
    phase = index[:, None] * index[None, :] % length
    angle = phase.astype(jnp.float32) * (2.0 * math.pi / length)
    factor = 1.0 / math.sqrt(length)
    return (jnp.cos(angle) * factor, jnp.sin(angle) * factor)


def forward(field, cosine, sine):
    first = jnp.einsum("zfplxy,yk->zfplkx", field, cosine, precision=highest)
    second = jnp.einsum("zfplxy,yk->zfplkx", field, sine, precision=highest)
    partial_spec = jnp.stack([first[0] + second[1], first[1] - second[0]])
    turned = lax.all_to_all(partial_spec, "lat", split_axis=4, concat_axis=5, tiled=True)
    first = jnp.einsum("zfplkx,xq->zfplkq", turned, cosine, precision=highest)
    second = jnp.einsum("zfplkx,xq->zfplkq", turned, sine, precision=highest)
    return jnp.stack([first[0] + second[1], first[1] - second[0]])


def inverse(mixed, cosine, sine):
    first = jnp.einsum("lzfpkq,qx->zfplkx", mixed, cosine, precision=highest)
    second = jnp.einsum("lzfpkq,qx->zfplkx", mixed, sine, precision=highest)
    half_back = jnp.stack([first[0] - second[1], first[1] + second[0]])
    turned = lax.all_to_all(half_back, "lat", split_axis=5, concat_axis=4, tiled=True)
    first = jnp.einsum("zfplkx,ky->zfplxy", turned, cosine, precision=highest)
    second = jnp.einsum("zfplkx,ky->zfplxy", turned, sine, precision=highest)
    return jnp.stack([first[0] - second[1], first[1] + second[0]])


def couple_product(left, right):
    return jnp.einsum("foiyx,fpiyx->ofpyx", left, right, precision=highest)


def couple(kernel, spectra):
    real_part = couple_product(kernel[0], spectra[0]) - couple_product(kernel[1], spectra[1])
    imag_part = couple_product(kernel[0], spectra[1]) + couple_product(kernel[1], spectra[0])
    return jnp.stack([real_part, imag_part], axis=1)


def cmul(factor, field):
    return jnp.stack(
        [factor[0] * field[0] - factor[1] * field[1], factor[0] * field[1] + factor[1] * field[0]]
    )


def plain_device(source, contrast, green, efield, cell_class):
    cosine, sine = tables(source.shape[5])
    factor = contrast[:, :, None]
    field = source
    for step in range(ITERS):
        spectra = forward(cmul(factor, field), cosine, sine)
        mixed = lax.psum_scatter(couple(green, spectra), "layer", scatter_dimension=0, tiled=True)
        field = source + cmul(factor, inverse(mixed, cosine, sine))
    cell_terms = jnp.sum(efield[0] * field[0] - efield[1] * field[1], axis=(0, 1))
    cell = lax.psum(cell_terms, "freq")
    onehot = (cell_class[None] == jnp.arange(CLASSES, dtype=jnp.int32)[:, None, None, None]).astype(
        jnp.float32
    )
    local_sums = jnp.einsum("clxy,lxy->lc", onehot, cell_terms, precision=highest) / float(NXY)
    classes = lax.psum(local_sums, ("freq", "lat"))
    return (cell, classes)


VMEM_BYTES = 40 * 1024 * 1024
FIRST_VMEM_BYTES = 62 * 1024 * 1024
FINE = 16
CHUNKS = 2


def small_tables(length):
    index = np.arange(length)

    def waves(first):
        angle = (first[:, None] * index[None, :] % length) * (2.0 * np.pi / length)
        return np.stack([np.cos(angle), np.sin(angle)])

    both = [waves(index[::FINE]) / math.sqrt(length), waves(index[:FINE])]
    return np.concatenate(both, axis=1).astype(np.float32)


def halves(value):
    high = value.astype(jnp.bfloat16)
    return high, (value - high.astype(jnp.float32)).astype(jnp.bfloat16)


def product(left_high, left_low, right_high, right_low):
    def dot(left, right):
        return jnp.dot(left, right, preferred_element_type=jnp.float32)

    return dot(left_high, right_high) + (dot(left_high, right_low) + dot(left_low, right_high))


def along_y(real, imag, high_ref, low_ref, where, sign):
    rows = real.shape[0]
    high, low = halves(jnp.concatenate([real, imag], axis=0))
    got = product(high, low, high_ref[where], low_ref[where])
    width = got.shape[1] // 2
    out_real = got[:rows, :width] - sign * got[rows:, width:]
    out_imag = got[rows:, :width] + sign * got[:rows, width:]
    return out_real, out_imag


def along_x(high_ref, low_ref, where, high, low, sign):
    got = product(high_ref[where], low_ref[where], high, low)
    rows, width = got.shape[0] // 2, got.shape[1] // 2
    out_real = got[:rows, :width] - sign * got[rows:, width:]
    out_imag = got[:rows, width:] + sign * got[rows:, :width]
    return out_real, out_imag


def call(body, outs, args, specs, flops, scratch=(), after=(), vmem=VMEM_BYTES):
    sizes = sum(math.prod(o.shape) * 4 for o in outs)
    taken, tied = len(args), len(after)

    def ordered(*refs):
        body(*refs[:taken], *refs[taken + tied :])

    return pl.pallas_call(
        ordered,
        grid=(1,),
        out_shape=outs,
        in_specs=list(specs) + [pl.BlockSpec(memory_space=pl.ANY)] * tied,
        out_specs=[whole(o.shape) for o in outs],
        scratch_shapes=list(scratch),
        compiler_params=pltpu.CompilerParams(vmem_limit_bytes=vmem),
        cost_estimate=pl.CostEstimate(flops=flops, bytes_accessed=2 * sizes, transcendentals=0),
    )(*args, *after)


def whole(shape):
    return pl.BlockSpec(tuple(shape), lambda step: (0,) * len(shape))


def pick(shape, pol):
    return pl.BlockSpec((shape[0], 1) + tuple(shape[2:]), lambda step: (0, pol, 0, 0))


def f32(*shape):
    return jax.ShapeDtypeStruct(shape, jnp.float32)


def turns(size):
    return sorted(range(size), key=lambda d: (d == 1, d))


def send(blocks, axis, size):
    got = [blocks[0]]
    for d, block in zip(turns(size)[1:], blocks[1:]):
        got.append(lax.ppermute(block, axis, [(i, i ^ d) for i in range(size)]))
    return got


def make_tables(small, col_high, col_low, row_high=None, row_low=None):
    blocks, length, width = col_high.shape
    width = width // 2
    steps = length // FINE
    f_real, f_imag = small[0, steps:], small[1, steps:]
    for a in range(steps):
        c_real, c_imag = small[0, a : a + 1], small[1, a : a + 1]
        pair = (c_real * f_real - c_imag * f_imag, c_real * f_imag + c_imag * f_real)
        block, first = a * FINE // width, a * FINE % width
        for z, part in enumerate(pair):
            for value, row, col in zip(halves(part), (row_high, row_low), (col_high, col_low)):
                if row is not None:
                    row[block, z * width + first : z * width + first + FINE] = value
                for k in range(blocks):
                    spot = slice(a * FINE, (a + 1) * FINE)
                    col[k, spot, z * width : (z + 1) * width] = value[:, k * width : (k + 1) * width]


def forward_blocks(real, imag, high_ref, low_ref, out_refs, bits):
    me = lax.axis_index("lat")
    for d, out in zip(bits, out_refs):
        out[0], out[1] = along_y(real, imag, high_ref, low_ref, me ^ d, -1)


def weighted(contrast, real, imag):
    m_real, m_imag = contrast[0], contrast[1]
    return m_real * real - m_imag * imag, m_real * imag + m_imag * real


def first_body(lat, source, contrast, small, *refs):
    outs, (field, factor, waves, high, low, sems) = refs[:lat], refs[lat:]
    copies = [
        pltpu.make_async_copy(small, waves, sems.at[0]),
        pltpu.make_async_copy(source.at[:, 0], field, sems.at[1]),
        pltpu.make_async_copy(contrast, factor, sems.at[2]),
    ]
    for copy in copies:
        copy.start()
    copies[0].wait()
    make_tables(waves, high, low)
    copies[1].wait()
    copies[2].wait()
    real, imag = weighted(factor, field[0], field[1])
    forward_blocks(real, imag, high, low, outs, turns(lat))


def start_body(lat, source, contrast, high_ref, low_ref, *outs):
    real, imag = weighted(contrast, source[0, 0], source[1, 0])
    forward_blocks(real, imag, high_ref, low_ref, outs, turns(lat))


def turn_body(green, out):
    for z in range(green.shape[0]):
        for o in range(green.shape[1]):
            out[z, o] = green[z, o].T


def blocks_of(bits, width):
    me = lax.axis_index("lat")
    return [pl.ds(pl.multiple_of((me ^ d) * width, width), width) for d in bits]


def spectrum_part(parts, bits, high_ref, low_ref, k):
    columns = blocks_of(bits, parts[0].shape[1])
    high, low = halves(jnp.concatenate([jnp.concatenate([part[0], part[1]], axis=1) for part in parts], axis=0))
    table_high, table_low = [jnp.concatenate([ref[k, :, at] for at in columns], axis=1) for ref in (high_ref, low_ref)]
    got = product(table_high, table_low, high, low)
    rows, width = got.shape[0] // 2, got.shape[1] // 2
    return got[:rows, :width] + got[rows:, width:], got[:rows, width:] - got[rows:, :width]


def spectrum_body(bits, *refs):
    parts, (high_ref, low_ref, out) = refs[: len(bits)], refs[len(bits) :]
    rows = high_ref.shape[1] // 2
    for k in range(high_ref.shape[0]):
        at = slice(k * rows, (k + 1) * rows)
        out[0, at], out[1, at] = spectrum_part(parts, bits, high_ref, low_ref, k)


def couple_body(bits, *refs):
    parts, (begun, green, high_ref, low_ref), outs = refs[: len(bits)], refs[len(bits) : len(bits) + 4], refs[len(bits) + 4 :]
    layer = lax.axis_index("layer")
    rows = high_ref.shape[1] // 2
    for k in range(high_ref.shape[0]):
        at = slice(k * rows, (k + 1) * rows)
        real, imag = spectrum_part(parts, bits, high_ref, low_ref, k)
        real, imag = begun[0, at] + real, begun[1, at] + imag
        chunks = len(outs) // green.shape[1]
        for e in range(green.shape[1]):
            g_real, g_imag = green[0, layer ^ e, at], green[1, layer ^ e, at]
            pair = (g_real * real - g_imag * imag, g_real * imag + g_imag * real)
            if chunks == 1:
                outs[e][0, at], outs[e][1, at] = pair
            else:
                half = real.shape[1] // chunks
                for c in range(chunks):
                    spot = slice(c * half, (c + 1) * half)
                    outs[e * chunks + c][at] = jnp.concatenate([part[:, spot] for part in pair], axis=1)


def back_body(bits, layers, *refs):
    parts, (high_ref, low_ref), outs = refs[:layers], refs[layers : layers + 2], refs[layers + 2 :]
    me = lax.axis_index("lat")
    mixed = [sum((part[z] for part in parts[1:]), parts[0][z]) for z in range(2)]
    high, low = halves(jnp.concatenate(mixed, axis=1))
    for d, out in zip(bits, outs):
        out[0], out[1] = along_x(high_ref, low_ref, me ^ d, high, low, +1)


def back_chunk_body(bits, layers, *refs):
    parts, (high_ref, low_ref), outs = refs[:layers], refs[layers : layers + 2], refs[layers + 2 :]
    me = lax.axis_index("lat")
    high, low = halves(sum((part[...] for part in parts[1:]), parts[0][...]))
    for d, out in zip(bits, outs):
        got = product(high_ref[me ^ d], low_ref[me ^ d], high, low)
        rows, width = got.shape[0] // 2, got.shape[1]
        lane = lax.broadcasted_iota(jnp.int32, (rows, width), 1)
        turned = pltpu.roll(got[rows:], width // 2, 1)
        out[...] = got[:rows] + jnp.where(lane < width // 2, -turned, turned)


def field_part(parts, bits, high_ref, low_ref, k, rows, chunk=None):
    if chunk is None:
        spots = blocks_of(bits, parts[0].shape[2])
        both = [jnp.concatenate([part[z, rows] for part in parts], axis=1) for z in range(2)]
    else:
        me = lax.axis_index("lat")
        half = parts[0].shape[1] // 2
        spots = [pl.ds(pl.multiple_of(((me ^ d) * CHUNKS + chunk) * half, half), half) for d in bits]
        lanes = [slice(z * half, (z + 1) * half) for z in range(2)]
        both = [jnp.concatenate([part[rows, at] for part in parts], axis=1) for at in lanes]
    high, low = halves(jnp.concatenate(both, axis=0))
    table_high, table_low = [jnp.concatenate([ref[k, at] for at in spots], axis=0) for ref in (high_ref, low_ref)]
    got = product(high, low, table_high, table_low)
    count, width = got.shape[0] // 2, got.shape[1] // 2
    return got[:count, :width] - got[count:, width:], got[:count, width:] + got[count:, :width]


def field_body(bits, chunk, *refs):
    parts, (high_ref, low_ref, out) = refs[: len(bits)], refs[len(bits) :]
    width = high_ref.shape[2] // 2
    for k in range(high_ref.shape[0]):
        at = slice(k * width, (k + 1) * width)
        out[0, :, at], out[1, :, at] = field_part(parts, bits, high_ref, low_ref, k, slice(None), chunk)


def update(parts, bits, begun, source, contrast, high_ref, low_ref, field, rows=slice(None), chunk=None):
    width = high_ref.shape[2] // 2
    for k in range(high_ref.shape[0]):
        at = slice(k * width, (k + 1) * width)
        real, imag = field_part(parts, bits, high_ref, low_ref, k, rows, chunk)
        real, imag = begun[0, rows, at] + real, begun[1, rows, at] + imag
        m_real, m_imag = contrast[0, rows, at], contrast[1, rows, at]
        field[0, :, at] = source[0, 0, rows, at] + (m_real * real - m_imag * imag)
        field[1, :, at] = source[1, 0, rows, at] + (m_real * imag + m_imag * real)


def again_body(lat, bits, *refs):
    parts, (begun, source, contrast, high_ref, low_ref), rest = refs[: len(bits)], refs[len(bits) : len(bits) + 5], refs[len(bits) + 5 :]
    out, ahead, field = rest
    update(parts, bits, begun, source, contrast, high_ref, low_ref, field)
    ahead[0], ahead[1] = weighted(contrast, field[0], field[1])
    forward_blocks(ahead[0], ahead[1], high_ref, low_ref, [out], turns(lat)[1:2])


def rest_body(bits, ahead, high_ref, low_ref, *outs):
    forward_blocks(ahead[0], ahead[1], high_ref, low_ref, outs, bits)


def end_body(bits, *refs):
    parts, rest = refs[: len(bits)], refs[len(bits) :]
    (begun, source, contrast, efield, high_ref, low_ref), rest = rest[:6], rest[6:]
    before, out, field = (rest[0] if len(rest) == 3 else None), rest[-2], rest[-1]
    update(parts, bits, begun, source, contrast, high_ref, low_ref, field)
    terms = efield[0, 0] * field[0] - efield[1, 0] * field[1]
    out[...] = terms if before is None else before[...] + terms


def half_rows(which, rows):
    return pl.ds(pl.multiple_of(which * rows, rows), rows)


def deal_body(bits, kept, *refs):
    parts, rest = refs[: len(bits)], refs[len(bits) :]
    begun, source, contrast, efield, high_ref, low_ref, before, out, field = rest
    bit = lax.axis_index("freq") & 1
    count = field.shape[1]
    at = half_rows(bit if kept else 1 - bit, count)
    update(parts, bits, begun, source, contrast, high_ref, low_ref, field, at, CHUNKS - 1)
    cell = before[at] + (efield[0, 0, at] * field[0] - efield[1, 0, at] * field[1])
    width = out.shape[1]
    for k in range(cell.shape[1] // width):
        out[k * count : (k + 1) * count] = cell[:, k * width : (k + 1) * width]


def class_body(gone, kept, kinds, table):
    bit = lax.axis_index("freq") & 1
    count, width = kinds.shape[0] // 2, gone.shape[1]
    spots = [slice(k * width, (k + 1) * width) for k in range(kinds.shape[1] // width)]
    sides = []
    for cell, which in ((gone, 1 - bit), (kept, bit)):
        sides.append((cell[...], jnp.concatenate([kinds[half_rows(which, count), at] for at in spots], axis=0)))
    lines = []
    for c in range(CLASSES):
        chosen = sum(jnp.where(kind == c, cell, 0.0) for cell, kind in sides)
        lines.append(jnp.full((1, width), jnp.sum(chosen), jnp.float32))
    table[...] = jnp.concatenate(lines, axis=0)


def sum_body(*refs):
    refs[-1][...] = sum((ref[...] for ref in refs[1:-1]), refs[0][...])


def join_body(one, two, table, other, out):
    rows = one.shape[0]
    out[:rows] = one[...] + two[...]
    out[rows:] = table[...] + other[...]


def place_body(own, other, cell, classes):
    bit = lax.axis_index("freq") & 1
    width = own.shape[1]
    count = cell.shape[1] // width
    rows = cell.shape[0] // 2
    for which, ref in ((bit, own), (1 - bit, other)):
        at = pl.ds(pl.multiple_of(which * rows, rows), rows)
        for k in range(count):
            cell[at, k * width : (k + 1) * width] = ref[k * rows : (k + 1) * rows]
    total = own[count * rows :] + other[count * rows :]
    row = lax.broadcasted_iota(jnp.int32, total.shape, 0)
    lane = lax.broadcasted_iota(jnp.int32, total.shape, 1)
    line = jnp.sum(jnp.where(row == lane, total, 0.0), axis=0, keepdims=True)
    classes[...] = line[:, :CLASSES] / float(NXY)


def fast_device(sizes, source, contrast, green, efield, cell_class):
    freqs, layers, lat = sizes["freq"], sizes["layer"], sizes["lat"]
    pols, rows, length = source.shape[2], source.shape[4], source.shape[5]
    source = source.reshape(2, pols, rows, length)
    efield = efield.reshape(2, pols, rows, length)
    contrast = contrast.reshape(2, rows, length)
    green = green.reshape(2, layers, rows, length)
    kinds = cell_class.reshape(rows, length)
    col_shape, row_shape = (lat, length, 2 * rows), (lat, 2 * rows, length)
    table_specs, row_specs = [whole(col_shape)] * 2, [whole(row_shape)] * 2
    block = f32(2, rows, rows)
    spectrum = f32(2, length, rows)
    full = pltpu.VMEM((2, rows, length), jnp.float32)
    stage_flops = 24 * rows * length * length
    last = pols - 1
    order = []
    bits, near = turns(lat), lat // 2

    def kernel(body, outs, args, specs, flops=stage_flops, scratch=(), vmem=VMEM_BYTES):
        got = call(body, outs, args, specs, flops, scratch, tuple(order[-1:]), vmem)
        order.append(got[0])
        return got

    small = jnp.asarray(small_tables(length))

    def first():
        specs = [pl.BlockSpec(memory_space=pltpu.HBM)] * 3
        scratch = [
            full,
            full,
            pltpu.VMEM(small.shape, jnp.float32),
            pltpu.VMEM(col_shape, jnp.bfloat16),
            pltpu.VMEM(col_shape, jnp.bfloat16),
            pltpu.SemaphoreType.DMA((3,)),
        ]
        body = functools.partial(first_body, lat)
        args = (source, contrast, small)
        return send(kernel(body, [block] * lat, args, specs, scratch=scratch, vmem=FIRST_VMEM_BYTES), "lat", lat)

    def start(p):
        specs = [pick(source.shape, p), whole(contrast.shape)] + table_specs
        return send(kernel(functools.partial(start_body, lat), [block] * lat, (source, contrast, *col), specs), "lat", lat)

    def couple(parts, chunks=1):
        specs = [whole(block.shape)] * near + row_specs
        begun = kernel(functools.partial(spectrum_body, bits[:near]), [spectrum], (*parts[:near], *row), specs)[0]
        specs = [whole(block.shape)] * (lat - near) + [whole(spectrum.shape), whole(turned.shape)] + row_specs
        body = functools.partial(couple_body, bits[near:])
        outs = [spectrum if chunks == 1 else f32(length, 2 * rows // chunks)] * (layers * chunks)
        got = kernel(body, outs, (*parts[near:], begun, turned, *row), specs)
        got = [send(got[c::chunks], "layer", layers) for c in range(chunks)]
        return got[0] if chunks == 1 else got

    early, later = bits[1:2], bits[:1] + bits[2:]

    def turn_block(value, d):
        return lax.ppermute(value, "lat", [(i, i ^ d) for i in range(lat)])

    def merged(ahead, got):
        return [got[0], ahead] + [turn_block(value, d) for value, d in zip(got[1:], later[1:])]

    def back(parts, chunk=False):
        specs = [whole(parts[0].shape)] * layers + row_specs

        def some(chosen):
            body = functools.partial(back_chunk_body if chunk else back_body, chosen, layers)
            outs = [f32(rows, parts[0].shape[1]) if chunk else block] * len(chosen)
            return kernel(body, outs, (*parts, *row), specs, stage_flops * len(chosen) // lat)

        ahead = turn_block(some(early)[0], early[0])
        return merged(ahead, some(later))

    def fields(p, parts):
        specs = [whole(block.shape)] * near + table_specs
        begun = kernel(functools.partial(field_body, bits[:near], None), [f32(2, rows, length)], (*parts[:near], *col), specs)[0]
        specs = [whole(block.shape)] * (lat - near) + [whole(begun.shape), pick(source.shape, p), whole(contrast.shape)]
        return (*parts[near:], begun, source, contrast), specs

    def again(p, parts):
        args, specs = fields(p, parts)
        outs = [block, f32(2, rows, length)]
        body = functools.partial(again_body, lat, bits[near:])
        got = kernel(body, outs, (*args, *col), specs + table_specs, stage_flops, [full])
        ahead = turn_block(got[0], early[0])
        body = functools.partial(rest_body, later)
        got = kernel(body, [block] * len(later), (got[1], *col), [whole((2, rows, length))] + table_specs)
        return merged(ahead, got)

    def end(p, operands, cells):
        more = () if cells is None else (cells,)
        args, specs = operands
        specs += [pick(efield.shape, p)] + table_specs + [whole((rows, length))] * len(more)
        args = (*args, efield, *col, *more)
        body = functools.partial(end_body, bits[near:])
        return kernel(body, [f32(rows, length)], args, specs, scratch=[full])[0]

    def chunk_fields(p, chunks):
        parts = chunks[0]
        packed = [whole(part.shape) for part in parts]
        body = functools.partial(field_body, bits, 0)
        begun = kernel(body, [f32(2, rows, length)], (*parts, *col), packed + table_specs)[0]
        specs = packed + [whole(begun.shape), pick(source.shape, p), whole(contrast.shape)]
        return (*chunks[1], begun, source, contrast), specs

    def deal(operands, cells, kept):
        args, specs = operands
        specs = specs + [pick(efield.shape, last)] + table_specs + [whole((rows, length))]
        args = (*args, efield, *col, cells)
        outs = [f32(rows // 2 * (length // 128), 128)]
        scratch = [pltpu.VMEM((2, rows // 2, length), jnp.float32)]
        body = functools.partial(deal_body, bits, kept)
        return kernel(body, outs, args, specs, stage_flops // 2, scratch)[0]

    def across(value, d):
        return lax.ppermute(value, "freq", [(i, i ^ d) for i in range(freqs)])

    def simple(body, shape, args):
        return kernel(body, [f32(*shape)], tuple(args), [whole(arg.shape) for arg in args], 1 << 16)[0]

    chains = [first()]
    tables = kernel(
        make_tables,
        [jax.ShapeDtypeStruct(shape, jnp.bfloat16) for shape in (col_shape,) * 2 + (row_shape,) * 2],
        (small,),
        [whole(small.shape)],
        1 << 20,
    )
    col, row = tuple(tables[:2]), tuple(tables[2:])
    chains += [start(p) for p in range(1, pols)]
    turned = kernel(turn_body, [f32(2, layers, length, rows)], (green,), [whole(green.shape)], 1 << 20)[0]
    chains = [couple(chain) for chain in chains]
    for step in range(ITERS - 1):
        moved = [None] * pols
        for p in range(pols):
            moved[p] = back(chains[p])
            if p > 0:
                chains[p - 1] = couple(moved[p - 1])
            moved[p] = again(p, moved[p])
        chains[last] = couple(moved[last], CHUNKS if step == ITERS - 2 else 1)
    cells = None
    for p in range(last - 1):
        cells = end(p, fields(p, back(chains[p])), cells)
    begun = fields(last - 1, back(chains[last - 1]))
    ahead = [back(chains[last][0], True)]
    cells = end(last - 1, begun, cells)
    ahead.append(back(chains[last][1], True))
    final = chunk_fields(last, ahead)
    gone = deal(final, cells, False)
    came = across(gone, 1)
    kept = deal(final, cells, True)
    found = simple(class_body, (CLASSES, 128), [gone, kept, kinds])
    found = send([found] * lat, "lat", lat)
    kept = simple(sum_body, kept.shape, [kept, came])
    came = across(kept, 2)
    found = simple(sum_body, (CLASSES, 128), found)
    other = across(found, 2)
    d = 4
    while d < freqs:
        kept, found = simple(sum_body, kept.shape, [kept, came]), simple(sum_body, found.shape, [found, other])
        came, other = across(kept, d), across(found, d)
        d *= 2
    kept = simple(join_body, (kept.shape[0] + CLASSES, 128), [kept, came, found, other])
    both = (kept, across(kept, 1))
    outs = [f32(rows, length), f32(1, CLASSES)]
    cell, classes = kernel(place_body, outs, both, [whole(part.shape) for part in both], 1 << 16)
    return cell.reshape(1, rows, length), classes


def solution(mesh):
    whole_lanes = (
        NXY % (mesh.shape["lat"] * 128) == 0
        and NXY % (mesh.shape["lat"] * 128) == 0
        and mesh.shape["freq"] > 2
        and all(mesh.shape[name] & (mesh.shape[name] - 1) == 0 for name in mesh.axis_names)
    )
    per_device = functools.partial(fast_device, dict(mesh.shape)) if whole_lanes else plain_device

    placed = (
        P(None, "freq", None, "layer", "lat", None),
        P(None, "freq", "layer", "lat", None),
        P(None, "freq", None, "layer", "lat", None),
        P(None, "freq", None, "layer", "lat", None),
        P("layer", "lat", None),
    )
    return jax.shard_map(
        per_device,
        mesh=mesh,
        in_specs=placed,
        out_specs=(P("layer", "lat", None), P("layer", None)),
        check_vma=False,
    )
```

```python
import functools
import math

import jax
import jax.numpy as jnp
import ml_dtypes
import numpy as np
from jax import lax
from jax.experimental import pallas as pl
from jax.experimental.pallas import tpu as pltpu
from jax.sharding import PartitionSpec as P

NXY = 512
ITERS = 2
CLASSES = 8


highest = lax.Precision.HIGHEST


def tables(length):
    index = jnp.arange(length, dtype=jnp.int32)
    phase = index[:, None] * index[None, :] % length
    angle = phase.astype(jnp.float32) * (2.0 * math.pi / length)
    factor = 1.0 / math.sqrt(length)
    return (jnp.cos(angle) * factor, jnp.sin(angle) * factor)


def forward(field, cosine, sine):
    first = jnp.einsum("zfplxy,yk->zfplkx", field, cosine, precision=highest)
    second = jnp.einsum("zfplxy,yk->zfplkx", field, sine, precision=highest)
    partial_spec = jnp.stack([first[0] + second[1], first[1] - second[0]])
    turned = lax.all_to_all(partial_spec, "lat", split_axis=4, concat_axis=5, tiled=True)
    first = jnp.einsum("zfplkx,xq->zfplkq", turned, cosine, precision=highest)
    second = jnp.einsum("zfplkx,xq->zfplkq", turned, sine, precision=highest)
    return jnp.stack([first[0] + second[1], first[1] - second[0]])


def inverse(mixed, cosine, sine):
    first = jnp.einsum("lzfpkq,qx->zfplkx", mixed, cosine, precision=highest)
    second = jnp.einsum("lzfpkq,qx->zfplkx", mixed, sine, precision=highest)
    half_back = jnp.stack([first[0] - second[1], first[1] + second[0]])
    turned = lax.all_to_all(half_back, "lat", split_axis=5, concat_axis=4, tiled=True)
    first = jnp.einsum("zfplkx,ky->zfplxy", turned, cosine, precision=highest)
    second = jnp.einsum("zfplkx,ky->zfplxy", turned, sine, precision=highest)
    return jnp.stack([first[0] - second[1], first[1] + second[0]])


def couple_product(left, right):
    return jnp.einsum("foiyx,fpiyx->ofpyx", left, right, precision=highest)


def couple(kernel, spectra):
    real_part = couple_product(kernel[0], spectra[0]) - couple_product(kernel[1], spectra[1])
    imag_part = couple_product(kernel[0], spectra[1]) + couple_product(kernel[1], spectra[0])
    return jnp.stack([real_part, imag_part], axis=1)


def cmul(factor, field):
    return jnp.stack(
        [factor[0] * field[0] - factor[1] * field[1], factor[0] * field[1] + factor[1] * field[0]]
    )


def plain_device(source, contrast, green, efield, cell_class):
    cosine, sine = tables(source.shape[5])
    factor = contrast[:, :, None]
    field = source
    for step in range(ITERS):
        spectra = forward(cmul(factor, field), cosine, sine)
        mixed = lax.psum_scatter(couple(green, spectra), "layer", scatter_dimension=0, tiled=True)
        field = source + cmul(factor, inverse(mixed, cosine, sine))
    cell_terms = jnp.sum(efield[0] * field[0] - efield[1] * field[1], axis=(0, 1))
    cell = lax.psum(cell_terms, "freq")
    onehot = (cell_class[None] == jnp.arange(CLASSES, dtype=jnp.int32)[:, None, None, None]).astype(
        jnp.float32
    )
    local_sums = jnp.einsum("clxy,lxy->lc", onehot, cell_terms, precision=highest) / float(NXY)
    classes = lax.psum(local_sums, ("freq", "lat"))
    return (cell, classes)


VMEM_BYTES = 40 * 1024 * 1024
FIRST_VMEM_BYTES = 62 * 1024 * 1024
FINE = 16
CHUNKS = 2


def small_tables(length):
    index = np.arange(length)

    def waves(first):
        angle = (first[:, None] * index[None, :] % length) * (2.0 * np.pi / length)
        return np.stack([np.cos(angle), np.sin(angle)])

    both = [waves(index[::FINE]) / math.sqrt(length), waves(index[:FINE])]
    return np.concatenate(both, axis=1).astype(np.float32)


def halves(value):
    high = value.astype(jnp.bfloat16)
    return high, (value - high.astype(jnp.float32)).astype(jnp.bfloat16)


def product(left_high, left_low, right_high, right_low):
    def dot(left, right):
        return jnp.dot(left, right, preferred_element_type=jnp.float32)

    return dot(left_high, right_high) + (dot(left_high, right_low) + dot(left_low, right_high))


def along_y(real, imag, high_ref, low_ref, where, sign):
    rows = real.shape[0]
    high, low = halves(jnp.concatenate([real, imag], axis=0))
    got = product(high, low, high_ref[where], low_ref[where])
    width = got.shape[1] // 2
    out_real = got[:rows, :width] - sign * got[rows:, width:]
    out_imag = got[rows:, :width] + sign * got[:rows, width:]
    return out_real, out_imag


def along_x(high_ref, low_ref, where, high, low, sign):
    got = product(high_ref[where], low_ref[where], high, low)
    rows, width = got.shape[0] // 2, got.shape[1] // 2
    out_real = got[:rows, :width] - sign * got[rows:, width:]
    out_imag = got[:rows, width:] + sign * got[rows:, :width]
    return out_real, out_imag


def call(body, outs, args, specs, flops, scratch=(), after=(), vmem=VMEM_BYTES):
    sizes = sum(math.prod(o.shape) * 4 for o in outs)
    taken, tied = len(args), len(after)

    def ordered(*refs):
        body(*refs[:taken], *refs[taken + tied :])

    return pl.pallas_call(
        ordered,
        grid=(1,),
        out_shape=outs,
        in_specs=list(specs) + [pl.BlockSpec(memory_space=pl.ANY)] * tied,
        out_specs=[whole(o.shape) for o in outs],
        scratch_shapes=list(scratch),
        compiler_params=pltpu.CompilerParams(vmem_limit_bytes=vmem),
        cost_estimate=pl.CostEstimate(flops=flops, bytes_accessed=2 * sizes, transcendentals=0),
    )(*args, *after)


def whole(shape):
    return pl.BlockSpec(tuple(shape), lambda step: (0,) * len(shape))


def pick(shape, pol):
    return pl.BlockSpec((shape[0], 1) + tuple(shape[2:]), lambda step: (0, pol, 0, 0))


def f32(*shape):
    return jax.ShapeDtypeStruct(shape, jnp.float32)


def turns(size):
    return sorted(range(size), key=lambda d: (d == 1, d))


def send(blocks, axis, size):
    got = [blocks[0]]
    for d, block in zip(turns(size)[1:], blocks[1:]):
        got.append(lax.ppermute(block, axis, [(i, i ^ d) for i in range(size)]))
    return got


def make_tables(small, col_high, col_low, row_high=None, row_low=None):
    blocks, length, width = col_high.shape
    width = width // 2
    steps = length // FINE
    f_real, f_imag = small[0, steps:], small[1, steps:]
    for a in range(steps):
        c_real, c_imag = small[0, a : a + 1], small[1, a : a + 1]
        pair = (c_real * f_real - c_imag * f_imag, c_real * f_imag + c_imag * f_real)
        block, first = a * FINE // width, a * FINE % width
        for z, part in enumerate(pair):
            for value, row, col in zip(halves(part), (row_high, row_low), (col_high, col_low)):
                if row is not None:
                    row[block, z * width + first : z * width + first + FINE] = value
                for k in range(blocks):
                    spot = slice(a * FINE, (a + 1) * FINE)
                    col[k, spot, z * width : (z + 1) * width] = value[:, k * width : (k + 1) * width]


def forward_blocks(real, imag, high_ref, low_ref, out_refs, bits):
    me = lax.axis_index("lat")
    for d, out in zip(bits, out_refs):
        out[0], out[1] = along_y(real, imag, high_ref, low_ref, me ^ d, -1)


def weighted(contrast, real, imag):
    m_real, m_imag = contrast[0], contrast[1]
    return m_real * real - m_imag * imag, m_real * imag + m_imag * real


def first_body(lat, source, contrast, small, *refs):
    outs, (field, factor, waves, high, low, sems) = refs[: lat * CHUNKS], refs[lat * CHUNKS :]
    copies = [
        pltpu.make_async_copy(small, waves, sems.at[0]),
        pltpu.make_async_copy(source.at[:, 0], field, sems.at[1]),
        pltpu.make_async_copy(contrast, factor, sems.at[2]),
    ]
    for copy in copies:
        copy.start()
    copies[0].wait()
    make_tables(waves, high, low)
    copies[1].wait()
    copies[2].wait()
    real, imag = weighted(factor, field[0], field[1])
    me = lax.axis_index("lat")
    for i, d in enumerate(turns(lat)):
        got = along_y(real, imag, high, low, me ^ d, -1)
        half = got[0].shape[1] // CHUNKS
        for c in range(CHUNKS):
            outs[c * lat + i][...] = jnp.concatenate([part[:, c * half : (c + 1) * half] for part in got], axis=1)


def start_body(lat, source, contrast, high_ref, low_ref, *outs):
    real, imag = weighted(contrast, source[0, 0], source[1, 0])
    forward_blocks(real, imag, high_ref, low_ref, outs, turns(lat))


def turn_body(green, out):
    for z in range(green.shape[0]):
        for o in range(green.shape[1]):
            out[z, o] = green[z, o].T


def blocks_of(bits, width):
    me = lax.axis_index("lat")
    return [pl.ds(pl.multiple_of((me ^ d) * width, width), width) for d in bits]


def spectrum_part(parts, bits, high_ref, low_ref, k):
    columns = blocks_of(bits, parts[0].shape[1])
    high, low = halves(jnp.concatenate([jnp.concatenate([part[0], part[1]], axis=1) for part in parts], axis=0))
    table_high, table_low = [jnp.concatenate([ref[k, :, at] for at in columns], axis=1) for ref in (high_ref, low_ref)]
    got = product(table_high, table_low, high, low)
    rows, width = got.shape[0] // 2, got.shape[1] // 2
    return got[:rows, :width] + got[rows:, width:], got[:rows, width:] - got[rows:, :width]


def spectrum_body(bits, *refs):
    parts, (high_ref, low_ref, out) = refs[: len(bits)], refs[len(bits) :]
    rows = high_ref.shape[1] // 2
    for k in range(high_ref.shape[0]):
        at = slice(k * rows, (k + 1) * rows)
        out[0, at], out[1, at] = spectrum_part(parts, bits, high_ref, low_ref, k)


def couple_body(bits, *refs):
    parts, (begun, green, high_ref, low_ref), outs = refs[: len(bits)], refs[len(bits) : len(bits) + 4], refs[len(bits) + 4 :]
    layer = lax.axis_index("layer")
    rows = high_ref.shape[1] // 2
    for k in range(high_ref.shape[0]):
        at = slice(k * rows, (k + 1) * rows)
        real, imag = spectrum_part(parts, bits, high_ref, low_ref, k)
        real, imag = begun[0, at] + real, begun[1, at] + imag
        chunks = len(outs) // green.shape[1]
        for e in range(green.shape[1]):
            g_real, g_imag = green[0, layer ^ e, at], green[1, layer ^ e, at]
            pair = (g_real * real - g_imag * imag, g_real * imag + g_imag * real)
            if chunks == 1:
                outs[e][0, at], outs[e][1, at] = pair
            else:
                half = real.shape[1] // chunks
                for c in range(chunks):
                    spot = slice(c * half, (c + 1) * half)
                    outs[e * chunks + c][at] = jnp.concatenate([part[:, spot] for part in pair], axis=1)


def swap(packed):
    return pltpu.roll(packed, packed.shape[1] // 2, 1)


def spectrum_chunk(parts, bits, high_ref, low_ref, k):
    columns = blocks_of(bits, parts[0].shape[0])
    high, low = halves(jnp.concatenate([part[...] for part in parts], axis=0))
    table_high, table_low = [jnp.concatenate([ref[k, :, at] for at in columns], axis=1) for ref in (high_ref, low_ref)]
    got = product(table_high, table_low, high, low)
    rows, width = got.shape[0] // 2, got.shape[1]
    lane = lax.broadcasted_iota(jnp.int32, (rows, width), 1)
    turned = swap(got[rows:])
    return got[:rows] + jnp.where(lane < width // 2, turned, -turned)


def spectrum_chunk_body(bits, *refs):
    parts, (high_ref, low_ref, out) = refs[: len(bits)], refs[len(bits) :]
    rows = high_ref.shape[1] // 2
    for k in range(high_ref.shape[0]):
        out[k * rows : (k + 1) * rows] = spectrum_chunk(parts, bits, high_ref, low_ref, k)


def couple_chunk_body(bits, chunk, *refs):
    parts, (begun, green, high_ref, low_ref), outs = refs[: len(bits)], refs[len(bits) : len(bits) + 4], refs[len(bits) + 4 :]
    layer = lax.axis_index("layer")
    rows, half = high_ref.shape[1] // 2, begun.shape[1] // 2
    for k in range(high_ref.shape[0]):
        at = slice(k * rows, (k + 1) * rows)
        spectra = begun[at] + spectrum_chunk(parts, bits, high_ref, low_ref, k)
        swapped = swap(spectra)
        for e, out in enumerate(outs):
            g_real, g_imag = [green[z, layer ^ e, at][:, chunk * half : (chunk + 1) * half] for z in range(2)]
            both = jnp.concatenate([g_real, g_real], axis=1)
            cross = jnp.concatenate([-g_imag, g_imag], axis=1)
            out[at] = both * spectra + cross * swapped


def back_pair_body(bits, layers, *refs):
    count = layers * CHUNKS
    parts, (high_ref, low_ref), outs = refs[:count], refs[count : count + 2], refs[count + 2 :]
    me = lax.axis_index("lat")
    mixed = []
    for c in range(CHUNKS):
        chunk = parts[c * layers : (c + 1) * layers]
        mixed.append(sum((part[...] for part in chunk[1:]), chunk[0][...]))
    half = mixed[0].shape[1] // 2
    pieces = [part[:, z * half : (z + 1) * half] for z in range(2) for part in mixed]
    high, low = halves(jnp.concatenate(pieces, axis=1))
    for d, out in zip(bits, outs):
        out[0], out[1] = along_x(high_ref, low_ref, me ^ d, high, low, +1)


def back_body(bits, layers, *refs):
    parts, (high_ref, low_ref), outs = refs[:layers], refs[layers : layers + 2], refs[layers + 2 :]
    me = lax.axis_index("lat")
    mixed = [sum((part[z] for part in parts[1:]), parts[0][z]) for z in range(2)]
    high, low = halves(jnp.concatenate(mixed, axis=1))
    for d, out in zip(bits, outs):
        out[0], out[1] = along_x(high_ref, low_ref, me ^ d, high, low, +1)


def back_chunk_body(bits, layers, *refs):
    parts, (high_ref, low_ref), outs = refs[:layers], refs[layers : layers + 2], refs[layers + 2 :]
    me = lax.axis_index("lat")
    high, low = halves(sum((part[...] for part in parts[1:]), parts[0][...]))
    for d, out in zip(bits, outs):
        got = product(high_ref[me ^ d], low_ref[me ^ d], high, low)
        rows, width = got.shape[0] // 2, got.shape[1]
        lane = lax.broadcasted_iota(jnp.int32, (rows, width), 1)
        turned = pltpu.roll(got[rows:], width // 2, 1)
        out[...] = got[:rows] + jnp.where(lane < width // 2, -turned, turned)


def field_part(parts, bits, high_ref, low_ref, k, rows, chunk=None):
    if chunk is None:
        spots = blocks_of(bits, parts[0].shape[2])
        both = [jnp.concatenate([part[z, rows] for part in parts], axis=1) for z in range(2)]
    else:
        me = lax.axis_index("lat")
        half = parts[0].shape[1] // 2
        spots = [pl.ds(pl.multiple_of(((me ^ d) * CHUNKS + chunk) * half, half), half) for d in bits]
        lanes = [slice(z * half, (z + 1) * half) for z in range(2)]
        both = [jnp.concatenate([part[rows, at] for part in parts], axis=1) for at in lanes]
    high, low = halves(jnp.concatenate(both, axis=0))
    table_high, table_low = [jnp.concatenate([ref[k, at] for at in spots], axis=0) for ref in (high_ref, low_ref)]
    got = product(high, low, table_high, table_low)
    count, width = got.shape[0] // 2, got.shape[1] // 2
    return got[:count, :width] - got[count:, width:], got[:count, width:] + got[count:, :width]


def field_body(bits, chunk, *refs):
    parts, (high_ref, low_ref, out) = refs[: len(bits)], refs[len(bits) :]
    width = high_ref.shape[2] // 2
    for k in range(high_ref.shape[0]):
        at = slice(k * width, (k + 1) * width)
        out[0, :, at], out[1, :, at] = field_part(parts, bits, high_ref, low_ref, k, slice(None), chunk)


def update(parts, bits, begun, source, contrast, high_ref, low_ref, field, rows=slice(None), chunk=None):
    width = high_ref.shape[2] // 2
    for k in range(high_ref.shape[0]):
        at = slice(k * width, (k + 1) * width)
        real, imag = field_part(parts, bits, high_ref, low_ref, k, rows, chunk)
        real, imag = begun[0, rows, at] + real, begun[1, rows, at] + imag
        m_real, m_imag = contrast[0, rows, at], contrast[1, rows, at]
        field[0, :, at] = source[0, 0, rows, at] + (m_real * real - m_imag * imag)
        field[1, :, at] = source[1, 0, rows, at] + (m_real * imag + m_imag * real)


def again_body(lat, bits, *refs):
    parts, (begun, source, contrast, high_ref, low_ref), rest = refs[: len(bits)], refs[len(bits) : len(bits) + 5], refs[len(bits) + 5 :]
    out, ahead, field = rest
    update(parts, bits, begun, source, contrast, high_ref, low_ref, field)
    ahead[0], ahead[1] = weighted(contrast, field[0], field[1])
    forward_blocks(ahead[0], ahead[1], high_ref, low_ref, [out], turns(lat)[1:2])


def rest_body(bits, ahead, high_ref, low_ref, *outs):
    forward_blocks(ahead[0], ahead[1], high_ref, low_ref, outs, bits)


def end_body(bits, *refs):
    parts, rest = refs[: len(bits)], refs[len(bits) :]
    (begun, source, contrast, efield, high_ref, low_ref), rest = rest[:6], rest[6:]
    before, out, field = (rest[0] if len(rest) == 3 else None), rest[-2], rest[-1]
    update(parts, bits, begun, source, contrast, high_ref, low_ref, field)
    terms = efield[0, 0] * field[0] - efield[1, 0] * field[1]
    out[...] = terms if before is None else before[...] + terms


def half_rows(which, rows):
    return pl.ds(pl.multiple_of(which * rows, rows), rows)


def deal_body(bits, kept, *refs):
    parts, rest = refs[: len(bits)], refs[len(bits) :]
    begun, source, contrast, efield, high_ref, low_ref, before, out, field = rest
    bit = lax.axis_index("freq") & 1
    count = field.shape[1]
    at = half_rows(bit if kept else 1 - bit, count)
    update(parts, bits, begun, source, contrast, high_ref, low_ref, field, at, CHUNKS - 1)
    cell = before[at] + (efield[0, 0, at] * field[0] - efield[1, 0, at] * field[1])
    width = out.shape[1]
    for k in range(cell.shape[1] // width):
        out[k * count : (k + 1) * count] = cell[:, k * width : (k + 1) * width]


def class_body(gone, kept, kinds, table):
    bit = lax.axis_index("freq") & 1
    count, width = kinds.shape[0] // 2, gone.shape[1]
    spots = [slice(k * width, (k + 1) * width) for k in range(kinds.shape[1] // width)]
    sides = []
    for cell, which in ((gone, 1 - bit), (kept, bit)):
        sides.append((cell[...], jnp.concatenate([kinds[half_rows(which, count), at] for at in spots], axis=0)))
    lines = []
    for c in range(CLASSES):
        chosen = sum(jnp.where(kind == c, cell, 0.0) for cell, kind in sides)
        lines.append(jnp.full((1, width), jnp.sum(chosen), jnp.float32))
    table[...] = jnp.concatenate(lines, axis=0)


def keep_body(one, two, *refs):
    tables, out = refs[:-1], refs[-1]
    rows = one.shape[0]
    out[:rows] = one[...] + two[...]
    out[rows:] = sum((table[...] for table in tables[1:]), tables[0][...])


def add_body(one, two, out):
    out[...] = one[...] + two[...]


def place_body(own, other, cell, classes):
    bit = lax.axis_index("freq") & 1
    width = own.shape[1]
    count = cell.shape[1] // width
    rows = cell.shape[0] // 2
    for which, ref in ((bit, own), (1 - bit, other)):
        at = pl.ds(pl.multiple_of(which * rows, rows), rows)
        for k in range(count):
            cell[at, k * width : (k + 1) * width] = ref[k * rows : (k + 1) * rows]
    total = own[count * rows :] + other[count * rows :]
    row = lax.broadcasted_iota(jnp.int32, total.shape, 0)
    lane = lax.broadcasted_iota(jnp.int32, total.shape, 1)
    line = jnp.sum(jnp.where(row == lane, total, 0.0), axis=0, keepdims=True)
    classes[...] = line[:, :CLASSES] / float(NXY)


def fast_device(sizes, source, contrast, green, efield, cell_class):
    freqs, layers, lat = sizes["freq"], sizes["layer"], sizes["lat"]
    pols, rows, length = source.shape[2], source.shape[4], source.shape[5]
    source = source.reshape(2, pols, rows, length)
    efield = efield.reshape(2, pols, rows, length)
    contrast = contrast.reshape(2, rows, length)
    green = green.reshape(2, layers, rows, length)
    kinds = cell_class.reshape(rows, length)
    col_shape, row_shape = (lat, length, 2 * rows), (lat, 2 * rows, length)
    table_specs, row_specs = [whole(col_shape)] * 2, [whole(row_shape)] * 2
    block = f32(2, rows, rows)
    spectrum = f32(2, length, rows)
    full = pltpu.VMEM((2, rows, length), jnp.float32)
    stage_flops = 24 * rows * length * length
    last = pols - 1
    order = []
    bits, near = turns(lat), lat // 2

    def kernel(body, outs, args, specs, flops=stage_flops, scratch=(), vmem=VMEM_BYTES):
        got = call(body, outs, args, specs, flops, scratch, tuple(order[-1:]), vmem)
        order.append(got[0])
        return got

    small = jnp.asarray(small_tables(length))

    def first():
        specs = [pl.BlockSpec(memory_space=pltpu.HBM)] * 3
        scratch = [
            full,
            full,
            pltpu.VMEM(small.shape, jnp.float32),
            pltpu.VMEM(col_shape, jnp.bfloat16),
            pltpu.VMEM(col_shape, jnp.bfloat16),
            pltpu.SemaphoreType.DMA((3,)),
        ]
        body = functools.partial(first_body, lat)
        args = (source, contrast, small)
        outs = [f32(rows, 2 * rows // CHUNKS)] * (lat * CHUNKS)
        got = kernel(body, outs, args, specs, scratch=scratch, vmem=FIRST_VMEM_BYTES)
        return [send(got[c * lat : (c + 1) * lat], "lat", lat) for c in range(CHUNKS)]

    def start(p):
        specs = [pick(source.shape, p), whole(contrast.shape)] + table_specs
        return send(kernel(functools.partial(start_body, lat), [block] * lat, (source, contrast, *col), specs), "lat", lat)

    def couple(parts, chunks=1):
        specs = [whole(block.shape)] * near + row_specs
        begun = kernel(functools.partial(spectrum_body, bits[:near]), [spectrum], (*parts[:near], *row), specs)[0]
        specs = [whole(block.shape)] * (lat - near) + [whole(spectrum.shape), whole(turned.shape)] + row_specs
        body = functools.partial(couple_body, bits[near:])
        outs = [spectrum if chunks == 1 else f32(length, 2 * rows // chunks)] * (layers * chunks)
        got = kernel(body, outs, (*parts[near:], begun, turned, *row), specs)
        got = [send(got[c::chunks], "layer", layers) for c in range(chunks)]
        return got[0] if chunks == 1 else got

    def couple_chunk(parts, c):
        packed, spread = [whole(part.shape) for part in parts], f32(length, parts[0].shape[1])
        body = functools.partial(spectrum_chunk_body, bits[:near])
        begun = kernel(body, [spread], (*parts[:near], *row), packed[:near] + row_specs)[0]
        body = functools.partial(couple_chunk_body, bits[near:], c)
        specs = packed[near:] + [whole(spread.shape), whole(turned.shape)] + row_specs
        return send(kernel(body, [spread] * layers, (*parts[near:], begun, turned, *row), specs), "layer", layers)

    early, later = bits[1:2], bits[:1] + bits[2:]

    def turn_block(value, d):
        return lax.ppermute(value, "lat", [(i, i ^ d) for i in range(lat)])

    def merged(ahead, got):
        return [got[0], ahead] + [turn_block(value, d) for value, d in zip(got[1:], later[1:])]

    def back(parts, chunk=False):
        specs = [whole(part.shape) for part in parts] + row_specs
        whole_body = back_pair_body if len(parts) > layers else back_body

        def some(chosen):
            body = functools.partial(back_chunk_body if chunk else whole_body, chosen, layers)
            outs = [f32(rows, parts[0].shape[1]) if chunk else block] * len(chosen)
            return kernel(body, outs, (*parts, *row), specs, stage_flops * len(chosen) // lat)

        ahead = turn_block(some(early)[0], early[0])
        return merged(ahead, some(later))

    def fields(p, parts):
        specs = [whole(block.shape)] * near + table_specs
        begun = kernel(functools.partial(field_body, bits[:near], None), [f32(2, rows, length)], (*parts[:near], *col), specs)[0]
        specs = [whole(block.shape)] * (lat - near) + [whole(begun.shape), pick(source.shape, p), whole(contrast.shape)]
        return (*parts[near:], begun, source, contrast), specs

    def again(p, parts):
        args, specs = fields(p, parts)
        outs = [block, f32(2, rows, length)]
        body = functools.partial(again_body, lat, bits[near:])
        got = kernel(body, outs, (*args, *col), specs + table_specs, stage_flops, [full])
        ahead = turn_block(got[0], early[0])
        body = functools.partial(rest_body, later)
        got = kernel(body, [block] * len(later), (got[1], *col), [whole((2, rows, length))] + table_specs)
        return merged(ahead, got)

    def end(p, operands, cells):
        more = () if cells is None else (cells,)
        args, specs = operands
        specs += [pick(efield.shape, p)] + table_specs + [whole((rows, length))] * len(more)
        args = (*args, efield, *col, *more)
        body = functools.partial(end_body, bits[near:])
        return kernel(body, [f32(rows, length)], args, specs, scratch=[full])[0]

    def chunk_fields(p, chunks):
        parts = chunks[0]
        packed = [whole(part.shape) for part in parts]
        body = functools.partial(field_body, bits, 0)
        begun = kernel(body, [f32(2, rows, length)], (*parts, *col), packed + table_specs)[0]
        specs = packed + [whole(begun.shape), pick(source.shape, p), whole(contrast.shape)]
        return (*chunks[1], begun, source, contrast), specs

    def deal(operands, cells, kept):
        args, specs = operands
        specs = specs + [pick(efield.shape, last)] + table_specs + [whole((rows, length))]
        args = (*args, efield, *col, cells)
        outs = [f32(rows // 2 * (length // 128), 128)]
        scratch = [pltpu.VMEM((2, rows // 2, length), jnp.float32)]
        body = functools.partial(deal_body, bits, kept)
        return kernel(body, outs, args, specs, stage_flops // 2, scratch)[0]

    def across(value, d):
        return lax.ppermute(value, "freq", [(i, i ^ d) for i in range(freqs)])

    def simple(body, shape, args):
        return kernel(body, [f32(*shape)], tuple(args), [whole(arg.shape) for arg in args], 1 << 16)[0]

    chains = [first()]
    tables = kernel(
        make_tables,
        [jax.ShapeDtypeStruct(shape, jnp.bfloat16) for shape in (col_shape,) * 2 + (row_shape,) * 2],
        (small,),
        [whole(small.shape)],
        1 << 20,
    )
    col, row = tuple(tables[:2]), tuple(tables[2:])
    turned = kernel(turn_body, [f32(2, layers, length, rows)], (green,), [whole(green.shape)], 1 << 20)[0]
    chunks = chains[0]
    chains[0] = couple_chunk(chunks[0], 0)
    chains += [start(p) for p in range(1, pols)]
    for c in range(1, CHUNKS):
        chains[0] = chains[0] + couple_chunk(chunks[c], c)
    chains[1:] = [couple(chain) for chain in chains[1:]]
    for step in range(ITERS - 1):
        moved = [None] * pols
        for p in range(pols):
            moved[p] = back(chains[p])
            if p > 0:
                chains[p - 1] = couple(moved[p - 1])
            moved[p] = again(p, moved[p])
        chains[last] = couple(moved[last], CHUNKS if step == ITERS - 2 else 1)
    cells = None
    for p in range(last - 1):
        cells = end(p, fields(p, back(chains[p])), cells)
    begun = fields(last - 1, back(chains[last - 1]))
    ahead = [back(chains[last][0], True)]
    cells = end(last - 1, begun, cells)
    ahead.append(back(chains[last][1], True))
    final = chunk_fields(last, ahead)
    gone = deal(final, cells, False)
    came = across(gone, 1)
    kept = deal(final, cells, True)
    found = simple(class_body, (CLASSES, 128), [gone, kept, kinds])
    found = send([found] * lat, "lat", lat)
    kept = simple(keep_body, (kept.shape[0] + CLASSES, 128), [kept, came, *found])
    d = 2
    while d < freqs:
        kept = simple(add_body, kept.shape, [kept, across(kept, d)])
        d *= 2
    both = (kept, across(kept, 1))
    outs = [f32(rows, length), f32(1, CLASSES)]
    cell, classes = kernel(place_body, outs, both, [whole(part.shape) for part in both], 1 << 16)
    return cell.reshape(1, rows, length), classes


def solution(mesh):
    whole_lanes = (
        NXY % (mesh.shape["lat"] * 128) == 0
        and NXY % (mesh.shape["lat"] * 128) == 0
        and mesh.shape["freq"] > 1
        and all(mesh.shape[name] & (mesh.shape[name] - 1) == 0 for name in mesh.axis_names)
    )
    per_device = functools.partial(fast_device, dict(mesh.shape)) if whole_lanes else plain_device

    placed = (
        P(None, "freq", None, "layer", "lat", None),
        P(None, "freq", "layer", "lat", None),
        P(None, "freq", None, "layer", "lat", None),
        P(None, "freq", None, "layer", "lat", None),
        P("layer", "lat", None),
    )
    return jax.shard_map(
        per_device,
        mesh=mesh,
        in_specs=placed,
        out_specs=(P("layer", "lat", None), P("layer", None)),
        check_vma=False,
    )
```

```python
import functools
import math

import jax
import jax.numpy as jnp
import ml_dtypes
import numpy as np
from jax import lax
from jax.experimental import pallas as pl
from jax.experimental.pallas import tpu as pltpu
from jax.sharding import PartitionSpec as P

NXY = 512
ITERS = 2
CLASSES = 8


highest = lax.Precision.HIGHEST


def tables(length):
    index = jnp.arange(length, dtype=jnp.int32)
    phase = index[:, None] * index[None, :] % length
    angle = phase.astype(jnp.float32) * (2.0 * math.pi / length)
    factor = 1.0 / math.sqrt(length)
    return (jnp.cos(angle) * factor, jnp.sin(angle) * factor)


def forward(field, cosine, sine):
    first = jnp.einsum("zfplxy,yk->zfplkx", field, cosine, precision=highest)
    second = jnp.einsum("zfplxy,yk->zfplkx", field, sine, precision=highest)
    partial_spec = jnp.stack([first[0] + second[1], first[1] - second[0]])
    turned = lax.all_to_all(partial_spec, "lat", split_axis=4, concat_axis=5, tiled=True)
    first = jnp.einsum("zfplkx,xq->zfplkq", turned, cosine, precision=highest)
    second = jnp.einsum("zfplkx,xq->zfplkq", turned, sine, precision=highest)
    return jnp.stack([first[0] + second[1], first[1] - second[0]])


def inverse(mixed, cosine, sine):
    first = jnp.einsum("lzfpkq,qx->zfplkx", mixed, cosine, precision=highest)
    second = jnp.einsum("lzfpkq,qx->zfplkx", mixed, sine, precision=highest)
    half_back = jnp.stack([first[0] - second[1], first[1] + second[0]])
    turned = lax.all_to_all(half_back, "lat", split_axis=5, concat_axis=4, tiled=True)
    first = jnp.einsum("zfplkx,ky->zfplxy", turned, cosine, precision=highest)
    second = jnp.einsum("zfplkx,ky->zfplxy", turned, sine, precision=highest)
    return jnp.stack([first[0] - second[1], first[1] + second[0]])


def couple_product(left, right):
    return jnp.einsum("foiyx,fpiyx->ofpyx", left, right, precision=highest)


def couple(kernel, spectra):
    real_part = couple_product(kernel[0], spectra[0]) - couple_product(kernel[1], spectra[1])
    imag_part = couple_product(kernel[0], spectra[1]) + couple_product(kernel[1], spectra[0])
    return jnp.stack([real_part, imag_part], axis=1)


def cmul(factor, field):
    return jnp.stack(
        [factor[0] * field[0] - factor[1] * field[1], factor[0] * field[1] + factor[1] * field[0]]
    )


def plain_device(source, contrast, green, efield, cell_class):
    cosine, sine = tables(source.shape[5])
    factor = contrast[:, :, None]
    field = source
    for step in range(ITERS):
        spectra = forward(cmul(factor, field), cosine, sine)
        mixed = lax.psum_scatter(couple(green, spectra), "layer", scatter_dimension=0, tiled=True)
        field = source + cmul(factor, inverse(mixed, cosine, sine))
    cell_terms = jnp.sum(efield[0] * field[0] - efield[1] * field[1], axis=(0, 1))
    cell = lax.psum(cell_terms, "freq")
    onehot = (cell_class[None] == jnp.arange(CLASSES, dtype=jnp.int32)[:, None, None, None]).astype(
        jnp.float32
    )
    local_sums = jnp.einsum("clxy,lxy->lc", onehot, cell_terms, precision=highest) / float(NXY)
    classes = lax.psum(local_sums, ("freq", "lat"))
    return (cell, classes)


VMEM_BYTES = 40 * 1024 * 1024
FIRST_VMEM_BYTES = 62 * 1024 * 1024
FINE = 16
CHUNKS = 2


def small_tables(length):
    index = np.arange(length)

    def waves(first):
        angle = (first[:, None] * index[None, :] % length) * (2.0 * np.pi / length)
        return np.stack([np.cos(angle), np.sin(angle)])

    both = [waves(index[::FINE]) / math.sqrt(length), waves(index[:FINE])]
    return np.concatenate(both, axis=1).astype(np.float32)


def halves(value):
    high = value.astype(jnp.bfloat16)
    return high, (value - high.astype(jnp.float32)).astype(jnp.bfloat16)


def product(left_high, left_low, right_high, right_low):
    def dot(left, right):
        return jnp.dot(left, right, preferred_element_type=jnp.float32)

    return dot(left_high, right_high) + (dot(left_high, right_low) + dot(left_low, right_high))


def along_y(real, imag, high_ref, low_ref, where, sign):
    rows = real.shape[0]
    high, low = halves(jnp.concatenate([real, imag], axis=0))
    got = product(high, low, high_ref[where], low_ref[where])
    width = got.shape[1] // 2
    out_real = got[:rows, :width] - sign * got[rows:, width:]
    out_imag = got[rows:, :width] + sign * got[:rows, width:]
    return out_real, out_imag


def along_x(high_ref, low_ref, where, high, low, sign):
    got = product(high_ref[where], low_ref[where], high, low)
    rows, width = got.shape[0] // 2, got.shape[1] // 2
    out_real = got[:rows, :width] - sign * got[rows:, width:]
    out_imag = got[:rows, width:] + sign * got[rows:, :width]
    return out_real, out_imag


def call(body, outs, args, specs, flops, scratch=(), after=(), vmem=VMEM_BYTES):
    sizes = sum(math.prod(o.shape) * 4 for o in outs)
    taken, tied = len(args), len(after)

    def ordered(*refs):
        body(*refs[:taken], *refs[taken + tied :])

    return pl.pallas_call(
        ordered,
        grid=(1,),
        out_shape=outs,
        in_specs=list(specs) + [pl.BlockSpec(memory_space=pl.ANY)] * tied,
        out_specs=[whole(o.shape) for o in outs],
        scratch_shapes=list(scratch),
        compiler_params=pltpu.CompilerParams(vmem_limit_bytes=vmem),
        cost_estimate=pl.CostEstimate(flops=flops, bytes_accessed=2 * sizes, transcendentals=0),
    )(*args, *after)


def whole(shape):
    return pl.BlockSpec(tuple(shape), lambda step: (0,) * len(shape))


def pick(shape, pol):
    return pl.BlockSpec((shape[0], 1) + tuple(shape[2:]), lambda step: (0, pol, 0, 0))


def f32(*shape):
    return jax.ShapeDtypeStruct(shape, jnp.float32)


def turns(size):
    return sorted(range(size), key=lambda d: (d == 1, d))


def send(blocks, axis, size):
    got = [blocks[0]]
    for d, block in zip(turns(size)[1:], blocks[1:]):
        got.append(lax.ppermute(block, axis, [(i, i ^ d) for i in range(size)]))
    return got


def make_tables(small, col_high, col_low, row_high=None, row_low=None):
    blocks, length, width = col_high.shape
    width = width // 2
    steps = length // FINE
    f_real, f_imag = small[0, steps:], small[1, steps:]
    for a in range(steps):
        c_real, c_imag = small[0, a : a + 1], small[1, a : a + 1]
        pair = (c_real * f_real - c_imag * f_imag, c_real * f_imag + c_imag * f_real)
        block, first = a * FINE // width, a * FINE % width
        for z, part in enumerate(pair):
            for value, row, col in zip(halves(part), (row_high, row_low), (col_high, col_low)):
                if row is not None:
                    row[block, z * width + first : z * width + first + FINE] = value
                for k in range(blocks):
                    spot = slice(a * FINE, (a + 1) * FINE)
                    col[k, spot, z * width : (z + 1) * width] = value[:, k * width : (k + 1) * width]


def forward_blocks(real, imag, high_ref, low_ref, out_refs, bits):
    me = lax.axis_index("lat")
    for d, out in zip(bits, out_refs):
        out[0], out[1] = along_y(real, imag, high_ref, low_ref, me ^ d, -1)


def weighted(contrast, real, imag):
    m_real, m_imag = contrast[0], contrast[1]
    return m_real * real - m_imag * imag, m_real * imag + m_imag * real


def first_body(lat, source, contrast, small, *refs):
    outs, (field, factor, waves, high, low, sems) = refs[: lat * CHUNKS], refs[lat * CHUNKS :]
    copies = [
        pltpu.make_async_copy(small, waves, sems.at[0]),
        pltpu.make_async_copy(source.at[:, 0], field, sems.at[1]),
        pltpu.make_async_copy(contrast, factor, sems.at[2]),
    ]
    for copy in copies:
        copy.start()
    copies[0].wait()
    make_tables(waves, high, low)
    copies[1].wait()
    copies[2].wait()
    real, imag = weighted(factor, field[0], field[1])
    me = lax.axis_index("lat")
    for i, d in enumerate(turns(lat)):
        got = along_y(real, imag, high, low, me ^ d, -1)
        half = got[0].shape[1] // CHUNKS
        for c in range(CHUNKS):
            outs[c * lat + i][...] = jnp.concatenate([part[:, c * half : (c + 1) * half] for part in got], axis=1)


def start_body(lat, source, contrast, high_ref, low_ref, *outs):
    real, imag = weighted(contrast, source[0, 0], source[1, 0])
    forward_blocks(real, imag, high_ref, low_ref, outs, turns(lat))


def turn_body(green, out):
    for z in range(green.shape[0]):
        for o in range(green.shape[1]):
            out[z, o] = green[z, o].T


def blocks_of(bits, width):
    me = lax.axis_index("lat")
    return [pl.ds(pl.multiple_of((me ^ d) * width, width), width) for d in bits]


def spectrum_part(parts, bits, high_ref, low_ref, k):
    columns = blocks_of(bits, parts[0].shape[1])
    high, low = halves(jnp.concatenate([jnp.concatenate([part[0], part[1]], axis=1) for part in parts], axis=0))
    table_high, table_low = [jnp.concatenate([ref[k, :, at] for at in columns], axis=1) for ref in (high_ref, low_ref)]
    got = product(table_high, table_low, high, low)
    rows, width = got.shape[0] // 2, got.shape[1] // 2
    return got[:rows, :width] + got[rows:, width:], got[:rows, width:] - got[rows:, :width]


def spectrum_body(bits, *refs):
    parts, (high_ref, low_ref, out) = refs[: len(bits)], refs[len(bits) :]
    rows = high_ref.shape[1] // 2
    for k in range(high_ref.shape[0]):
        at = slice(k * rows, (k + 1) * rows)
        out[0, at], out[1, at] = spectrum_part(parts, bits, high_ref, low_ref, k)


def couple_body(bits, *refs):
    parts, (begun, green, high_ref, low_ref), outs = refs[: len(bits)], refs[len(bits) : len(bits) + 4], refs[len(bits) + 4 :]
    layer = lax.axis_index("layer")
    rows = high_ref.shape[1] // 2
    for k in range(high_ref.shape[0]):
        at = slice(k * rows, (k + 1) * rows)
        real, imag = spectrum_part(parts, bits, high_ref, low_ref, k)
        real, imag = begun[0, at] + real, begun[1, at] + imag
        chunks = len(outs) // green.shape[1]
        for e in range(green.shape[1]):
            g_real, g_imag = green[0, layer ^ e, at], green[1, layer ^ e, at]
            pair = (g_real * real - g_imag * imag, g_real * imag + g_imag * real)
            if chunks == 1:
                outs[e][0, at], outs[e][1, at] = pair
            else:
                half = real.shape[1] // chunks
                for c in range(chunks):
                    spot = slice(c * half, (c + 1) * half)
                    outs[e * chunks + c][at] = jnp.concatenate([part[:, spot] for part in pair], axis=1)


def swap(packed):
    return pltpu.roll(packed, packed.shape[1] // 2, 1)


def spectrum_chunk(parts, bits, high_ref, low_ref, k):
    columns = blocks_of(bits, parts[0].shape[0])
    high, low = halves(jnp.concatenate([part[...] for part in parts], axis=0))
    table_high, table_low = [jnp.concatenate([ref[k, :, at] for at in columns], axis=1) for ref in (high_ref, low_ref)]
    got = product(table_high, table_low, high, low)
    rows, width = got.shape[0] // 2, got.shape[1]
    lane = lax.broadcasted_iota(jnp.int32, (rows, width), 1)
    turned = swap(got[rows:])
    return got[:rows] + jnp.where(lane < width // 2, turned, -turned)


def spectrum_chunk_body(bits, *refs):
    parts, (high_ref, low_ref, out) = refs[: len(bits)], refs[len(bits) :]
    rows = high_ref.shape[1] // 2
    for k in range(high_ref.shape[0]):
        out[k * rows : (k + 1) * rows] = spectrum_chunk(parts, bits, high_ref, low_ref, k)


def couple_chunk_body(bits, chunk, *refs):
    parts, (begun, green, high_ref, low_ref), outs = refs[: len(bits)], refs[len(bits) : len(bits) + 4], refs[len(bits) + 4 :]
    layer = lax.axis_index("layer")
    rows, half = high_ref.shape[1] // 2, begun.shape[1] // 2
    for k in range(high_ref.shape[0]):
        at = slice(k * rows, (k + 1) * rows)
        spectra = begun[at] + spectrum_chunk(parts, bits, high_ref, low_ref, k)
        swapped = swap(spectra)
        for e, out in enumerate(outs):
            g_real, g_imag = [green[z, layer ^ e, at][:, chunk * half : (chunk + 1) * half] for z in range(2)]
            both = jnp.concatenate([g_real, g_real], axis=1)
            cross = jnp.concatenate([-g_imag, g_imag], axis=1)
            out[at] = both * spectra + cross * swapped


def back_body(bits, layers, *refs):
    parts, (high_ref, low_ref), outs = refs[:layers], refs[layers : layers + 2], refs[layers + 2 :]
    me = lax.axis_index("lat")
    mixed = [sum((part[z] for part in parts[1:]), parts[0][z]) for z in range(2)]
    high, low = halves(jnp.concatenate(mixed, axis=1))
    for d, out in zip(bits, outs):
        out[0], out[1] = along_x(high_ref, low_ref, me ^ d, high, low, +1)


def back_chunk_body(bits, layers, *refs):
    parts, (high_ref, low_ref), outs = refs[:layers], refs[layers : layers + 2], refs[layers + 2 :]
    me = lax.axis_index("lat")
    high, low = halves(sum((part[...] for part in parts[1:]), parts[0][...]))
    for d, out in zip(bits, outs):
        got = product(high_ref[me ^ d], low_ref[me ^ d], high, low)
        rows, width = got.shape[0] // 2, got.shape[1]
        lane = lax.broadcasted_iota(jnp.int32, (rows, width), 1)
        turned = pltpu.roll(got[rows:], width // 2, 1)
        out[...] = got[:rows] + jnp.where(lane < width // 2, -turned, turned)


def field_part(parts, bits, high_ref, low_ref, k, rows, chunk=None):
    if chunk is None:
        spots = blocks_of(bits, parts[0].shape[2])
        both = [jnp.concatenate([part[z, rows] for part in parts], axis=1) for z in range(2)]
    else:
        me = lax.axis_index("lat")
        half = parts[0].shape[1] // 2
        spots = [pl.ds(pl.multiple_of(((me ^ d) * CHUNKS + chunk) * half, half), half) for d in bits]
        lanes = [slice(z * half, (z + 1) * half) for z in range(2)]
        both = [jnp.concatenate([part[rows, at] for part in parts], axis=1) for at in lanes]
    high, low = halves(jnp.concatenate(both, axis=0))
    table_high, table_low = [jnp.concatenate([ref[k, at] for at in spots], axis=0) for ref in (high_ref, low_ref)]
    got = product(high, low, table_high, table_low)
    count, width = got.shape[0] // 2, got.shape[1] // 2
    return got[:count, :width] - got[count:, width:], got[:count, width:] + got[count:, :width]


def field_body(bits, chunk, *refs):
    parts, (high_ref, low_ref, out) = refs[: len(bits)], refs[len(bits) :]
    width = high_ref.shape[2] // 2
    for k in range(high_ref.shape[0]):
        at = slice(k * width, (k + 1) * width)
        out[0, :, at], out[1, :, at] = field_part(parts, bits, high_ref, low_ref, k, slice(None), chunk)


def update(parts, bits, begun, source, contrast, high_ref, low_ref, field, rows=slice(None), chunk=None):
    width = high_ref.shape[2] // 2
    for k in range(high_ref.shape[0]):
        at = slice(k * width, (k + 1) * width)
        real, imag = field_part(parts, bits, high_ref, low_ref, k, rows, chunk)
        real, imag = begun[0, rows, at] + real, begun[1, rows, at] + imag
        m_real, m_imag = contrast[0, rows, at], contrast[1, rows, at]
        field[0, :, at] = source[0, 0, rows, at] + (m_real * real - m_imag * imag)
        field[1, :, at] = source[1, 0, rows, at] + (m_real * imag + m_imag * real)


def again_body(lat, bits, chunk, *refs):
    parts, (begun, source, contrast, high_ref, low_ref), rest = refs[: len(bits)], refs[len(bits) : len(bits) + 5], refs[len(bits) + 5 :]
    out, ahead, field = rest
    update(parts, bits, begun, source, contrast, high_ref, low_ref, field, chunk=chunk)
    ahead[0], ahead[1] = weighted(contrast, field[0], field[1])
    forward_blocks(ahead[0], ahead[1], high_ref, low_ref, [out], turns(lat)[1:2])


def rest_body(bits, ahead, high_ref, low_ref, *outs):
    forward_blocks(ahead[0], ahead[1], high_ref, low_ref, outs, bits)


def end_body(bits, *refs):
    parts, rest = refs[: len(bits)], refs[len(bits) :]
    (begun, source, contrast, efield, high_ref, low_ref), rest = rest[:6], rest[6:]
    before, out, field = (rest[0] if len(rest) == 3 else None), rest[-2], rest[-1]
    update(parts, bits, begun, source, contrast, high_ref, low_ref, field)
    terms = efield[0, 0] * field[0] - efield[1, 0] * field[1]
    out[...] = terms if before is None else before[...] + terms


def half_rows(which, rows):
    return pl.ds(pl.multiple_of(which * rows, rows), rows)


def deal_body(bits, kept, *refs):
    parts, rest = refs[: len(bits)], refs[len(bits) :]
    begun, source, contrast, efield, high_ref, low_ref, before, out, field = rest
    bit = lax.axis_index("freq") & 1
    count = field.shape[1]
    at = half_rows(bit if kept else 1 - bit, count)
    update(parts, bits, begun, source, contrast, high_ref, low_ref, field, at, CHUNKS - 1)
    cell = before[at] + (efield[0, 0, at] * field[0] - efield[1, 0, at] * field[1])
    width = out.shape[1]
    for k in range(cell.shape[1] // width):
        out[k * count : (k + 1) * count] = cell[:, k * width : (k + 1) * width]


def class_body(gone, kept, kinds, table):
    bit = lax.axis_index("freq") & 1
    count, width = kinds.shape[0] // 2, gone.shape[1]
    spots = [slice(k * width, (k + 1) * width) for k in range(kinds.shape[1] // width)]
    sides = []
    for cell, which in ((gone, 1 - bit), (kept, bit)):
        sides.append((cell[...], jnp.concatenate([kinds[half_rows(which, count), at] for at in spots], axis=0)))
    lines = []
    for c in range(CLASSES):
        chosen = sum(jnp.where(kind == c, cell, 0.0) for cell, kind in sides)
        lines.append(jnp.full((1, width), jnp.sum(chosen), jnp.float32))
    table[...] = jnp.concatenate(lines, axis=0)


def keep_body(one, two, *refs):
    tables, out = refs[:-1], refs[-1]
    rows = one.shape[0]
    out[:rows] = one[...] + two[...]
    out[rows:] = sum((table[...] for table in tables[1:]), tables[0][...])


def add_body(one, two, out):
    out[...] = one[...] + two[...]


def place_body(own, other, cell, classes):
    bit = lax.axis_index("freq") & 1
    width = own.shape[1]
    count = cell.shape[1] // width
    rows = cell.shape[0] // 2
    for which, ref in ((bit, own), (1 - bit, other)):
        at = pl.ds(pl.multiple_of(which * rows, rows), rows)
        for k in range(count):
            cell[at, k * width : (k + 1) * width] = ref[k * rows : (k + 1) * rows]
    total = own[count * rows :] + other[count * rows :]
    row = lax.broadcasted_iota(jnp.int32, total.shape, 0)
    lane = lax.broadcasted_iota(jnp.int32, total.shape, 1)
    line = jnp.sum(jnp.where(row == lane, total, 0.0), axis=0, keepdims=True)
    classes[...] = line[:, :CLASSES] / float(NXY)


def fast_device(sizes, source, contrast, green, efield, cell_class):
    freqs, layers, lat = sizes["freq"], sizes["layer"], sizes["lat"]
    pols, rows, length = source.shape[2], source.shape[4], source.shape[5]
    source = source.reshape(2, pols, rows, length)
    efield = efield.reshape(2, pols, rows, length)
    contrast = contrast.reshape(2, rows, length)
    green = green.reshape(2, layers, rows, length)
    kinds = cell_class.reshape(rows, length)
    col_shape, row_shape = (lat, length, 2 * rows), (lat, 2 * rows, length)
    table_specs, row_specs = [whole(col_shape)] * 2, [whole(row_shape)] * 2
    block = f32(2, rows, rows)
    spectrum = f32(2, length, rows)
    full = pltpu.VMEM((2, rows, length), jnp.float32)
    stage_flops = 24 * rows * length * length
    last = pols - 1
    order = []
    bits, near = turns(lat), lat // 2

    def kernel(body, outs, args, specs, flops=stage_flops, scratch=(), vmem=VMEM_BYTES):
        got = call(body, outs, args, specs, flops, scratch, tuple(order[-1:]), vmem)
        order.append(got[0])
        return got

    small = jnp.asarray(small_tables(length))

    def first():
        specs = [pl.BlockSpec(memory_space=pltpu.HBM)] * 3
        scratch = [
            full,
            full,
            pltpu.VMEM(small.shape, jnp.float32),
            pltpu.VMEM(col_shape, jnp.bfloat16),
            pltpu.VMEM(col_shape, jnp.bfloat16),
            pltpu.SemaphoreType.DMA((3,)),
        ]
        body = functools.partial(first_body, lat)
        args = (source, contrast, small)
        outs = [f32(rows, 2 * rows // CHUNKS)] * (lat * CHUNKS)
        got = kernel(body, outs, args, specs, scratch=scratch, vmem=FIRST_VMEM_BYTES)
        return [send(got[c * lat : (c + 1) * lat], "lat", lat) for c in range(CHUNKS)]

    def start(p):
        specs = [pick(source.shape, p), whole(contrast.shape)] + table_specs
        return send(kernel(functools.partial(start_body, lat), [block] * lat, (source, contrast, *col), specs), "lat", lat)

    def couple(parts, chunks=1):
        specs = [whole(block.shape)] * near + row_specs
        begun = kernel(functools.partial(spectrum_body, bits[:near]), [spectrum], (*parts[:near], *row), specs)[0]
        specs = [whole(block.shape)] * (lat - near) + [whole(spectrum.shape), whole(turned.shape)] + row_specs
        body = functools.partial(couple_body, bits[near:])
        outs = [spectrum if chunks == 1 else f32(length, 2 * rows // chunks)] * (layers * chunks)
        got = kernel(body, outs, (*parts[near:], begun, turned, *row), specs)
        got = [send(got[c::chunks], "layer", layers) for c in range(chunks)]
        return got[0] if chunks == 1 else got

    def couple_chunk(parts, c):
        packed, spread = [whole(part.shape) for part in parts], f32(length, parts[0].shape[1])
        body = functools.partial(spectrum_chunk_body, bits[:near])
        begun = kernel(body, [spread], (*parts[:near], *row), packed[:near] + row_specs)[0]
        body = functools.partial(couple_chunk_body, bits[near:], c)
        specs = packed[near:] + [whole(spread.shape), whole(turned.shape)] + row_specs
        return send(kernel(body, [spread] * layers, (*parts[near:], begun, turned, *row), specs), "layer", layers)

    early, later = bits[1:2], bits[:1] + bits[2:]

    def turn_block(value, d):
        return lax.ppermute(value, "lat", [(i, i ^ d) for i in range(lat)])

    def merged(ahead, got):
        return [got[0], ahead] + [turn_block(value, d) for value, d in zip(got[1:], later[1:])]

    def back(parts, chunk=False):
        specs = [whole(part.shape) for part in parts] + row_specs

        def some(chosen):
            body = functools.partial(back_chunk_body if chunk else back_body, chosen, layers)
            outs = [f32(rows, parts[0].shape[1]) if chunk else block] * len(chosen)
            return kernel(body, outs, (*parts, *row), specs, stage_flops * len(chosen) // lat)

        ahead = turn_block(some(early)[0], early[0])
        return merged(ahead, some(later))

    def fields(p, parts):
        specs = [whole(block.shape)] * near + table_specs
        begun = kernel(functools.partial(field_body, bits[:near], None), [f32(2, rows, length)], (*parts[:near], *col), specs)[0]
        specs = [whole(block.shape)] * (lat - near) + [whole(begun.shape), pick(source.shape, p), whole(contrast.shape)]
        return (*parts[near:], begun, source, contrast), specs

    def again(operands, chosen, chunk=None):
        args, specs = operands
        outs = [block, f32(2, rows, length)]
        body = functools.partial(again_body, lat, chosen, chunk)
        got = kernel(body, outs, (*args, *col), specs + table_specs, stage_flops, [full])
        ahead = turn_block(got[0], early[0])
        body = functools.partial(rest_body, later)
        got = kernel(body, [block] * len(later), (got[1], *col), [whole((2, rows, length))] + table_specs)
        return merged(ahead, got)

    def end(p, operands, cells):
        more = () if cells is None else (cells,)
        args, specs = operands
        specs += [pick(efield.shape, p)] + table_specs + [whole((rows, length))] * len(more)
        args = (*args, efield, *col, *more)
        body = functools.partial(end_body, bits[near:])
        return kernel(body, [f32(rows, length)], args, specs, scratch=[full])[0]

    def chunk_fields(p, chunks):
        parts = chunks[0]
        packed = [whole(part.shape) for part in parts]
        body = functools.partial(field_body, bits, 0)
        begun = kernel(body, [f32(2, rows, length)], (*parts, *col), packed + table_specs)[0]
        specs = packed + [whole(begun.shape), pick(source.shape, p), whole(contrast.shape)]
        return (*chunks[1], begun, source, contrast), specs

    def deal(operands, cells, kept):
        args, specs = operands
        specs = specs + [pick(efield.shape, last)] + table_specs + [whole((rows, length))]
        args = (*args, efield, *col, cells)
        outs = [f32(rows // 2 * (length // 128), 128)]
        scratch = [pltpu.VMEM((2, rows // 2, length), jnp.float32)]
        body = functools.partial(deal_body, bits, kept)
        return kernel(body, outs, args, specs, stage_flops // 2, scratch)[0]

    def across(value, d):
        return lax.ppermute(value, "freq", [(i, i ^ d) for i in range(freqs)])

    def simple(body, shape, args):
        return kernel(body, [f32(*shape)], tuple(args), [whole(arg.shape) for arg in args], 1 << 16)[0]

    chains = [first()]
    tables = kernel(
        make_tables,
        [jax.ShapeDtypeStruct(shape, jnp.bfloat16) for shape in (col_shape,) * 2 + (row_shape,) * 2],
        (small,),
        [whole(small.shape)],
        1 << 20,
    )
    col, row = tuple(tables[:2]), tuple(tables[2:])
    turned = kernel(turn_body, [f32(2, layers, length, rows)], (green,), [whole(green.shape)], 1 << 20)[0]
    chunks = chains[0]
    summed = [couple_chunk(chunks[0], 0)]
    chains += [start(p) for p in range(1, pols)]
    for c in range(1, CHUNKS):
        summed.append(couple_chunk(chunks[c], c))
    ahead = [back(chunk, True) for chunk in summed[:-1]]
    chains[1:] = [couple(chain) for chain in chains[1:]]
    for step in range(ITERS - 1):
        moved = [None] * pols
        for p in range(pols):
            if p == 0 and step == 0:
                ahead.append(back(summed[-1], True))
                moved[p] = again(chunk_fields(p, ahead), bits, CHUNKS - 1)
                continue
            moved[p] = back(chains[p])
            if p > 0:
                chains[p - 1] = couple(moved[p - 1])
            moved[p] = again(fields(p, moved[p]), bits[near:])
        chains[last] = couple(moved[last], CHUNKS if step == ITERS - 2 else 1)
    cells = None
    for p in range(last - 1):
        cells = end(p, fields(p, back(chains[p])), cells)
    begun = fields(last - 1, back(chains[last - 1]))
    ahead = [back(chains[last][0], True)]
    cells = end(last - 1, begun, cells)
    ahead.append(back(chains[last][1], True))
    final = chunk_fields(last, ahead)
    gone = deal(final, cells, False)
    came = across(gone, 1)
    kept = deal(final, cells, True)
    found = simple(class_body, (CLASSES, 128), [gone, kept, kinds])
    found = send([found] * lat, "lat", lat)
    kept = simple(keep_body, (kept.shape[0] + CLASSES, 128), [kept, came, *found])
    d = 2
    while d < freqs:
        kept = simple(add_body, kept.shape, [kept, across(kept, d)])
        d *= 2
    both = (kept, across(kept, 1))
    outs = [f32(rows, length), f32(1, CLASSES)]
    cell, classes = kernel(place_body, outs, both, [whole(part.shape) for part in both], 1 << 16)
    return cell.reshape(1, rows, length), classes


def solution(mesh):
    whole_lanes = (
        NXY % (mesh.shape["lat"] * 128) == 0
        and NXY % (mesh.shape["lat"] * 128) == 0
        and mesh.shape["freq"] > 1
        and all(mesh.shape[name] & (mesh.shape[name] - 1) == 0 for name in mesh.axis_names)
    )
    per_device = functools.partial(fast_device, dict(mesh.shape)) if whole_lanes else plain_device

    placed = (
        P(None, "freq", None, "layer", "lat", None),
        P(None, "freq", "layer", "lat", None),
        P(None, "freq", None, "layer", "lat", None),
        P(None, "freq", None, "layer", "lat", None),
        P("layer", "lat", None),
    )
    return jax.shard_map(
        per_device,
        mesh=mesh,
        in_specs=placed,
        out_specs=(P("layer", "lat", None), P("layer", None)),
        check_vma=False,
    )
```

```python
import functools
import math

import jax
import jax.numpy as jnp
import ml_dtypes
import numpy as np
from jax import lax
from jax.experimental import pallas as pl
from jax.experimental.pallas import tpu as pltpu
from jax.sharding import PartitionSpec as P

NXY = 512
ITERS = 2
CLASSES = 8


highest = lax.Precision.HIGHEST


def tables(length):
    index = jnp.arange(length, dtype=jnp.int32)
    phase = index[:, None] * index[None, :] % length
    angle = phase.astype(jnp.float32) * (2.0 * math.pi / length)
    factor = 1.0 / math.sqrt(length)
    return (jnp.cos(angle) * factor, jnp.sin(angle) * factor)


def forward(field, cosine, sine):
    first = jnp.einsum("zfplxy,yk->zfplkx", field, cosine, precision=highest)
    second = jnp.einsum("zfplxy,yk->zfplkx", field, sine, precision=highest)
    partial_spec = jnp.stack([first[0] + second[1], first[1] - second[0]])
    turned = lax.all_to_all(partial_spec, "lat", split_axis=4, concat_axis=5, tiled=True)
    first = jnp.einsum("zfplkx,xq->zfplkq", turned, cosine, precision=highest)
    second = jnp.einsum("zfplkx,xq->zfplkq", turned, sine, precision=highest)
    return jnp.stack([first[0] + second[1], first[1] - second[0]])


def inverse(mixed, cosine, sine):
    first = jnp.einsum("lzfpkq,qx->zfplkx", mixed, cosine, precision=highest)
    second = jnp.einsum("lzfpkq,qx->zfplkx", mixed, sine, precision=highest)
    half_back = jnp.stack([first[0] - second[1], first[1] + second[0]])
    turned = lax.all_to_all(half_back, "lat", split_axis=5, concat_axis=4, tiled=True)
    first = jnp.einsum("zfplkx,ky->zfplxy", turned, cosine, precision=highest)
    second = jnp.einsum("zfplkx,ky->zfplxy", turned, sine, precision=highest)
    return jnp.stack([first[0] - second[1], first[1] + second[0]])


def couple_product(left, right):
    return jnp.einsum("foiyx,fpiyx->ofpyx", left, right, precision=highest)


def couple(kernel, spectra):
    real_part = couple_product(kernel[0], spectra[0]) - couple_product(kernel[1], spectra[1])
    imag_part = couple_product(kernel[0], spectra[1]) + couple_product(kernel[1], spectra[0])
    return jnp.stack([real_part, imag_part], axis=1)


def cmul(factor, field):
    return jnp.stack(
        [factor[0] * field[0] - factor[1] * field[1], factor[0] * field[1] + factor[1] * field[0]]
    )


def plain_device(source, contrast, green, efield, cell_class):
    cosine, sine = tables(source.shape[5])
    factor = contrast[:, :, None]
    field = source
    for step in range(ITERS):
        spectra = forward(cmul(factor, field), cosine, sine)
        mixed = lax.psum_scatter(couple(green, spectra), "layer", scatter_dimension=0, tiled=True)
        field = source + cmul(factor, inverse(mixed, cosine, sine))
    cell_terms = jnp.sum(efield[0] * field[0] - efield[1] * field[1], axis=(0, 1))
    cell = lax.psum(cell_terms, "freq")
    onehot = (cell_class[None] == jnp.arange(CLASSES, dtype=jnp.int32)[:, None, None, None]).astype(
        jnp.float32
    )
    local_sums = jnp.einsum("clxy,lxy->lc", onehot, cell_terms, precision=highest) / float(NXY)
    classes = lax.psum(local_sums, ("freq", "lat"))
    return (cell, classes)


VMEM_BYTES = 40 * 1024 * 1024
FIRST_VMEM_BYTES = 62 * 1024 * 1024
FINE = 16
CHUNKS = 2


def small_tables(length):
    index = np.arange(length)

    def waves(first):
        angle = (first[:, None] * index[None, :] % length) * (2.0 * np.pi / length)
        return np.stack([np.cos(angle), np.sin(angle)])

    both = [waves(index[::FINE]) / math.sqrt(length), waves(index[:FINE])]
    return np.concatenate(both, axis=1).astype(np.float32)


def halves(value):
    high = value.astype(jnp.bfloat16)
    return high, (value - high.astype(jnp.float32)).astype(jnp.bfloat16)


def product(left_high, left_low, right_high, right_low):
    def dot(left, right):
        return jnp.dot(left, right, preferred_element_type=jnp.float32)

    return dot(left_high, right_high) + (dot(left_high, right_low) + dot(left_low, right_high))


def along_y(real, imag, high_ref, low_ref, where, sign):
    rows = real.shape[0]
    high, low = halves(jnp.concatenate([real, imag], axis=0))
    got = product(high, low, high_ref[where], low_ref[where])
    width = got.shape[1] // 2
    out_real = got[:rows, :width] - sign * got[rows:, width:]
    out_imag = got[rows:, :width] + sign * got[:rows, width:]
    return out_real, out_imag


def along_x(high_ref, low_ref, where, high, low, sign):
    got = product(high_ref[where], low_ref[where], high, low)
    rows, width = got.shape[0] // 2, got.shape[1] // 2
    out_real = got[:rows, :width] - sign * got[rows:, width:]
    out_imag = got[:rows, width:] + sign * got[rows:, :width]
    return out_real, out_imag


def call(body, outs, args, specs, flops, scratch=(), after=(), vmem=VMEM_BYTES):
    sizes = sum(math.prod(o.shape) * 4 for o in outs)
    taken, tied = len(args), len(after)

    def ordered(*refs):
        body(*refs[:taken], *refs[taken + tied :])

    return pl.pallas_call(
        ordered,
        grid=(1,),
        out_shape=outs,
        in_specs=list(specs) + [pl.BlockSpec(memory_space=pl.ANY)] * tied,
        out_specs=[whole(o.shape) for o in outs],
        scratch_shapes=list(scratch),
        compiler_params=pltpu.CompilerParams(vmem_limit_bytes=vmem),
        cost_estimate=pl.CostEstimate(flops=flops, bytes_accessed=2 * sizes, transcendentals=0),
    )(*args, *after)


def whole(shape):
    return pl.BlockSpec(tuple(shape), lambda step: (0,) * len(shape))


def pick(shape, pol):
    return pl.BlockSpec((shape[0], 1) + tuple(shape[2:]), lambda step: (0, pol, 0, 0))


def f32(*shape):
    return jax.ShapeDtypeStruct(shape, jnp.float32)


def turns(size):
    return sorted(range(size), key=lambda d: (d == 1, d > 0, -d))


def send(blocks, axis, size):
    got = [blocks[0]]
    for d, block in zip(turns(size)[1:], blocks[1:]):
        got.append(lax.ppermute(block, axis, [(i, i ^ d) for i in range(size)]))
    return got


def make_tables(small, col_high, col_low, row_high=None, row_low=None):
    blocks, length, width = col_high.shape
    width = width // 2
    steps = length // FINE
    f_real, f_imag = small[0, steps:], small[1, steps:]
    for a in range(steps):
        c_real, c_imag = small[0, a : a + 1], small[1, a : a + 1]
        pair = (c_real * f_real - c_imag * f_imag, c_real * f_imag + c_imag * f_real)
        block, first = a * FINE // width, a * FINE % width
        for z, part in enumerate(pair):
            for value, row, col in zip(halves(part), (row_high, row_low), (col_high, col_low)):
                if row is not None:
                    row[block, z * width + first : z * width + first + FINE] = value
                for k in range(blocks):
                    spot = slice(a * FINE, (a + 1) * FINE)
                    col[k, spot, z * width : (z + 1) * width] = value[:, k * width : (k + 1) * width]


def forward_blocks(real, imag, high_ref, low_ref, out_refs, bits):
    me = lax.axis_index("lat")
    for d, out in zip(bits, out_refs):
        out[0], out[1] = along_y(real, imag, high_ref, low_ref, me ^ d, -1)


def weighted(contrast, real, imag):
    m_real, m_imag = contrast[0], contrast[1]
    return m_real * real - m_imag * imag, m_real * imag + m_imag * real


def first_body(lat, source, contrast, small, *refs):
    outs, (field, factor, waves, high, low, sems) = refs[: lat * CHUNKS], refs[lat * CHUNKS :]
    copies = [
        pltpu.make_async_copy(small, waves, sems.at[0]),
        pltpu.make_async_copy(source.at[:, 0], field, sems.at[1]),
        pltpu.make_async_copy(contrast, factor, sems.at[2]),
    ]
    for copy in copies:
        copy.start()
    copies[0].wait()
    make_tables(waves, high, low)
    copies[1].wait()
    copies[2].wait()
    real, imag = weighted(factor, field[0], field[1])
    me = lax.axis_index("lat")
    for i, d in enumerate(turns(lat)):
        got = along_y(real, imag, high, low, me ^ d, -1)
        half = got[0].shape[1] // CHUNKS
        for c in range(CHUNKS):
            outs[c * lat + i][...] = jnp.concatenate([part[:, c * half : (c + 1) * half] for part in got], axis=1)


def start_body(lat, source, contrast, high_ref, low_ref, *outs):
    real, imag = weighted(contrast, source[0, 0], source[1, 0])
    forward_blocks(real, imag, high_ref, low_ref, outs, turns(lat))


def turn_body(green, out):
    for z in range(green.shape[0]):
        for o in range(green.shape[1]):
            out[z, o] = green[z, o].T


def blocks_of(bits, width):
    me = lax.axis_index("lat")
    return [pl.ds(pl.multiple_of((me ^ d) * width, width), width) for d in bits]


def spectrum_part(parts, bits, high_ref, low_ref, k):
    columns = blocks_of(bits, parts[0].shape[1])
    high, low = halves(jnp.concatenate([jnp.concatenate([part[0], part[1]], axis=1) for part in parts], axis=0))
    table_high, table_low = [jnp.concatenate([ref[k, :, at] for at in columns], axis=1) for ref in (high_ref, low_ref)]
    got = product(table_high, table_low, high, low)
    rows, width = got.shape[0] // 2, got.shape[1] // 2
    return got[:rows, :width] + got[rows:, width:], got[:rows, width:] - got[rows:, :width]


def spectrum_body(bits, *refs):
    parts, (high_ref, low_ref, out) = refs[: len(bits)], refs[len(bits) :]
    rows = high_ref.shape[1] // 2
    for k in range(high_ref.shape[0]):
        at = slice(k * rows, (k + 1) * rows)
        out[0, at], out[1, at] = spectrum_part(parts, bits, high_ref, low_ref, k)


def couple_body(bits, *refs):
    parts, (begun, green, high_ref, low_ref), outs = refs[: len(bits)], refs[len(bits) : len(bits) + 4], refs[len(bits) + 4 :]
    layer = lax.axis_index("layer")
    rows = high_ref.shape[1] // 2
    for k in range(high_ref.shape[0]):
        at = slice(k * rows, (k + 1) * rows)
        real, imag = spectrum_part(parts, bits, high_ref, low_ref, k)
        real, imag = begun[0, at] + real, begun[1, at] + imag
        chunks = len(outs) // green.shape[1]
        for e in range(green.shape[1]):
            g_real, g_imag = green[0, layer ^ e, at], green[1, layer ^ e, at]
            pair = (g_real * real - g_imag * imag, g_real * imag + g_imag * real)
            if chunks == 1:
                outs[e][0, at], outs[e][1, at] = pair
            else:
                half = real.shape[1] // chunks
                for c in range(chunks):
                    spot = slice(c * half, (c + 1) * half)
                    outs[e * chunks + c][at] = jnp.concatenate([part[:, spot] for part in pair], axis=1)


def swap(packed):
    return pltpu.roll(packed, packed.shape[1] // 2, 1)


def spectrum_chunk(parts, bits, high_ref, low_ref, k):
    columns = blocks_of(bits, parts[0].shape[0])
    high, low = halves(jnp.concatenate([part[...] for part in parts], axis=0))
    table_high, table_low = [jnp.concatenate([ref[k, :, at] for at in columns], axis=1) for ref in (high_ref, low_ref)]
    got = product(table_high, table_low, high, low)
    rows, width = got.shape[0] // 2, got.shape[1]
    lane = lax.broadcasted_iota(jnp.int32, (rows, width), 1)
    turned = swap(got[rows:])
    return got[:rows] + jnp.where(lane < width // 2, turned, -turned)


def spectrum_chunk_body(bits, *refs):
    parts, (high_ref, low_ref, out) = refs[: len(bits)], refs[len(bits) :]
    rows = high_ref.shape[1] // 2
    for k in range(high_ref.shape[0]):
        out[k * rows : (k + 1) * rows] = spectrum_chunk(parts, bits, high_ref, low_ref, k)


def couple_chunk_body(bits, chunk, *refs):
    parts, (begun, green, high_ref, low_ref), outs = refs[: len(bits)], refs[len(bits) : len(bits) + 4], refs[len(bits) + 4 :]
    layer = lax.axis_index("layer")
    rows, half = high_ref.shape[1] // 2, begun.shape[1] // 2
    for k in range(high_ref.shape[0]):
        at = slice(k * rows, (k + 1) * rows)
        spectra = begun[at] + spectrum_chunk(parts, bits, high_ref, low_ref, k)
        swapped = swap(spectra)
        for e, out in enumerate(outs):
            g_real, g_imag = [green[z, layer ^ e, at][:, chunk * half : (chunk + 1) * half] for z in range(2)]
            both = jnp.concatenate([g_real, g_real], axis=1)
            cross = jnp.concatenate([-g_imag, g_imag], axis=1)
            out[at] = both * spectra + cross * swapped


def back_pair_body(bits, layers, *refs):
    count = layers * CHUNKS
    parts, (high_ref, low_ref), outs = refs[:count], refs[count : count + 2], refs[count + 2 :]
    me = lax.axis_index("lat")
    mixed = []
    for c in range(CHUNKS):
        chunk = parts[c * layers : (c + 1) * layers]
        mixed.append(sum((part[...] for part in chunk[1:]), chunk[0][...]))
    half = mixed[0].shape[1] // 2
    pieces = [part[:, z * half : (z + 1) * half] for z in range(2) for part in mixed]
    high, low = halves(jnp.concatenate(pieces, axis=1))
    for d, out in zip(bits, outs):
        out[0], out[1] = along_x(high_ref, low_ref, me ^ d, high, low, +1)


def back_body(bits, layers, *refs):
    parts, (high_ref, low_ref), outs = refs[:layers], refs[layers : layers + 2], refs[layers + 2 :]
    me = lax.axis_index("lat")
    mixed = [sum((part[z] for part in parts[1:]), parts[0][z]) for z in range(2)]
    high, low = halves(jnp.concatenate(mixed, axis=1))
    for d, out in zip(bits, outs):
        out[0], out[1] = along_x(high_ref, low_ref, me ^ d, high, low, +1)


def back_chunk_body(bits, layers, *refs):
    parts, (high_ref, low_ref), outs = refs[:layers], refs[layers : layers + 2], refs[layers + 2 :]
    me = lax.axis_index("lat")
    high, low = halves(sum((part[...] for part in parts[1:]), parts[0][...]))
    for d, out in zip(bits, outs):
        got = product(high_ref[me ^ d], low_ref[me ^ d], high, low)
        rows, width = got.shape[0] // 2, got.shape[1]
        lane = lax.broadcasted_iota(jnp.int32, (rows, width), 1)
        turned = pltpu.roll(got[rows:], width // 2, 1)
        out[...] = got[:rows] + jnp.where(lane < width // 2, -turned, turned)


def field_part(parts, bits, high_ref, low_ref, k, rows, chunk=None):
    if chunk is None:
        spots = blocks_of(bits, parts[0].shape[2])
        both = [jnp.concatenate([part[z, rows] for part in parts], axis=1) for z in range(2)]
    else:
        me = lax.axis_index("lat")
        half = parts[0].shape[1] // 2
        spots = [pl.ds(pl.multiple_of(((me ^ d) * CHUNKS + chunk) * half, half), half) for d in bits]
        lanes = [slice(z * half, (z + 1) * half) for z in range(2)]
        both = [jnp.concatenate([part[rows, at] for part in parts], axis=1) for at in lanes]
    high, low = halves(jnp.concatenate(both, axis=0))
    table_high, table_low = [jnp.concatenate([ref[k, at] for at in spots], axis=0) for ref in (high_ref, low_ref)]
    got = product(high, low, table_high, table_low)
    count, width = got.shape[0] // 2, got.shape[1] // 2
    return got[:count, :width] - got[count:, width:], got[:count, width:] + got[count:, :width]


def field_body(bits, chunk, *refs):
    parts, (high_ref, low_ref, out) = refs[: len(bits)], refs[len(bits) :]
    width = high_ref.shape[2] // 2
    for k in range(high_ref.shape[0]):
        at = slice(k * width, (k + 1) * width)
        out[0, :, at], out[1, :, at] = field_part(parts, bits, high_ref, low_ref, k, slice(None), chunk)


def update(parts, bits, begun, source, contrast, high_ref, low_ref, field, rows=slice(None), chunk=None):
    width = high_ref.shape[2] // 2
    for k in range(high_ref.shape[0]):
        at = slice(k * width, (k + 1) * width)
        real, imag = field_part(parts, bits, high_ref, low_ref, k, rows, chunk)
        real, imag = begun[0, rows, at] + real, begun[1, rows, at] + imag
        m_real, m_imag = contrast[0, rows, at], contrast[1, rows, at]
        field[0, :, at] = source[0, 0, rows, at] + (m_real * real - m_imag * imag)
        field[1, :, at] = source[1, 0, rows, at] + (m_real * imag + m_imag * real)


def again_body(lat, bits, *refs):
    parts, (begun, source, contrast, high_ref, low_ref), rest = refs[: len(bits)], refs[len(bits) : len(bits) + 5], refs[len(bits) + 5 :]
    out, ahead, field = rest
    update(parts, bits, begun, source, contrast, high_ref, low_ref, field)
    ahead[0], ahead[1] = weighted(contrast, field[0], field[1])
    forward_blocks(ahead[0], ahead[1], high_ref, low_ref, [out], turns(lat)[1:2])


def rest_body(bits, ahead, high_ref, low_ref, *outs):
    forward_blocks(ahead[0], ahead[1], high_ref, low_ref, outs, bits)


def end_body(bits, *refs):
    parts, rest = refs[: len(bits)], refs[len(bits) :]
    (begun, source, contrast, efield, high_ref, low_ref), rest = rest[:6], rest[6:]
    before, out, field = (rest[0] if len(rest) == 3 else None), rest[-2], rest[-1]
    update(parts, bits, begun, source, contrast, high_ref, low_ref, field)
    terms = efield[0, 0] * field[0] - efield[1, 0] * field[1]
    out[...] = terms if before is None else before[...] + terms


def half_rows(which, rows):
    return pl.ds(pl.multiple_of(which * rows, rows), rows)


def deal_body(bits, kept, *refs):
    parts, rest = refs[: len(bits)], refs[len(bits) :]
    begun, source, contrast, efield, high_ref, low_ref, before, out, field = rest
    bit = lax.axis_index("freq") & 1
    count = field.shape[1]
    at = half_rows(bit if kept else 1 - bit, count)
    update(parts, bits, begun, source, contrast, high_ref, low_ref, field, at, CHUNKS - 1)
    cell = before[at] + (efield[0, 0, at] * field[0] - efield[1, 0, at] * field[1])
    width = out.shape[1]
    for k in range(cell.shape[1] // width):
        out[k * count : (k + 1) * count] = cell[:, k * width : (k + 1) * width]


def class_body(gone, kept, kinds, table):
    bit = lax.axis_index("freq") & 1
    count, width = kinds.shape[0] // 2, gone.shape[1]
    spots = [slice(k * width, (k + 1) * width) for k in range(kinds.shape[1] // width)]
    sides = []
    for cell, which in ((gone, 1 - bit), (kept, bit)):
        sides.append((cell[...], jnp.concatenate([kinds[half_rows(which, count), at] for at in spots], axis=0)))
    lines = []
    for c in range(CLASSES):
        chosen = sum(jnp.where(kind == c, cell, 0.0) for cell, kind in sides)
        lines.append(jnp.full((1, width), jnp.sum(chosen), jnp.float32))
    table[...] = jnp.concatenate(lines, axis=0)


def keep_body(one, two, *refs):
    tables, out = refs[:-1], refs[-1]
    rows = one.shape[0]
    out[:rows] = one[...] + two[...]
    out[rows:] = sum((table[...] for table in tables[1:]), tables[0][...])


def add_body(one, two, out):
    out[...] = one[...] + two[...]


def place_body(own, other, cell, classes):
    bit = lax.axis_index("freq") & 1
    width = own.shape[1]
    count = cell.shape[1] // width
    rows = cell.shape[0] // 2
    for which, ref in ((bit, own), (1 - bit, other)):
        at = pl.ds(pl.multiple_of(which * rows, rows), rows)
        for k in range(count):
            cell[at, k * width : (k + 1) * width] = ref[k * rows : (k + 1) * rows]
    total = own[count * rows :] + other[count * rows :]
    row = lax.broadcasted_iota(jnp.int32, total.shape, 0)
    lane = lax.broadcasted_iota(jnp.int32, total.shape, 1)
    line = jnp.sum(jnp.where(row == lane, total, 0.0), axis=0, keepdims=True)
    classes[...] = line[:, :CLASSES] / float(NXY)


def fast_device(sizes, source, contrast, green, efield, cell_class):
    freqs, layers, lat = sizes["freq"], sizes["layer"], sizes["lat"]
    pols, rows, length = source.shape[2], source.shape[4], source.shape[5]
    source = source.reshape(2, pols, rows, length)
    efield = efield.reshape(2, pols, rows, length)
    contrast = contrast.reshape(2, rows, length)
    green = green.reshape(2, layers, rows, length)
    kinds = cell_class.reshape(rows, length)
    col_shape, row_shape = (lat, length, 2 * rows), (lat, 2 * rows, length)
    table_specs, row_specs = [whole(col_shape)] * 2, [whole(row_shape)] * 2
    block = f32(2, rows, rows)
    spectrum = f32(2, length, rows)
    full = pltpu.VMEM((2, rows, length), jnp.float32)
    stage_flops = 24 * rows * length * length
    last = pols - 1
    order = []
    bits, near = turns(lat), lat // 2

    def kernel(body, outs, args, specs, flops=stage_flops, scratch=(), vmem=VMEM_BYTES):
        got = call(body, outs, args, specs, flops, scratch, tuple(order[-1:]), vmem)
        order.append(got[0])
        return got

    small = jnp.asarray(small_tables(length))

    def first():
        specs = [pl.BlockSpec(memory_space=pltpu.HBM)] * 3
        scratch = [
            full,
            full,
            pltpu.VMEM(small.shape, jnp.float32),
            pltpu.VMEM(col_shape, jnp.bfloat16),
            pltpu.VMEM(col_shape, jnp.bfloat16),
            pltpu.SemaphoreType.DMA((3,)),
        ]
        body = functools.partial(first_body, lat)
        args = (source, contrast, small)
        outs = [f32(rows, 2 * rows // CHUNKS)] * (lat * CHUNKS)
        got = kernel(body, outs, args, specs, scratch=scratch, vmem=FIRST_VMEM_BYTES)
        return [send(got[c * lat : (c + 1) * lat], "lat", lat) for c in range(CHUNKS)]

    def start(p):
        specs = [pick(source.shape, p), whole(contrast.shape)] + table_specs
        return send(kernel(functools.partial(start_body, lat), [block] * lat, (source, contrast, *col), specs), "lat", lat)

    def couple(parts, chunks=1):
        specs = [whole(block.shape)] * near + row_specs
        begun = kernel(functools.partial(spectrum_body, bits[:near]), [spectrum], (*parts[:near], *row), specs)[0]
        specs = [whole(block.shape)] * (lat - near) + [whole(spectrum.shape), whole(turned.shape)] + row_specs
        body = functools.partial(couple_body, bits[near:])
        outs = [spectrum if chunks == 1 else f32(length, 2 * rows // chunks)] * (layers * chunks)
        got = kernel(body, outs, (*parts[near:], begun, turned, *row), specs)
        got = [send(got[c::chunks], "layer", layers) for c in range(chunks)]
        return got[0] if chunks == 1 else got

    def couple_chunk(parts, c):
        packed, spread = [whole(part.shape) for part in parts], f32(length, parts[0].shape[1])
        body = functools.partial(spectrum_chunk_body, bits[:near])
        begun = kernel(body, [spread], (*parts[:near], *row), packed[:near] + row_specs)[0]
        body = functools.partial(couple_chunk_body, bits[near:], c)
        specs = packed[near:] + [whole(spread.shape), whole(turned.shape)] + row_specs
        return send(kernel(body, [spread] * layers, (*parts[near:], begun, turned, *row), specs), "layer", layers)

    early, later = bits[1:2], bits[:1] + bits[2:]

    def turn_block(value, d):
        return lax.ppermute(value, "lat", [(i, i ^ d) for i in range(lat)])

    def merged(ahead, got):
        return [got[0], ahead] + [turn_block(value, d) for value, d in zip(got[1:], later[1:])]

    def back(parts, chunk=False):
        specs = [whole(part.shape) for part in parts] + row_specs
        whole_body = back_pair_body if len(parts) > layers else back_body

        def some(chosen):
            body = functools.partial(back_chunk_body if chunk else whole_body, chosen, layers)
            outs = [f32(rows, parts[0].shape[1]) if chunk else block] * len(chosen)
            return kernel(body, outs, (*parts, *row), specs, stage_flops * len(chosen) // lat)

        ahead = turn_block(some(early)[0], early[0])
        return merged(ahead, some(later))

    def fields(p, parts):
        specs = [whole(block.shape)] * near + table_specs
        begun = kernel(functools.partial(field_body, bits[:near], None), [f32(2, rows, length)], (*parts[:near], *col), specs)[0]
        specs = [whole(block.shape)] * (lat - near) + [whole(begun.shape), pick(source.shape, p), whole(contrast.shape)]
        return (*parts[near:], begun, source, contrast), specs

    def again(p, parts):
        args, specs = fields(p, parts)
        outs = [block, f32(2, rows, length)]
        body = functools.partial(again_body, lat, bits[near:])
        got = kernel(body, outs, (*args, *col), specs + table_specs, stage_flops, [full])
        ahead = turn_block(got[0], early[0])
        body = functools.partial(rest_body, later)
        got = kernel(body, [block] * len(later), (got[1], *col), [whole((2, rows, length))] + table_specs)
        return merged(ahead, got)

    def end(p, operands, cells):
        more = () if cells is None else (cells,)
        args, specs = operands
        specs += [pick(efield.shape, p)] + table_specs + [whole((rows, length))] * len(more)
        args = (*args, efield, *col, *more)
        body = functools.partial(end_body, bits[near:])
        return kernel(body, [f32(rows, length)], args, specs, scratch=[full])[0]

    def chunk_fields(p, chunks):
        parts = chunks[0]
        packed = [whole(part.shape) for part in parts]
        body = functools.partial(field_body, bits, 0)
        begun = kernel(body, [f32(2, rows, length)], (*parts, *col), packed + table_specs)[0]
        specs = packed + [whole(begun.shape), pick(source.shape, p), whole(contrast.shape)]
        return (*chunks[1], begun, source, contrast), specs

    def deal(operands, cells, kept):
        args, specs = operands
        specs = specs + [pick(efield.shape, last)] + table_specs + [whole((rows, length))]
        args = (*args, efield, *col, cells)
        outs = [f32(rows // 2 * (length // 128), 128)]
        scratch = [pltpu.VMEM((2, rows // 2, length), jnp.float32)]
        body = functools.partial(deal_body, bits, kept)
        return kernel(body, outs, args, specs, stage_flops // 2, scratch)[0]

    def across(value, d):
        return lax.ppermute(value, "freq", [(i, i ^ d) for i in range(freqs)])

    def simple(body, shape, args):
        return kernel(body, [f32(*shape)], tuple(args), [whole(arg.shape) for arg in args], 1 << 16)[0]

    chains = [first()]
    tables = kernel(
        make_tables,
        [jax.ShapeDtypeStruct(shape, jnp.bfloat16) for shape in (col_shape,) * 2 + (row_shape,) * 2],
        (small,),
        [whole(small.shape)],
        1 << 20,
    )
    col, row = tuple(tables[:2]), tuple(tables[2:])
    turned = kernel(turn_body, [f32(2, layers, length, rows)], (green,), [whole(green.shape)], 1 << 20)[0]
    chunks = chains[0]
    chains[0] = couple_chunk(chunks[0], 0)
    chains += [start(p) for p in range(1, pols)]
    for c in range(1, CHUNKS):
        chains[0] = chains[0] + couple_chunk(chunks[c], c)
    chains[1:] = [couple(chain) for chain in chains[1:]]
    for step in range(ITERS - 1):
        moved = [None] * pols
        for p in range(pols):
            moved[p] = back(chains[p])
            if p > 0:
                chains[p - 1] = couple(moved[p - 1])
            moved[p] = again(p, moved[p])
        chains[last] = couple(moved[last], CHUNKS if step == ITERS - 2 else 1)
    cells = None
    for p in range(last - 1):
        cells = end(p, fields(p, back(chains[p])), cells)
    begun = fields(last - 1, back(chains[last - 1]))
    ahead = [back(chains[last][0], True)]
    cells = end(last - 1, begun, cells)
    ahead.append(back(chains[last][1], True))
    final = chunk_fields(last, ahead)
    gone = deal(final, cells, False)
    came = across(gone, 1)
    kept = deal(final, cells, True)
    found = simple(class_body, (CLASSES, 128), [gone, kept, kinds])
    found = send([found] * lat, "lat", lat)
    kept = simple(keep_body, (kept.shape[0] + CLASSES, 128), [kept, came, *found])
    d = 2
    while d < freqs:
        kept = simple(add_body, kept.shape, [kept, across(kept, d)])
        d *= 2
    both = (kept, across(kept, 1))
    outs = [f32(rows, length), f32(1, CLASSES)]
    cell, classes = kernel(place_body, outs, both, [whole(part.shape) for part in both], 1 << 16)
    return cell.reshape(1, rows, length), classes


def solution(mesh):
    whole_lanes = (
        NXY % (mesh.shape["lat"] * 128) == 0
        and NXY % (mesh.shape["lat"] * 128) == 0
        and mesh.shape["freq"] > 1
        and all(mesh.shape[name] & (mesh.shape[name] - 1) == 0 for name in mesh.axis_names)
    )
    per_device = functools.partial(fast_device, dict(mesh.shape)) if whole_lanes else plain_device

    placed = (
        P(None, "freq", None, "layer", "lat", None),
        P(None, "freq", "layer", "lat", None),
        P(None, "freq", None, "layer", "lat", None),
        P(None, "freq", None, "layer", "lat", None),
        P("layer", "lat", None),
    )
    return jax.shard_map(
        per_device,
        mesh=mesh,
        in_specs=placed,
        out_specs=(P("layer", "lat", None), P("layer", None)),
        check_vma=False,
    )
```
